512 devices in a mesh: slab: 64 (over x, z, core), filt: 8 (over y).
Axes of the slice: x: 4, y: 8, z: 8, core: 2. Of those that a mesh axis runs over, the one named last changes fastest.
Arguments:
- volume: bfloat16 [128, 128, 16, 256], P('slab', 'filt'), may hold values from -6 to 6
- weights: bfloat16 [3, 3, 3, 128, 256], replicated, may hold values from -0.109375 to 0.109375
- out_error: bfloat16 [64, 256, 8, 128], P('slab', 'filt'), may hold values from -6 to 6
Outputs:
- in_grad: bfloat16 [128, 128, 16, 256], P('slab', None, 'filt')
- weight_grad: float32 [3, 3, 3, 128, 256], P(None, None, None, None, 'filt')
The draws below stay inside these ranges and needn't reach their ends.
All inputs are finite; a program needn't handle non-finite values.
Results may differ from the reference program's by a relative error of at most 0.0049.
Values may be sent and summed in bfloat16 or wider, within the bound.
No kernel may reach another device: no remote copies, remote signals or barrier semaphores. Data moves between devices by JAX's collectives and lax.ppermute only.
A program may use at most 64 MiB of HBM per device.

```python
import math
import jax
import jax.numpy as jnp
from jax import lax

CI = 128
CO = 256
HO = 8
WO = 128
DO = 64
DIN = 128
H = 16
W = 256


def block_levels(key, extent, cuts, least, top_value):
    def one(dim, shards_of):
        steps = jax.random.uniform(jax.random.fold_in(jax.random.fold_in(key, 6), dim), (shards_of,), jnp.float32, least / len(cuts), top_value / len(cuts))
        return jnp.repeat(jnp.exp(steps), extent[dim] // shards_of).reshape((-1,) + (1,) * (len(extent) - dim - 1))

    level = one(*cuts[0])
    for cut in cuts[1:]:
        level = level * one(*cut)
    return level


def normal_values(stream_key, dims, spread, most, pieces=(), held_as=jnp.bfloat16):
    loudness = block_levels(stream_key, dims, pieces, -0.22, 0.18) if pieces else 1.0
    array = jax.random.normal(stream_key, dims, jnp.float32) * spread * loudness
    return jnp.minimum(jnp.maximum(array, -most), most).astype(held_as)


def setup_inputs(seed: int = 0) -> dict:
    seeds = jax.random.split(jax.random.key(seed), 4)
    volume = normal_values(seeds[0], (DIN, CI, H, W), 1.0, 6.0, ((0, 64), (1, 8)))
    weights = normal_values(seeds[1], (3, 3, 3, CI, CO), (27 * CI) ** -0.5, 0.109375)
    out_error = normal_values(seeds[2], (DO, CO, HO, WO), 1.0, 6.0, ((0, 64), (1, 8)))
    return {"volume": volume, "weights": weights, "out_error": out_error}


def convolve(inputs, kernel):
    return lax.conv_general_dilated(inputs, kernel, (2, 2, 2), ((1, 1), (1, 1), (1, 1)), dimension_numbers=('NCDHW', 'DHWIO', 'NCDHW'), precision=lax.Precision.HIGHEST)

def reference(volume, weights, out_error):
    inputs = volume.astype(jnp.float32).transpose(1, 0, 2, 3)[None]
    kernel = weights.astype(jnp.float32)
    preact, pullback = jax.vjp(convolve, inputs, kernel)
    sigma = jax.nn.sigmoid(preact)
    error = out_error.astype(jnp.float32).transpose(1, 0, 2, 3)[None]
    grad = (error * (sigma * (1.0 + preact * (1.0 - sigma)))).astype(jnp.bfloat16)
    input_part, kernel_part = pullback(grad.astype(jnp.float32))
    count = preact.shape[2] * preact.shape[3] * preact.shape[4]
    in_grad = input_part[0].transpose(1, 0, 2, 3).astype(jnp.bfloat16)
    weight_grad = kernel_part * (1.0 / math.sqrt(count))
    return (in_grad, weight_grad)
```

```python
import jax
import jax.numpy as jnp
from jax import lax
from jax.experimental import pallas as pl
from jax.experimental.pallas import tpu as pltpu
from jax.sharding import PartitionSpec as P

F32 = jnp.float32
BF16 = jnp.bfloat16
VMEM = pl.BlockSpec(memory_space=pltpu.VMEM)
SMEM = pl.BlockSpec(memory_space=pltpu.SMEM)
LIMIT = 48 * 1024 * 1024

NX, NZ, NC = 4, 8, 2
XC_GROUPS = [[(x * NZ + z) * NC + c for x in range(NX) for c in range(NC)] for z in range(NZ)]
Z_GROUPS = [[(x * NZ + z) * NC + c for z in range(NZ)] for x in range(NX) for c in range(NC)]
Y_GROUPS = [[0, 1, 2, 3], [4, 5, 6, 7]]


def call(body, out_shape, in_specs, cost, scratch=()):
    many = isinstance(out_shape, (tuple, list))
    return pl.pallas_call(
        body,
        out_shape=out_shape,
        in_specs=in_specs,
        out_specs=[VMEM] * len(out_shape) if many else VMEM,
        scratch_shapes=list(scratch),
        compiler_params=pltpu.CompilerParams(vmem_limit_bytes=LIMIT),
        cost_estimate=pl.CostEstimate(flops=cost[0], bytes_accessed=cost[1], transcendentals=0),
    )


def mm(left, right):
    return jnp.dot(left, right, preferred_element_type=F32)


def mm_nt(left, right):
    return lax.dot_general(left, right, (((1,), (1,)), ((), ())), preferred_element_type=F32)


def ones_where(cond):
    return jnp.where(cond, 1.0, 0.0).astype(BF16)


def iotas(rows, cols):
    return (
        lax.broadcasted_iota(jnp.int32, (rows, cols), 0),
        lax.broadcasted_iota(jnp.int32, (rows, cols), 1),
    )


def pack_body(vol_ref, err_ref, send_ref):
    i, j = iotas(256, 256)
    row_first = ones_where(j == ((i & 15) << 4) + (i >> 4))
    even_odd = ones_where(i == ((j & 127) << 1) + (j >> 7))
    error_rows = ones_where(j == ((i & 31) << 3) + (i >> 5))
    for p in range(2):
        plane = vol_ref[p].reshape(256, 256)
        plane = mm(row_first, plane).astype(BF16)
        plane = mm(plane, even_odd).astype(BF16)
        for yr in range(4):
            for rr in range(5):
                row = 4 * yr - 1 + rr
                if row < 0:
                    piece = jnp.zeros((16, 256), BF16)
                else:
                    piece = plane[row * 16 : row * 16 + 16]
                send_ref[yr, p * 5 + rr] = piece
                send_ref[yr + 4, p * 5 + rr] = piece
    error = mm(error_rows, err_ref[0].reshape(256, 128)).astype(BF16)
    for yr in range(4):
        for u in range(2):
            for j in range(2):
                start = (2 * yr + j) * 32 + u * 16
                piece = error[start : start + 16]
                send_ref[yr, 10 + u, :, j * 128 : j * 128 + 128] = piece
                send_ref[yr + 4, 10 + u, :, j * 128 : j * 128 + 128] = piece


def turn_body(half_ref, w_ref, even_ref, odd_ref):
    i, j = iotas(128, 256)
    pick = ones_where(j == i + half_ref[0] * 128)
    for ab in range(9):
        cols = slice(ab * 128, ab * 128 + 128)
        even_ref[:, cols] = mm_nt(pick, w_ref[ab, 1]).astype(BF16)
        odd_ref[:128, cols] = mm_nt(pick, w_ref[ab, 2]).astype(BF16)
        odd_ref[128:, cols] = mm_nt(pick, w_ref[ab, 0]).astype(BF16)


def conv_body(half_ref, rec_ref, rim_ref, even_ref, odd_ref, grad_ref, part_ref, ze, zo):
    for a in range(3):
        for b in range(3):
            rows = slice((a * 3 + b) * 128, (a * 3 + b) * 128 + 128)
            for j in range(2):
                if a == 0:
                    tile = rim_ref[:, 2 * j + b]
                else:
                    tile = rec_ref[:, (a - 1) * 5 + 2 * j + b]
                tile = tile.reshape(128, 256)
                ze[rows, j * 128 : j * 128 + 128] = tile[:, :128]
                zo[rows, j * 128 : j * 128 + 128] = tile[:, 128:]
    center = mm(even_ref[...], ze[...])
    sides = mm(odd_ref[...], zo[...])
    error = rec_ref[pl.ds(half_ref[0] * 4, 4), 10:12].reshape(128, 256).astype(F32)
    lane = lax.broadcasted_iota(jnp.int32, (128, 128), 1)
    grads, nexts = [], []
    for j in range(2):
        cols = slice(j * 128, j * 128 + 128)
        before = jnp.where(lane == 0, 0.0, pltpu.roll(sides[128:, cols], 1, 1))
        preact = center[:, cols] + sides[:128, cols] + before
        sigma = jax.nn.sigmoid(preact)
        grad = (error[:, cols] * (sigma * (1.0 + preact * (1.0 - sigma)))).astype(BF16)
        grads.append(grad)
        shifted = jnp.where(lane == 127, 0.0, pltpu.roll(grad.astype(F32), 127, 1))
        nexts.append(shifted.astype(BF16))
    grad = jnp.concatenate(grads, 1)
    grad_ref[...] = grad
    i, j = iotas(128, 128)
    order = ones_where(j == (((i >> 2) & 3) << 5) + ((i >> 4) << 2) + (i & 3))
    grad = mm(order, grad).astype(BF16)
    after = mm(order, jnp.concatenate(nexts, 1)).astype(BF16)
    part_ref[:, 1152:2304] = mm_nt(grad, ze[...]).astype(BF16)
    part_ref[:, 2304:3456] = mm_nt(grad, zo[...]).astype(BF16)
    part_ref[:, 0:1152] = mm_nt(after, zo[...]).astype(BF16)


def rows_body(member_ref, all_ref, out_ref):
    y = member_ref[0]
    nxt = jnp.minimum(y + 1, 7)
    for h in range(2):
        for n, row in enumerate((y, nxt)):
            both = all_ref[4 * h + (row >> 1)].astype(F32)
            one = jnp.where((row & 1) == 0, both[:, :128], both[:, 128:])
            if n == 1:
                one = jnp.where(y == 7, 0.0, one)
            out_ref[n, h * 128 : h * 128 + 128] = one.astype(BF16)


def input_body(own_ref, up_ref, w_ref, out_ref):
    lane = lax.broadcasted_iota(jnp.int32, (128, 128), 1)
    i, j = iotas(256, 256)
    weave = ones_where(j == ((i & 127) << 1) + (i >> 7))
    taps = ((( 1, 0),), ((2, 0), (0, 1)))
    for ed in range(2):
        for er in range(2):
            sums = []
            for c in range(3):
                total = None
                for a, od in taps[ed]:
                    for b, pd in taps[er]:
                        grad = (up_ref if od else own_ref)[pd]
                        term = mm(w_ref[a * 3 + b, c], grad)
                        total = term if total is None else total + term
                sums.append(total)
            nxt = jnp.where(lane == 127, 0.0, pltpu.roll(sums[0], 127, 1))
            both = jnp.concatenate([sums[1].astype(BF16), (sums[2] + nxt).astype(BF16)], 1)
            out_ref[ed, er] = mm(both, weave).astype(BF16)


def shifted_2(value, axis, steps):
    count = lax.axis_size(axis)
    first, last = (max(0, -steps), min(count, count - steps))
    return lax.ppermute(value, axis, [(source, source + steps) for source in range(first, last)])


def exchange(value, axis, groups=None):
    return lax.all_to_all(
        value, axis, split_axis=0, concat_axis=0, axis_index_groups=groups, tiled=True
    )


def to_all(value, count):
    return jnp.broadcast_to(value[None], (count,) + value.shape)


def on_device(volume, weights, out_error):
    member = lax.axis_index("filt")
    half = (member // 4).astype(jnp.int32).reshape(1)
    taps = weights.reshape(9, 3, 128, 256)
    shape = jax.ShapeDtypeStruct
    mb = 1 << 20

    send = call(pack_body, shape((8, 12, 16, 256), BF16), [VMEM] * 2, (2 * mb, mb))(
        volume, out_error
    )
    received = exchange(send, "filt")
    even, odd = call(
        turn_body,
        (shape((128, 1152), BF16), shape((256, 1152), BF16)),
        [SMEM, VMEM],
        (226 * mb, 3 * mb),
    )(half, taps)
    rim = shifted_2(received[:, 5:10], "slab", 1)
    grad, part = call(
        conv_body,
        (shape((128, 256), BF16), shape((128, 3456), BF16)),
        [SMEM, VMEM, VMEM, VMEM, VMEM],
        (453 * mb, 4 * mb),
        [pltpu.VMEM((1152, 256), BF16), pltpu.VMEM((1152, 256), BF16)],
    )(half, received, rim, even, odd)

    pieces = exchange(part.reshape(8, 16, 3456), "slab", XC_GROUPS)
    piece = jnp.sum(pieces.astype(F32), 0).astype(BF16)
    rows = exchange(to_all(grad, 8), "filt")

    own = call(rows_body, shape((2, 256, 128), BF16), [SMEM, VMEM], (mb, mb))(
        member.astype(jnp.int32).reshape(1), rows
    )
    upper = shifted_2(own, "slab", -1)
    in_grad = call(
        input_body, shape((2, 2, 128, 256), BF16), [VMEM] * 3, (226 * mb, 3 * mb)
    )(own, upper, taps)
    in_grad = in_grad.transpose(0, 2, 1, 3)

    tiles = exchange(piece.reshape(4, 4, 3456), "filt", Y_GROUPS)
    tile = jnp.sum(tiles.astype(F32), 0).astype(BF16)
    tiles = exchange(to_all(tile, 8), "slab", Z_GROUPS)
    tile = (jnp.sum(tiles.astype(F32), 0) * (1.0 / 256.0)).astype(BF16)
    tiles = exchange(to_all(tile, 8), "slab", XC_GROUPS)
    tiles = tiles.astype(F32).reshape(32, 3, 3, 3, 128)
    weight_grad = tiles.transpose(2, 3, 1, 4, 0)
    return (in_grad, weight_grad)


def solution(mesh):
    in_specs = (P("slab", "filt", None, None), P(), P("slab", "filt", None, None))
    out_specs = (P("slab", None, "filt", None), P(None, None, None, None, "filt"))
    return jax.shard_map(
        on_device, mesh=mesh, in_specs=in_specs, out_specs=out_specs, check_vma=False
    )
```

```python
import jax
import jax.numpy as jnp
from jax import lax
from jax.experimental import pallas as pl
from jax.experimental.pallas import tpu as pltpu
from jax.sharding import PartitionSpec as P

F32 = jnp.float32
BF16 = jnp.bfloat16
VMEM = pl.BlockSpec(memory_space=pltpu.VMEM)
SMEM = pl.BlockSpec(memory_space=pltpu.SMEM)
LIMIT = 48 * 1024 * 1024

NX, NZ, NC = 4, 8, 2
X_GROUPS = [[(x * NZ + z) * NC + c for x in range(NX)] for z in range(NZ) for c in range(NC)]
XC_GROUPS = [[(x * NZ + z) * NC + c for x in range(NX) for c in range(NC)] for z in range(NZ)]
Z_GROUPS = [[(x * NZ + z) * NC + c for z in range(NZ)] for x in range(NX) for c in range(NC)]
CORE_PAIRS = [(s, s ^ 1) for s in range(NX * NZ * NC)]


def call(body, out_shape, in_specs, cost, scratch=()):
    many = isinstance(out_shape, (tuple, list))
    return pl.pallas_call(
        body,
        out_shape=out_shape,
        in_specs=in_specs,
        out_specs=[VMEM] * len(out_shape) if many else VMEM,
        scratch_shapes=list(scratch),
        compiler_params=pltpu.CompilerParams(vmem_limit_bytes=LIMIT),
        cost_estimate=pl.CostEstimate(flops=cost[0], bytes_accessed=cost[1], transcendentals=0),
    )


def mm(left, right):
    return jnp.dot(left, right, preferred_element_type=F32)


def mm_nt(left, right):
    return lax.dot_general(left, right, (((1,), (1,)), ((), ())), preferred_element_type=F32)


def ones_where(cond):
    return jnp.where(cond, 1.0, 0.0).astype(BF16)


def iotas(rows, cols):
    return (
        lax.broadcasted_iota(jnp.int32, (rows, cols), 0),
        lax.broadcasted_iota(jnp.int32, (rows, cols), 1),
    )


def pack_body(vol_ref, err_ref, send_ref):
    i, j = iotas(256, 256)
    row_first = ones_where(j == ((i & 15) << 4) + (i >> 4))
    even_odd = ones_where(i == ((j & 127) << 1) + (j >> 7))
    error_rows = ones_where(j == ((i & 31) << 3) + (i >> 5))
    for p in range(2):
        plane = vol_ref[p].reshape(256, 256)
        plane = mm(row_first, plane).astype(BF16)
        plane = mm(plane, even_odd).astype(BF16)
        for y in range(8):
            for b in range(3):
                row = 2 * y - 1 + b
                if row < 0:
                    piece = jnp.zeros((16, 256), BF16)
                else:
                    piece = plane[row * 16 : row * 16 + 16]
                send_ref[y, p * 3 + b] = piece
    error = mm(error_rows, err_ref[0].reshape(256, 128)).astype(BF16)
    for y in range(8):
        for u in range(2):
            start = y * 32 + u * 16
            send_ref[y, 6, :, u * 128 : u * 128 + 128] = error[start : start + 16]


def turn_body(w_ref, even_ref, odd_ref):
    i, j = iotas(256, 256)
    same = ones_where(i == j)
    for ab in range(9):
        cols = slice(ab * 128, ab * 128 + 128)
        even_ref[:, cols] = mm_nt(same, w_ref[ab, 1]).astype(BF16)
        odd_ref[:256, cols] = mm_nt(same, w_ref[ab, 2]).astype(BF16)
        odd_ref[256:, cols] = mm_nt(same, w_ref[ab, 0]).astype(BF16)


def core_rows(core):
    i, j = iotas(128, 256)
    return ones_where(j == (((i >> 2) & 7) << 5) + ((i >> 5) << 3) + (i & 3) + core * 4)


def taps_of(order, both, ze, zo):
    now = mm(order, both[:, :128]).astype(BF16)
    after = mm(order, both[:, 128:]).astype(BF16)
    return mm_nt(after, zo[...]), mm_nt(now, ze[...]), mm_nt(now, zo[...])


def conv_body(core_ref, rec_ref, rim_ref, even_ref, odd_ref, grad_ref, both_ref, ze, zo, part_ref):
    for a in range(3):
        for b in range(3):
            rows = slice((a * 3 + b) * 128, (a * 3 + b) * 128 + 128)
            tile = rim_ref[:, b] if a == 0 else rec_ref[:, (a - 1) * 3 + b]
            tile = tile.reshape(128, 256)
            ze[rows] = tile[:, :128]
            zo[rows] = tile[:, 128:]
    center = mm(even_ref[...], ze[...])
    sides = mm(odd_ref[...], zo[...])
    errors = []
    for y in range(8):
        errors += [rec_ref[y, 6][:, :128], rec_ref[y, 6][:, 128:]]
    error = jnp.concatenate(errors, 0).astype(F32)
    lane = lax.broadcasted_iota(jnp.int32, (256, 128), 1)
    before = jnp.where(lane == 0, 0.0, pltpu.roll(sides[256:], 1, 1))
    preact = center + sides[:256] + before
    sigma = jax.nn.sigmoid(preact)
    grad = (error * (sigma * (1.0 + preact * (1.0 - sigma)))).astype(BF16)
    grad_ref[...] = grad
    after = jnp.where(lane == 127, 0.0, pltpu.roll(grad.astype(F32), 127, 1)).astype(BF16)
    both = jnp.concatenate([grad, after], 1)
    both_ref[...] = both
    parts = taps_of(core_rows(1 - core_ref[0]), both, ze, zo)
    for c in range(3):
        part_ref[:, c * 1152 : c * 1152 + 1152] = parts[c].astype(BF16)


def keep_body(core_ref, both_ref, ze, zo, other_ref, part_ref):
    parts = taps_of(core_rows(core_ref[0]), both_ref[...], ze, zo)
    for c in range(3):
        cols = slice(c * 1152, c * 1152 + 1152)
        part_ref[:, cols] = (parts[c] + other_ref[:, cols].astype(F32)).astype(BF16)


def sum_body(in_ref, out_ref):
    total = in_ref[0].astype(F32)
    for n in range(1, in_ref.shape[0]):
        total = total + in_ref[n].astype(F32)
    out_ref[...] = total.astype(BF16)


def input_body(own_ref, up_ref, w_ref, out_ref):
    lane = lax.broadcasted_iota(jnp.int32, (128, 128), 1)
    i, j = iotas(256, 256)
    weave = ones_where(j == ((i & 127) << 1) + (i >> 7))
    taps = ((( 1, 0),), ((2, 0), (0, 1)))
    for ed in range(2):
        for er in range(2):
            sums = []
            for c in range(3):
                total = None
                for a, od in taps[ed]:
                    for b, pd in taps[er]:
                        grad = (up_ref if od else own_ref)[pd]
                        term = mm(w_ref[a * 3 + b, c], grad)
                        total = term if total is None else total + term
                sums.append(total)
            nxt = jnp.where(lane == 127, 0.0, pltpu.roll(sums[0], 127, 1))
            both = jnp.concatenate([sums[1].astype(BF16), (sums[2] + nxt).astype(BF16)], 1)
            out_ref[ed, er] = mm(both, weave).astype(BF16)


def shifted_2(value, axis, steps):
    count = lax.axis_size(axis)
    first, last = (max(0, -steps), min(count, count - steps))
    return lax.ppermute(value, axis, [(source, source + steps) for source in range(first, last)])


def exchange(value, axis, groups=None):
    return lax.all_to_all(
        value, axis, split_axis=0, concat_axis=0, axis_index_groups=groups, tiled=True
    )


def to_all(value, count):
    return jnp.broadcast_to(value[None], (count,) + value.shape)


def add_up(value):
    size = value.size * 2
    return call(sum_body, jax.ShapeDtypeStruct(value.shape[1:], BF16), [VMEM], (size, size))(value)


def on_device(volume, weights, out_error):
    core = (lax.axis_index("slab") & 1).astype(jnp.int32).reshape(1)
    taps = weights.reshape(9, 3, 128, 256)
    shape = jax.ShapeDtypeStruct
    mb = 1 << 20

    send = call(pack_body, shape((8, 7, 16, 256), BF16), [VMEM] * 2, (2 * mb, mb))(
        volume, out_error
    )
    received = exchange(send, "filt")
    even, odd = call(
        turn_body, (shape((256, 1152), BF16), shape((512, 1152), BF16)), [VMEM], (452 * mb, 4 * mb)
    )(taps)
    rim = shifted_2(received[:, 3:6], "slab", 1)
    stack = shape((1152, 128), BF16)
    grad, both, ze, zo, part = call(
        conv_body,
        (shape((256, 128), BF16), shape((256, 256), BF16), stack, stack, shape((128, 3456), BF16)),
        [SMEM, VMEM, VMEM, VMEM, VMEM],
        (453 * mb, 4 * mb),
    )(core, received, rim, even, odd)

    other = lax.ppermute(part, "slab", CORE_PAIRS)
    right = shifted_2(grad, "filt", -1)
    part = call(
        keep_body, shape((128, 3456), BF16), [SMEM, VMEM, VMEM, VMEM, VMEM], (113 * mb, 3 * mb)
    )(core, both, ze, zo, other)
    piece = add_up(exchange(part.reshape(4, 32, 3456), "slab", X_GROUPS))

    own = jnp.stack([grad, right])
    upper = shifted_2(own, "slab", -1)
    in_grad = call(
        input_body, shape((2, 2, 128, 256), BF16), [VMEM] * 3, (226 * mb, 3 * mb)
    )(own, upper, taps)
    in_grad = in_grad.transpose(0, 2, 1, 3)

    tile = add_up(exchange(piece.reshape(8, 4, 3456), "filt"))
    tile = add_up(exchange(to_all(tile, 8), "slab", Z_GROUPS))
    tiles = exchange(to_all(tile, 8), "slab", XC_GROUPS)
    tiles = tiles.astype(F32).reshape(32, 3, 3, 3, 128) * (1.0 / 256.0)
    weight_grad = tiles.transpose(2, 3, 1, 4, 0)
    return (in_grad, weight_grad)


def solution(mesh):
    in_specs = (P("slab", "filt", None, None), P(), P("slab", "filt", None, None))
    out_specs = (P("slab", None, "filt", None), P(None, None, None, None, "filt"))
    return jax.shard_map(
        on_device, mesh=mesh, in_specs=in_specs, out_specs=out_specs, check_vma=False
    )
```

```python
import jax
import jax.numpy as jnp
from jax import lax
from jax.experimental import pallas as pl
from jax.experimental.pallas import tpu as pltpu
from jax.sharding import PartitionSpec as P

F32 = jnp.float32
BF16 = jnp.bfloat16
VMEM = pl.BlockSpec(memory_space=pltpu.VMEM)
ANY = pl.BlockSpec(memory_space=pl.ANY)
SMEM = pl.BlockSpec(memory_space=pltpu.SMEM)
LIMIT = 48 * 1024 * 1024

NX, NZ, NC = 4, 8, 2
X_GROUPS = [[(x * NZ + z) * NC + c for x in range(NX)] for z in range(NZ) for c in range(NC)]
XC_GROUPS = [[(x * NZ + z) * NC + c for x in range(NX) for c in range(NC)] for z in range(NZ)]
Z_GROUPS = [[(x * NZ + z) * NC + c for z in range(NZ)] for x in range(NX) for c in range(NC)]
CORE_PAIRS = [(s, s ^ 1) for s in range(NX * NZ * NC)]


def call(body, out_shape, in_specs, cost, scratch=(), limit=LIMIT):
    many = isinstance(out_shape, (tuple, list))
    return pl.pallas_call(
        body,
        out_shape=out_shape,
        in_specs=in_specs,
        out_specs=[VMEM] * len(out_shape) if many else VMEM,
        scratch_shapes=list(scratch),
        compiler_params=pltpu.CompilerParams(vmem_limit_bytes=limit),
        cost_estimate=pl.CostEstimate(flops=cost[0], bytes_accessed=cost[1], transcendentals=0),
    )


def mm(left, right):
    return jnp.dot(left, right, preferred_element_type=F32)


def mm_nt(left, right):
    return lax.dot_general(left, right, (((1,), (1,)), ((), ())), preferred_element_type=F32)


def ones_where(cond):
    return jnp.where(cond, 1.0, 0.0).astype(BF16)


def iotas(rows, cols):
    return (
        lax.broadcasted_iota(jnp.int32, (rows, cols), 0),
        lax.broadcasted_iota(jnp.int32, (rows, cols), 1),
    )


def pack_body(vol_hbm, err_hbm, send_ref, vol_ref, err_ref, sems):
    copies = [
        pltpu.make_async_copy(vol_hbm, vol_ref, sems.at[0]),
        pltpu.make_async_copy(err_hbm, err_ref, sems.at[1]),
    ]
    for copy in copies:
        copy.start()
    i, j = iotas(256, 256)
    row_first = ones_where(j == ((i & 15) << 4) + (i >> 4))
    even_odd = ones_where(i == ((j & 127) << 1) + (j >> 7))
    error_rows = ones_where(j == ((i & 31) << 3) + (i >> 5))
    copies[0].wait()
    for p in range(2):
        plane = vol_ref[p].reshape(256, 256)
        plane = mm(row_first, plane).astype(BF16)
        plane = mm(plane, even_odd).astype(BF16)
        for y in range(8):
            for b in range(3):
                row = 2 * y - 1 + b
                if row < 0:
                    piece = jnp.zeros((16, 256), BF16)
                else:
                    piece = plane[row * 16 : row * 16 + 16]
                send_ref[y, p * 3 + b] = piece
    copies[1].wait()
    error = mm(error_rows, err_ref[0].reshape(256, 128)).astype(BF16)
    for y in range(8):
        for u in range(2):
            start = y * 32 + u * 16
            send_ref[y, 6, :, u * 128 : u * 128 + 128] = error[start : start + 16]


def turn_body(w_ref, even_ref, odd_ref):
    i, j = iotas(256, 256)
    same = ones_where(i == j)
    for ab in range(9):
        cols = slice(ab * 128, ab * 128 + 128)
        even_ref[:, cols] = mm_nt(same, w_ref[ab, 1]).astype(BF16)
        odd_ref[:256, cols] = mm_nt(same, w_ref[ab, 2]).astype(BF16)
        odd_ref[256:, cols] = mm_nt(same, w_ref[ab, 0]).astype(BF16)


def core_rows(core):
    i, j = iotas(128, 256)
    return ones_where(j == (((i >> 2) & 7) << 5) + ((i >> 5) << 3) + (i & 3) + core * 4)


def taps_of(order, both, ze, zo):
    now = mm(order, both[:, :128]).astype(BF16)
    after = mm(order, both[:, 128:]).astype(BF16)
    return mm_nt(after, zo[...]), mm_nt(now, ze[...]), mm_nt(now, zo[...])


def conv_body(core_ref, rec_ref, rim_ref, even_ref, odd_ref, grad_ref, both_ref, ze, zo, part_ref):
    for a in range(3):
        for b in range(3):
            rows = slice((a * 3 + b) * 128, (a * 3 + b) * 128 + 128)
            tile = rim_ref[:, b] if a == 0 else rec_ref[:, (a - 1) * 3 + b]
            tile = tile.reshape(128, 256)
            ze[rows] = tile[:, :128]
            zo[rows] = tile[:, 128:]
    center = mm(even_ref[...], ze[...])
    sides = mm(odd_ref[...], zo[...])
    errors = []
    for y in range(8):
        errors += [rec_ref[y, 6][:, :128], rec_ref[y, 6][:, 128:]]
    error = jnp.concatenate(errors, 0).astype(F32)
    lane = lax.broadcasted_iota(jnp.int32, (256, 128), 1)
    before = jnp.where(lane == 0, 0.0, pltpu.roll(sides[256:], 1, 1))
    preact = center + sides[:256] + before
    sigma = jax.nn.sigmoid(preact)
    grad = (error * (sigma * (1.0 + preact * (1.0 - sigma)))).astype(BF16)
    grad_ref[...] = grad
    after = jnp.where(lane == 127, 0.0, pltpu.roll(grad.astype(F32), 127, 1)).astype(BF16)
    both = jnp.concatenate([grad, after], 1)
    both_ref[...] = both
    parts = taps_of(core_rows(1 - core_ref[0]), both, ze, zo)
    for c in range(3):
        part_ref[:, c * 1152 : c * 1152 + 1152] = parts[c].astype(BF16)


def keep_body(core_ref, both_ref, ze, zo, other_ref, part_ref):
    parts = taps_of(core_rows(core_ref[0]), both_ref[...], ze, zo)
    for c in range(3):
        cols = slice(c * 1152, c * 1152 + 1152)
        part_ref[:, cols] = (parts[c] + other_ref[:, cols].astype(F32)).astype(BF16)


def sum_body(in_ref, out_ref):
    total = in_ref[0].astype(F32)
    for n in range(1, in_ref.shape[0]):
        total = total + in_ref[n].astype(F32)
    total = total.astype(BF16)
    if len(out_ref.shape) == len(total.shape):
        out_ref[...] = total
    else:
        for n in range(out_ref.shape[0]):
            out_ref[n] = total


def last_body(in_ref, out_ref):
    for m in range(8):
        rows = in_ref[m].astype(F32) * (1.0 / 256.0)
        for c in range(3):
            for ab in range(9):
                start = (c * 9 + ab) * 128
                out_ref[ab * 3 + c, 4 * m : 4 * m + 4] = rows[:, start : start + 128]


def input_body(own_ref, up_ref, w_ref, out_ref):
    lane = lax.broadcasted_iota(jnp.int32, (128, 128), 1)
    i, j = iotas(256, 256)
    weave = ones_where(j == ((i & 127) << 1) + (i >> 7))
    taps = ((( 1, 0),), ((2, 0), (0, 1)))
    for ed in range(2):
        for er in range(2):
            sums = []
            for c in range(3):
                total = None
                for a, od in taps[ed]:
                    for b, pd in taps[er]:
                        grad = (up_ref if od else own_ref)[pd]
                        term = mm(w_ref[a * 3 + b, c], grad)
                        total = term if total is None else total + term
                sums.append(total)
            nxt = jnp.where(lane == 127, 0.0, pltpu.roll(sums[0], 127, 1))
            both = jnp.concatenate([sums[1].astype(BF16), (sums[2] + nxt).astype(BF16)], 1)
            out_ref[ed, er] = mm(both, weave).astype(BF16)


def shifted_2(value, axis, steps):
    count = lax.axis_size(axis)
    first, last = (max(0, -steps), min(count, count - steps))
    return lax.ppermute(value, axis, [(source, source + steps) for source in range(first, last)])


def exchange(value, axis, groups=None):
    return lax.all_to_all(
        value, axis, split_axis=0, concat_axis=0, axis_index_groups=groups, tiled=True
    )


def add_up(value, copies=()):
    size = value.size * 2
    out_shape = jax.ShapeDtypeStruct(copies + value.shape[1:], BF16)
    return call(sum_body, out_shape, [VMEM], (size, size))(value)


def on_device(volume, weights, out_error):
    core = (lax.axis_index("slab") & 1).astype(jnp.int32).reshape(1)
    taps = weights.reshape(9, 3, 128, 256)
    shape = jax.ShapeDtypeStruct
    mb = 1 << 20

    send = call(
        pack_body,
        shape((8, 7, 16, 256), BF16),
        [ANY] * 2,
        (2 * mb, mb),
        [
            pltpu.VMEM(volume.shape, BF16),
            pltpu.VMEM(out_error.shape, BF16),
            pltpu.SemaphoreType.DMA((2,)),
        ],
        64 * 1024 * 1024,
    )(volume, out_error)
    received = exchange(send, "filt")
    even, odd = call(
        turn_body, (shape((256, 1152), BF16), shape((512, 1152), BF16)), [VMEM], (452 * mb, 4 * mb)
    )(taps)
    rim = shifted_2(received[:, 3:6], "slab", 1)
    stack = shape((1152, 128), BF16)
    grad, both, ze, zo, part = call(
        conv_body,
        (shape((256, 128), BF16), shape((256, 256), BF16), stack, stack, shape((128, 3456), BF16)),
        [SMEM, VMEM, VMEM, VMEM, VMEM],
        (453 * mb, 4 * mb),
    )(core, received, rim, even, odd)

    other = lax.ppermute(part, "slab", CORE_PAIRS)
    right = shifted_2(grad, "filt", -1)
    part = call(
        keep_body, shape((128, 3456), BF16), [SMEM, VMEM, VMEM, VMEM, VMEM], (113 * mb, 3 * mb)
    )(core, both, ze, zo, other)
    own = jnp.stack([grad, right])
    part, own = lax.optimization_barrier((part, own))
    upper = shifted_2(own, "slab", -1)
    piece = add_up(exchange(part.reshape(4, 32, 3456), "slab", X_GROUPS))
    piece, upper = lax.optimization_barrier((piece, upper))

    in_grad = call(
        input_body, shape((2, 2, 128, 256), BF16), [VMEM] * 3, (226 * mb, 3 * mb)
    )(own, upper, taps)
    in_grad = in_grad.transpose(0, 2, 1, 3)

    tiles = add_up(exchange(piece.reshape(8, 4, 3456), "filt"), (8,))
    tiles = add_up(exchange(tiles, "slab", Z_GROUPS), (8,))
    tiles = exchange(tiles, "slab", XC_GROUPS)
    out = call(last_body, shape((27, 32, 128), F32), [VMEM], (mb, mb))(tiles)
    weight_grad = out.reshape(3, 3, 3, 32, 128).transpose(0, 1, 2, 4, 3)
    return (in_grad, weight_grad)


def solution(mesh):
    in_specs = (P("slab", "filt", None, None), P(), P("slab", "filt", None, None))
    out_specs = (P("slab", None, "filt", None), P(None, None, None, None, "filt"))
    return jax.shard_map(
        on_device, mesh=mesh, in_specs=in_specs, out_specs=out_specs, check_vma=False
    )
```

```python
import jax
import jax.numpy as jnp
from jax import lax
from jax.experimental import pallas as pl
from jax.experimental.pallas import tpu as pltpu
from jax.sharding import PartitionSpec as P

F32 = jnp.float32
BF16 = jnp.bfloat16
VMEM = pl.BlockSpec(memory_space=pltpu.VMEM)
ANY = pl.BlockSpec(memory_space=pl.ANY)
SMEM = pl.BlockSpec(memory_space=pltpu.SMEM)
LIMIT = 48 * 1024 * 1024


def slab_of(px, pz, bx, bz, core):
    x = 2 * px + (bx ^ px)
    z = 2 * pz + (bz ^ (pz & 1))
    return (x * 8 + z) * 2 + core


B2, B4 = range(2), range(4)
SQUARES = [
    [slab_of(px, pz, bx, bz, c) for bx in B2 for bz in B2] for px in B2 for pz in B4 for c in B2
]
ACROSS = [
    [slab_of(px, pz, bx, bz, c) for px in B2 for pz in B4] for bx in B2 for bz in B2 for c in B2
]
CUBES = [
    [slab_of(px, pz, bx, bz, c) for bx in B2 for bz in B2 for c in B2] for px in B2 for pz in B4
]
CORE_PAIRS = [(s, s ^ 1) for s in range(64)]


def call(body, out_shape, in_specs, cost, scratch=(), limit=LIMIT):
    many = isinstance(out_shape, (tuple, list))
    return pl.pallas_call(
        body,
        out_shape=out_shape,
        in_specs=in_specs,
        out_specs=[VMEM] * len(out_shape) if many else VMEM,
        scratch_shapes=list(scratch),
        compiler_params=pltpu.CompilerParams(vmem_limit_bytes=limit),
        cost_estimate=pl.CostEstimate(flops=cost[0], bytes_accessed=cost[1], transcendentals=0),
    )


def mm(left, right):
    return jnp.dot(left, right, preferred_element_type=F32)


def mm_nt(left, right):
    return lax.dot_general(left, right, (((1,), (1,)), ((), ())), preferred_element_type=F32)


def ones_where(cond):
    return jnp.where(cond, 1.0, 0.0).astype(BF16)


def iotas(rows, cols):
    return (
        lax.broadcasted_iota(jnp.int32, (rows, cols), 0),
        lax.broadcasted_iota(jnp.int32, (rows, cols), 1),
    )


def pack_body(vol_hbm, err_hbm, send_ref, vol_ref, err_ref, sems):
    copies = [
        pltpu.make_async_copy(vol_hbm, vol_ref, sems.at[0]),
        pltpu.make_async_copy(err_hbm, err_ref, sems.at[1]),
    ]
    for copy in copies:
        copy.start()
    i, j = iotas(256, 256)
    row_first = ones_where(j == ((i & 15) << 4) + (i >> 4))
    even_odd = ones_where(i == ((j & 127) << 1) + (j >> 7))
    error_rows = ones_where(j == ((i & 31) << 3) + (i >> 5))
    copies[0].wait()
    for p in range(2):
        plane = vol_ref[p].reshape(256, 256)
        plane = mm(row_first, plane).astype(BF16)
        plane = mm(plane, even_odd).astype(BF16)
        for y in range(8):
            for b in range(3):
                row = 2 * y - 1 + b
                if row < 0:
                    piece = jnp.zeros((16, 256), BF16)
                else:
                    piece = plane[row * 16 : row * 16 + 16]
                send_ref[y, p * 3 + b] = piece
    copies[1].wait()
    error = mm(error_rows, err_ref[0].reshape(256, 128)).astype(BF16)
    for y in range(8):
        for u in range(2):
            start = y * 32 + u * 16
            send_ref[y, 6, :, u * 128 : u * 128 + 128] = error[start : start + 16]


def turn_body(w_ref, even_ref, odd_ref):
    i, j = iotas(256, 256)
    same = ones_where(i == j)
    for ab in range(9):
        cols = slice(ab * 128, ab * 128 + 128)
        even_ref[:, cols] = mm_nt(same, w_ref[ab, 1]).astype(BF16)
        odd_ref[:256, cols] = mm_nt(same, w_ref[ab, 2]).astype(BF16)
        odd_ref[256:, cols] = mm_nt(same, w_ref[ab, 0]).astype(BF16)


def core_rows(core):
    i, j = iotas(128, 256)
    return ones_where(j == (((i >> 2) & 7) << 5) + ((i >> 5) << 3) + (i & 3) + core * 4)


def taps_of(order, both, ze, zo):
    now = mm(order, both[:, :128]).astype(BF16)
    after = mm(order, both[:, 128:]).astype(BF16)
    return mm_nt(after, zo[...]), mm_nt(now, ze[...]), mm_nt(now, zo[...])


def conv_body(core_ref, rec_ref, rim_ref, even_ref, odd_ref, grad_ref, both_ref, ze, zo, part_ref):
    for a in range(3):
        for b in range(3):
            rows = slice((a * 3 + b) * 128, (a * 3 + b) * 128 + 128)
            tile = rim_ref[:, b] if a == 0 else rec_ref[:, (a - 1) * 3 + b]
            tile = tile.reshape(128, 256)
            ze[rows] = tile[:, :128]
            zo[rows] = tile[:, 128:]
    center = mm(even_ref[...], ze[...])
    sides = mm(odd_ref[...], zo[...])
    errors = []
    for y in range(8):
        errors += [rec_ref[y, 6][:, :128], rec_ref[y, 6][:, 128:]]
    error = jnp.concatenate(errors, 0).astype(F32)
    lane = lax.broadcasted_iota(jnp.int32, (256, 128), 1)
    before = jnp.where(lane == 0, 0.0, pltpu.roll(sides[256:], 1, 1))
    preact = center + sides[:256] + before
    sigma = jax.nn.sigmoid(preact)
    grad = (error * (sigma * (1.0 + preact * (1.0 - sigma)))).astype(BF16)
    grad_ref[...] = grad
    after = jnp.where(lane == 127, 0.0, pltpu.roll(grad.astype(F32), 127, 1)).astype(BF16)
    both = jnp.concatenate([grad, after], 1)
    both_ref[...] = both
    parts = taps_of(core_rows(1 - core_ref[0]), both, ze, zo)
    for c in range(3):
        part_ref[:, c * 1152 : c * 1152 + 1152] = parts[c].astype(BF16)


def keep_body(core_ref, both_ref, ze, zo, other_ref, part_ref):
    parts = taps_of(core_rows(core_ref[0]), both_ref[...], ze, zo)
    for c in range(3):
        cols = slice(c * 1152, c * 1152 + 1152)
        part_ref[:, cols] = (parts[c] + other_ref[:, cols].astype(F32)).astype(BF16)


def sum_body(in_ref, out_ref):
    total = in_ref[0].astype(F32)
    for n in range(1, in_ref.shape[0]):
        total = total + in_ref[n].astype(F32)
    total = total.astype(BF16)
    if len(out_ref.shape) == len(total.shape):
        out_ref[...] = total
    else:
        for n in range(out_ref.shape[0]):
            out_ref[n] = total


def last_body(in_ref, out_ref):
    for m in range(8):
        rows = in_ref[m].astype(F32) * (1.0 / 256.0)
        for c in range(3):
            for ab in range(9):
                start = (c * 9 + ab) * 128
                out_ref[ab * 3 + c, 4 * m : 4 * m + 4] = rows[:, start : start + 128]


def input_body(own_ref, up_ref, w_ref, out_ref):
    lane = lax.broadcasted_iota(jnp.int32, (128, 128), 1)
    i, j = iotas(256, 256)
    weave = ones_where(j == ((i & 127) << 1) + (i >> 7))
    taps = ((( 1, 0),), ((2, 0), (0, 1)))
    for ed in range(2):
        for er in range(2):
            sums = []
            for c in range(3):
                total = None
                for a, od in taps[ed]:
                    for b, pd in taps[er]:
                        grad = (up_ref if od else own_ref)[pd]
                        term = mm(w_ref[a * 3 + b, c], grad)
                        total = term if total is None else total + term
                sums.append(total)
            nxt = jnp.where(lane == 127, 0.0, pltpu.roll(sums[0], 127, 1))
            both = jnp.concatenate([sums[1].astype(BF16), (sums[2] + nxt).astype(BF16)], 1)
            out_ref[ed, er] = mm(both, weave).astype(BF16)


def shifted_2(value, axis, steps):
    count = lax.axis_size(axis)
    first, last = (max(0, -steps), min(count, count - steps))
    return lax.ppermute(value, axis, [(source, source + steps) for source in range(first, last)])


def exchange(value, axis, groups=None):
    return lax.all_to_all(
        value, axis, split_axis=0, concat_axis=0, axis_index_groups=groups, tiled=True
    )


def add_up(value, copies=()):
    size = value.size * 2
    out_shape = jax.ShapeDtypeStruct(copies + value.shape[1:], BF16)
    return call(sum_body, out_shape, [VMEM], (size, size))(value)


def on_device(volume, weights, out_error):
    core = (lax.axis_index("slab") & 1).astype(jnp.int32).reshape(1)
    taps = weights.reshape(9, 3, 128, 256)
    shape = jax.ShapeDtypeStruct
    mb = 1 << 20

    send = call(
        pack_body,
        shape((8, 7, 16, 256), BF16),
        [ANY] * 2,
        (2 * mb, mb),
        [
            pltpu.VMEM(volume.shape, BF16),
            pltpu.VMEM(out_error.shape, BF16),
            pltpu.SemaphoreType.DMA((2,)),
        ],
        62500000,
    )(volume, out_error)
    received = exchange(send, "filt")
    even, odd = call(
        turn_body, (shape((256, 1152), BF16), shape((512, 1152), BF16)), [VMEM], (452 * mb, 4 * mb)
    )(taps)
    rim = shifted_2(received[:, 3:6], "slab", 1)
    stack = shape((1152, 128), BF16)
    grad, both, ze, zo, part = call(
        conv_body,
        (shape((256, 128), BF16), shape((256, 256), BF16), stack, stack, shape((128, 3456), BF16)),
        [SMEM, VMEM, VMEM, VMEM, VMEM],
        (453 * mb, 4 * mb),
    )(core, received, rim, even, odd)

    other = lax.ppermute(part, "slab", CORE_PAIRS)
    right = shifted_2(grad, "filt", -1)
    part = call(
        keep_body, shape((128, 3456), BF16), [SMEM, VMEM, VMEM, VMEM, VMEM], (113 * mb, 3 * mb)
    )(core, both, ze, zo, other)
    piece = add_up(exchange(part.reshape(4, 32, 3456), "slab", SQUARES))
    tiles = add_up(exchange(piece.reshape(8, 4, 3456), "filt"), (8,))
    tiles, right = lax.optimization_barrier((tiles, right))
    own = jnp.stack([grad, right])
    upper = shifted_2(own, "slab", -1)
    tiles = add_up(exchange(tiles, "slab", ACROSS), (8,))
    tiles, upper = lax.optimization_barrier((tiles, upper))
    in_grad = call(
        input_body, shape((2, 2, 128, 256), BF16), [VMEM] * 3, (226 * mb, 3 * mb)
    )(own, upper, taps)
    in_grad = in_grad.transpose(0, 2, 1, 3)

    tiles = exchange(tiles, "slab", CUBES)
    out = call(last_body, shape((27, 32, 128), F32), [VMEM], (mb, mb))(tiles)
    weight_grad = out.reshape(3, 3, 3, 32, 128).transpose(0, 1, 2, 4, 3)
    return (in_grad, weight_grad)


def solution(mesh):
    in_specs = (P("slab", "filt", None, None), P(), P("slab", "filt", None, None))
    out_specs = (P("slab", None, "filt", None), P(None, None, None, None, "filt"))
    return jax.shard_map(
        on_device, mesh=mesh, in_specs=in_specs, out_specs=out_specs, check_vma=False
    )
```

```python
import jax
import jax.numpy as jnp
from jax import lax
from jax.experimental import pallas as pl
from jax.experimental.pallas import tpu as pltpu
from jax.sharding import PartitionSpec as P

F32 = jnp.float32
BF16 = jnp.bfloat16
VMEM = pl.BlockSpec(memory_space=pltpu.VMEM)
ANY = pl.BlockSpec(memory_space=pl.ANY)
SMEM = pl.BlockSpec(memory_space=pltpu.SMEM)
LIMIT = 48 * 1024 * 1024

def slab_of(x, z, core):
    return (x * 8 + z) * 2 + core


XS, ZS, CS = range(4), range(8), range(2)
X_RINGS = [[slab_of(x, z, c) for x in XS] for z in ZS for c in CS]
Z_RINGS = [[slab_of(x, z, c) for z in ZS] for x in XS for c in CS]
XC_RINGS = [[slab_of(x, z, c) for x in XS for c in CS] for z in ZS]
CORE_PAIRS = [(s, s ^ 1) for s in range(64)]


def call(body, out_shape, in_specs, cost, scratch=(), limit=LIMIT):
    many = isinstance(out_shape, (tuple, list))
    return pl.pallas_call(
        body,
        out_shape=out_shape,
        in_specs=in_specs,
        out_specs=[VMEM] * len(out_shape) if many else VMEM,
        scratch_shapes=list(scratch),
        compiler_params=pltpu.CompilerParams(vmem_limit_bytes=limit),
        cost_estimate=pl.CostEstimate(flops=cost[0], bytes_accessed=cost[1], transcendentals=0),
    )


def mm(left, right):
    return jnp.dot(left, right, preferred_element_type=F32)


def mm_nt(left, right):
    return lax.dot_general(left, right, (((1,), (1,)), ((), ())), preferred_element_type=F32)


def ones_where(cond):
    return jnp.where(cond, 1.0, 0.0).astype(BF16)


def iotas(rows, cols):
    return (
        lax.broadcasted_iota(jnp.int32, (rows, cols), 0),
        lax.broadcasted_iota(jnp.int32, (rows, cols), 1),
    )


def pack_body(vol_hbm, err_hbm, send_ref, vol_ref, err_ref, sems):
    copies = [
        pltpu.make_async_copy(vol_hbm, vol_ref, sems.at[0]),
        pltpu.make_async_copy(err_hbm, err_ref, sems.at[1]),
    ]
    for copy in copies:
        copy.start()
    i, j = iotas(256, 256)
    row_first = ones_where(j == ((i & 15) << 4) + (i >> 4))
    even_odd = ones_where(i == ((j & 127) << 1) + (j >> 7))
    error_rows = ones_where(j == ((i & 31) << 3) + (i >> 5))
    copies[0].wait()
    for p in range(2):
        plane = vol_ref[p].reshape(256, 256)
        plane = mm(row_first, plane).astype(BF16)
        plane = mm(plane, even_odd).astype(BF16)
        for y in range(8):
            for b in range(3):
                row = 2 * y - 1 + b
                if row < 0:
                    piece = jnp.zeros((16, 256), BF16)
                else:
                    piece = plane[row * 16 : row * 16 + 16]
                send_ref[y, p * 3 + b] = piece
    copies[1].wait()
    error = mm(error_rows, err_ref[0].reshape(256, 128)).astype(BF16)
    for y in range(8):
        for u in range(2):
            start = y * 32 + u * 16
            send_ref[y, 6, :, u * 128 : u * 128 + 128] = error[start : start + 16]


def turn_body(w_ref, even_ref, odd_ref):
    i, j = iotas(256, 256)
    same = ones_where(i == j)
    for ab in range(9):
        cols = slice(ab * 128, ab * 128 + 128)
        even_ref[:, cols] = mm_nt(same, w_ref[ab, 1]).astype(BF16)
        odd_ref[:256, cols] = mm_nt(same, w_ref[ab, 2]).astype(BF16)
        odd_ref[256:, cols] = mm_nt(same, w_ref[ab, 0]).astype(BF16)


def core_rows(core):
    i, j = iotas(128, 256)
    return ones_where(j == (((i >> 2) & 7) << 5) + ((i >> 5) << 3) + (i & 3) + core * 4)


def taps_of(order, both, ze, zo):
    now = mm(order, both[:, :128]).astype(BF16)
    after = mm(order, both[:, 128:]).astype(BF16)
    return mm_nt(after, zo[...]), mm_nt(now, ze[...]), mm_nt(now, zo[...])


def conv_body(core_ref, rec_ref, rim_ref, even_ref, odd_ref, grad_ref, both_ref, ze, zo, part_ref):
    for a in range(3):
        for b in range(3):
            rows = slice((a * 3 + b) * 128, (a * 3 + b) * 128 + 128)
            tile = rim_ref[:, b] if a == 0 else rec_ref[:, (a - 1) * 3 + b]
            tile = tile.reshape(128, 256)
            ze[rows] = tile[:, :128]
            zo[rows] = tile[:, 128:]
    center = mm(even_ref[...], ze[...])
    sides = mm(odd_ref[...], zo[...])
    errors = []
    for y in range(8):
        errors += [rec_ref[y, 6][:, :128], rec_ref[y, 6][:, 128:]]
    error = jnp.concatenate(errors, 0).astype(F32)
    lane = lax.broadcasted_iota(jnp.int32, (256, 128), 1)
    before = jnp.where(lane == 0, 0.0, pltpu.roll(sides[256:], 1, 1))
    preact = center + sides[:256] + before
    sigma = jax.nn.sigmoid(preact)
    grad = (error * (sigma * (1.0 + preact * (1.0 - sigma)))).astype(BF16)
    grad_ref[...] = grad
    after = jnp.where(lane == 127, 0.0, pltpu.roll(grad.astype(F32), 127, 1)).astype(BF16)
    both = jnp.concatenate([grad, after], 1)
    both_ref[...] = both
    parts = taps_of(core_rows(1 - core_ref[0]), both, ze, zo)
    for c in range(3):
        part_ref[:, c * 1152 : c * 1152 + 1152] = parts[c].astype(BF16)


def keep_body(core_ref, both_ref, ze, zo, other_ref, part_ref):
    parts = taps_of(core_rows(core_ref[0]), both_ref[...], ze, zo)
    for c in range(3):
        cols = slice(c * 1152, c * 1152 + 1152)
        part_ref[:, cols] = (parts[c] + other_ref[:, cols].astype(F32)).astype(BF16)


def sum_body(in_ref, out_ref):
    total = in_ref[0].astype(F32)
    for n in range(1, in_ref.shape[0]):
        total = total + in_ref[n].astype(F32)
    total = total.astype(BF16)
    rows = out_ref.shape[1]
    for n in range(out_ref.shape[0]):
        out_ref[n] = total if total.shape[0] == rows else total[n * rows : n * rows + rows]


def last_body(in_ref, out_ref):
    for m in range(8):
        rows = in_ref[m].astype(F32) * (1.0 / 256.0)
        for c in range(3):
            for ab in range(9):
                start = (c * 9 + ab) * 128
                out_ref[ab * 3 + c, 4 * m : 4 * m + 4] = rows[:, start : start + 128]


def input_body(own_ref, up_ref, w_ref, out_ref):
    lane = lax.broadcasted_iota(jnp.int32, (128, 128), 1)
    i, j = iotas(256, 256)
    weave = ones_where(j == ((i & 127) << 1) + (i >> 7))
    taps = ((( 1, 0),), ((2, 0), (0, 1)))
    for ed in range(2):
        for er in range(2):
            sums = []
            for c in range(3):
                total = None
                for a, od in taps[ed]:
                    for b, pd in taps[er]:
                        grad = (up_ref if od else own_ref)[pd]
                        term = mm(w_ref[a * 3 + b, c], grad)
                        total = term if total is None else total + term
                sums.append(total)
            nxt = jnp.where(lane == 127, 0.0, pltpu.roll(sums[0], 127, 1))
            both = jnp.concatenate([sums[1].astype(BF16), (sums[2] + nxt).astype(BF16)], 1)
            out_ref[ed, er] = mm(both, weave).astype(BF16)


def shifted_2(value, axis, steps):
    count = lax.axis_size(axis)
    first, last = (max(0, -steps), min(count, count - steps))
    return lax.ppermute(value, axis, [(source, source + steps) for source in range(first, last)])


def exchange(value, axis, groups=None):
    return lax.all_to_all(
        value, axis, split_axis=0, concat_axis=0, axis_index_groups=groups, tiled=True
    )


def add_up(value):
    size = value.size * 2
    out_shape = jax.ShapeDtypeStruct((8, 4, 3456), BF16)
    return call(sum_body, out_shape, [VMEM], (size, size))(value)


def on_device(volume, weights, out_error):
    core = (lax.axis_index("slab") & 1).astype(jnp.int32).reshape(1)
    taps = weights.reshape(9, 3, 128, 256)
    shape = jax.ShapeDtypeStruct
    mb = 1 << 20

    send = call(
        pack_body,
        shape((8, 7, 16, 256), BF16),
        [ANY] * 2,
        (2 * mb, mb),
        [
            pltpu.VMEM(volume.shape, BF16),
            pltpu.VMEM(out_error.shape, BF16),
            pltpu.SemaphoreType.DMA((2,)),
        ],
        62500000,
    )(volume, out_error)
    received = exchange(send, "filt")
    even, odd = call(
        turn_body, (shape((256, 1152), BF16), shape((512, 1152), BF16)), [VMEM], (452 * mb, 4 * mb)
    )(taps)
    rim = shifted_2(received[:, 3:6], "slab", 1)
    stack = shape((1152, 128), BF16)
    grad, both, ze, zo, part = call(
        conv_body,
        (shape((256, 128), BF16), shape((256, 256), BF16), stack, stack, shape((128, 3456), BF16)),
        [SMEM, VMEM, VMEM, VMEM, VMEM],
        (453 * mb, 4 * mb),
    )(core, received, rim, even, odd)

    other = lax.ppermute(part, "slab", CORE_PAIRS)
    right = shifted_2(grad, "filt", -1)
    part = call(
        keep_body, shape((128, 3456), BF16), [SMEM, VMEM, VMEM, VMEM, VMEM], (113 * mb, 3 * mb)
    )(core, both, ze, zo, other)
    tiles = add_up(exchange(part.reshape(4, 32, 3456), "slab", X_RINGS))
    tiles = add_up(exchange(tiles, "filt"))
    tiles, right = lax.optimization_barrier((tiles, right))
    own = jnp.stack([grad, right])
    upper = shifted_2(own, "slab", -1)
    tiles = add_up(exchange(tiles, "slab", Z_RINGS))
    tiles, upper = lax.optimization_barrier((tiles, upper))
    in_grad = call(
        input_body, shape((2, 2, 128, 256), BF16), [VMEM] * 3, (226 * mb, 3 * mb)
    )(own, upper, taps)
    in_grad = in_grad.transpose(0, 2, 1, 3)

    tiles = exchange(tiles, "slab", XC_RINGS)
    out = call(last_body, shape((27, 32, 128), F32), [VMEM], (mb, mb))(tiles)
    weight_grad = out.reshape(3, 3, 3, 32, 128).transpose(0, 1, 2, 4, 3)
    return (in_grad, weight_grad)


def solution(mesh):
    in_specs = (P("slab", "filt", None, None), P(), P("slab", "filt", None, None))
    out_specs = (P("slab", None, "filt", None), P(None, None, None, None, "filt"))
    return jax.shard_map(
        on_device, mesh=mesh, in_specs=in_specs, out_specs=out_specs, check_vma=False
    )
```

```python
import jax
import jax.numpy as jnp
from jax import lax
from jax.experimental import pallas as pl
from jax.experimental.pallas import tpu as pltpu
from jax.sharding import PartitionSpec as P

F32 = jnp.float32
BF16 = jnp.bfloat16
VMEM = pl.BlockSpec(memory_space=pltpu.VMEM)
ANY = pl.BlockSpec(memory_space=pl.ANY)
SMEM = pl.BlockSpec(memory_space=pltpu.SMEM)
LIMIT = 48 * 1024 * 1024

def slab_of(x, z, core):
    return (x * 8 + z) * 2 + core


X4, Z4, B2 = range(4), range(4), range(2)
WIDE = [[slab_of(x, 2 * zh + zl, c) for x in X4 for zl in B2] for zh in Z4 for c in B2]
FAR = [[slab_of(x, 2 * zh + zl, c) for zh in Z4] for x in X4 for zl in B2 for c in B2]
NEAR = [[slab_of(x, 2 * zh + zl, c) for x in X4 for zl in B2 for c in B2] for zh in Z4]
CORE_PAIRS = [(s, s ^ 1) for s in range(64)]


def call(body, out_shape, in_specs, cost, scratch=(), limit=LIMIT):
    many = isinstance(out_shape, (tuple, list))
    return pl.pallas_call(
        body,
        out_shape=out_shape,
        in_specs=in_specs,
        out_specs=[VMEM] * len(out_shape) if many else VMEM,
        scratch_shapes=list(scratch),
        compiler_params=pltpu.CompilerParams(vmem_limit_bytes=limit),
        cost_estimate=pl.CostEstimate(flops=cost[0], bytes_accessed=cost[1], transcendentals=0),
    )


def mm(left, right):
    return jnp.dot(left, right, preferred_element_type=F32)


def mm_nt(left, right):
    return lax.dot_general(left, right, (((1,), (1,)), ((), ())), preferred_element_type=F32)


def ones_where(cond):
    return jnp.where(cond, 1.0, 0.0).astype(BF16)


def iotas(rows, cols):
    return (
        lax.broadcasted_iota(jnp.int32, (rows, cols), 0),
        lax.broadcasted_iota(jnp.int32, (rows, cols), 1),
    )


def pack_body(vol_hbm, err_hbm, send_ref, vol_ref, err_ref, sems):
    copies = [
        pltpu.make_async_copy(vol_hbm, vol_ref, sems.at[0]),
        pltpu.make_async_copy(err_hbm, err_ref, sems.at[1]),
    ]
    for copy in copies:
        copy.start()
    i, j = iotas(256, 256)
    row_first = ones_where(j == ((i & 15) << 4) + (i >> 4))
    even_odd = ones_where(i == ((j & 127) << 1) + (j >> 7))
    error_rows = ones_where(j == ((i & 31) << 3) + (i >> 5))
    copies[0].wait()
    for p in range(2):
        plane = vol_ref[p].reshape(256, 256)
        plane = mm(row_first, plane).astype(BF16)
        plane = mm(plane, even_odd).astype(BF16)
        for y in range(8):
            for b in range(3):
                row = 2 * y - 1 + b
                if row < 0:
                    piece = jnp.zeros((16, 256), BF16)
                else:
                    piece = plane[row * 16 : row * 16 + 16]
                send_ref[y, p * 3 + b] = piece
    copies[1].wait()
    error = mm(error_rows, err_ref[0].reshape(256, 128)).astype(BF16)
    for y in range(8):
        for u in range(2):
            start = y * 32 + u * 16
            send_ref[y, 6, :, u * 128 : u * 128 + 128] = error[start : start + 16]


def turn_body(w_ref, even_ref, odd_ref):
    i, j = iotas(256, 256)
    same = ones_where(i == j)
    for ab in range(9):
        cols = slice(ab * 128, ab * 128 + 128)
        even_ref[:, cols] = mm_nt(same, w_ref[ab, 1]).astype(BF16)
        odd_ref[:256, cols] = mm_nt(same, w_ref[ab, 2]).astype(BF16)
        odd_ref[256:, cols] = mm_nt(same, w_ref[ab, 0]).astype(BF16)


def core_rows(core):
    i, j = iotas(128, 256)
    return ones_where(j == (((i >> 1) & 7) << 5) + ((i >> 4) << 2) + (i & 1) + core * 2)


def taps_of(order, both, ze, zo):
    now = mm(order, both[:, :128]).astype(BF16)
    after = mm(order, both[:, 128:]).astype(BF16)
    return mm_nt(after, zo[...]), mm_nt(now, ze[...]), mm_nt(now, zo[...])


def conv_body(core_ref, rec_ref, rim_ref, even_ref, odd_ref, grad_ref, both_ref, ze, zo, part_ref):
    for a in range(3):
        for b in range(3):
            rows = slice((a * 3 + b) * 128, (a * 3 + b) * 128 + 128)
            tile = rim_ref[:, b] if a == 0 else rec_ref[:, (a - 1) * 3 + b]
            tile = tile.reshape(128, 256)
            ze[rows] = tile[:, :128]
            zo[rows] = tile[:, 128:]
    center = mm(even_ref[...], ze[...])
    sides = mm(odd_ref[...], zo[...])
    errors = []
    for y in range(8):
        errors += [rec_ref[y, 6][:, :128], rec_ref[y, 6][:, 128:]]
    error = jnp.concatenate(errors, 0).astype(F32)
    lane = lax.broadcasted_iota(jnp.int32, (256, 128), 1)
    before = jnp.where(lane == 0, 0.0, pltpu.roll(sides[256:], 1, 1))
    preact = center + sides[:256] + before
    sigma = jax.nn.sigmoid(preact)
    grad = (error * (sigma * (1.0 + preact * (1.0 - sigma)))).astype(BF16)
    grad_ref[...] = grad
    after = jnp.where(lane == 127, 0.0, pltpu.roll(grad.astype(F32), 127, 1)).astype(BF16)
    both = jnp.concatenate([grad, after], 1)
    both_ref[...] = both
    parts = taps_of(core_rows(1 - core_ref[0]), both, ze, zo)
    for c in range(3):
        part_ref[:, c * 1152 : c * 1152 + 1152] = parts[c].astype(BF16)


def keep_body(core_ref, both_ref, ze, zo, other_ref, part_ref):
    parts = taps_of(core_rows(core_ref[0]), both_ref[...], ze, zo)
    for c in range(3):
        cols = slice(c * 1152, c * 1152 + 1152)
        part_ref[:, cols] = (parts[c] + other_ref[:, cols].astype(F32)).astype(BF16)


def sum_body(in_ref, out_ref):
    total = in_ref[0].astype(F32)
    for n in range(1, in_ref.shape[0]):
        total = total + in_ref[n].astype(F32)
    for n in range(out_ref.shape[0]):
        rows = total if total.shape[0] == 2 else total[2 * n : 2 * n + 2]
        out_ref[n] = rows.astype(BF16)


def last_body(in_ref, out_ref):
    for m in range(16):
        rows = in_ref[m].astype(F32) * (1.0 / 256.0)
        for c in range(3):
            for ab in range(9):
                start = (c * 9 + ab) * 128
                out_ref[ab * 3 + c, 2 * m : 2 * m + 2] = rows[:, start : start + 128]


def input_body(own_ref, up_ref, w_ref, out_ref):
    lane = lax.broadcasted_iota(jnp.int32, (128, 128), 1)
    i, j = iotas(256, 256)
    weave = ones_where(j == ((i & 127) << 1) + (i >> 7))
    taps = ((( 1, 0),), ((2, 0), (0, 1)))
    for ed in range(2):
        for er in range(2):
            sums = []
            for c in range(3):
                total = None
                for a, od in taps[ed]:
                    for b, pd in taps[er]:
                        grad = (up_ref if od else own_ref)[pd]
                        term = mm(w_ref[a * 3 + b, c], grad)
                        total = term if total is None else total + term
                sums.append(total)
            nxt = jnp.where(lane == 127, 0.0, pltpu.roll(sums[0], 127, 1))
            both = jnp.concatenate([sums[1].astype(BF16), (sums[2] + nxt).astype(BF16)], 1)
            out_ref[ed, er] = mm(both, weave).astype(BF16)


def shifted_2(value, axis, steps):
    count = lax.axis_size(axis)
    first, last = (max(0, -steps), min(count, count - steps))
    return lax.ppermute(value, axis, [(source, source + steps) for source in range(first, last)])


def exchange(value, axis, groups=None):
    return lax.all_to_all(
        value, axis, split_axis=0, concat_axis=0, axis_index_groups=groups, tiled=True
    )


def add_up(value, count):
    size = value.size * 2
    out_shape = jax.ShapeDtypeStruct((count, 2, 3456), BF16)
    return call(sum_body, out_shape, [VMEM], (size, size))(value)


def on_device(volume, weights, out_error):
    core = (lax.axis_index("slab") & 1).astype(jnp.int32).reshape(1)
    taps = weights.reshape(9, 3, 128, 256)
    shape = jax.ShapeDtypeStruct
    mb = 1 << 20

    send = call(
        pack_body,
        shape((8, 7, 16, 256), BF16),
        [ANY] * 2,
        (2 * mb, mb),
        [
            pltpu.VMEM(volume.shape, BF16),
            pltpu.VMEM(out_error.shape, BF16),
            pltpu.SemaphoreType.DMA((2,)),
        ],
        62500000,
    )(volume, out_error)
    received = exchange(send, "filt")
    even, odd = call(
        turn_body, (shape((256, 1152), BF16), shape((512, 1152), BF16)), [VMEM], (452 * mb, 4 * mb)
    )(taps)
    rim = shifted_2(received[:, 3:6], "slab", 1)
    stack = shape((1152, 128), BF16)
    grad, both, ze, zo, part = call(
        conv_body,
        (shape((256, 128), BF16), shape((256, 256), BF16), stack, stack, shape((128, 3456), BF16)),
        [SMEM, VMEM, VMEM, VMEM, VMEM],
        (453 * mb, 4 * mb),
    )(core, received, rim, even, odd)

    other = lax.ppermute(part, "slab", CORE_PAIRS)
    right = shifted_2(grad, "filt", -1)
    part = call(
        keep_body, shape((128, 3456), BF16), [SMEM, VMEM, VMEM, VMEM, VMEM], (113 * mb, 3 * mb)
    )(core, both, ze, zo, other)
    tiles = add_up(exchange(part.reshape(8, 16, 3456), "slab", WIDE), 8)
    tiles = add_up(exchange(tiles, "filt"), 4)
    tiles, right = lax.optimization_barrier((tiles, right))
    own = jnp.stack([grad, right])
    upper = shifted_2(own, "slab", -1)
    tiles = add_up(exchange(tiles, "slab", FAR), 16)
    tiles, upper = lax.optimization_barrier((tiles, upper))
    in_grad = call(
        input_body, shape((2, 2, 128, 256), BF16), [VMEM] * 3, (226 * mb, 3 * mb)
    )(own, upper, taps)
    in_grad = in_grad.transpose(0, 2, 1, 3)

    tiles = exchange(tiles, "slab", NEAR)
    out = call(last_body, shape((27, 32, 128), F32), [VMEM], (mb, mb))(tiles)
    weight_grad = out.reshape(3, 3, 3, 32, 128).transpose(0, 1, 2, 4, 3)
    return (in_grad, weight_grad)


def solution(mesh):
    in_specs = (P("slab", "filt", None, None), P(), P("slab", "filt", None, None))
    out_specs = (P("slab", None, "filt", None), P(None, None, None, None, "filt"))
    return jax.shard_map(
        on_device, mesh=mesh, in_specs=in_specs, out_specs=out_specs, check_vma=False
    )
```

```python
import jax
import jax.numpy as jnp
from jax import lax
from jax.experimental import pallas as pl
from jax.experimental.pallas import tpu as pltpu
from jax.sharding import PartitionSpec as P

F32 = jnp.float32
BF16 = jnp.bfloat16
VMEM = pl.BlockSpec(memory_space=pltpu.VMEM)
ANY = pl.BlockSpec(memory_space=pl.ANY)
SMEM = pl.BlockSpec(memory_space=pltpu.SMEM)
LIMIT = 48 * 1024 * 1024

def slab_of(x, z, core):
    return (x * 8 + z) * 2 + core


X4, Z4, B2 = range(4), range(4), range(2)
WIDE = [[slab_of(x, 2 * zh + zl, c) for x in X4 for zl in B2] for zh in Z4 for c in B2]
FAR = [[slab_of(x, 2 * zh + zl, c) for zh in Z4] for x in X4 for zl in B2 for c in B2]
NEAR = [[slab_of(x, 2 * zh + zl, c) for x in X4 for zl in B2 for c in B2] for zh in Z4]
CORE_PAIRS = [(s, s ^ 1) for s in range(64)]


def call(body, out_shape, in_specs, cost, scratch=(), limit=LIMIT):
    many = isinstance(out_shape, (tuple, list))
    return pl.pallas_call(
        body,
        out_shape=out_shape,
        in_specs=in_specs,
        out_specs=[VMEM] * len(out_shape) if many else VMEM,
        scratch_shapes=list(scratch),
        compiler_params=pltpu.CompilerParams(vmem_limit_bytes=limit),
        cost_estimate=pl.CostEstimate(flops=cost[0], bytes_accessed=cost[1], transcendentals=0),
    )


def mm(left, right):
    return jnp.dot(left, right, preferred_element_type=F32)


def mm_nt(left, right):
    return lax.dot_general(left, right, (((1,), (1,)), ((), ())), preferred_element_type=F32)


def ones_where(cond):
    return jnp.where(cond, 1.0, 0.0).astype(BF16)


def iotas(rows, cols):
    return (
        lax.broadcasted_iota(jnp.int32, (rows, cols), 0),
        lax.broadcasted_iota(jnp.int32, (rows, cols), 1),
    )


def pack_body(vol_hbm, err_hbm, send_ref, vol_ref, err_ref, sems):
    copies = [
        pltpu.make_async_copy(vol_hbm, vol_ref, sems.at[0]),
        pltpu.make_async_copy(err_hbm, err_ref, sems.at[1]),
    ]
    for copy in copies:
        copy.start()
    i, j = iotas(256, 256)
    row_first = ones_where(j == ((i & 15) << 4) + (i >> 4))
    even_odd = ones_where(i == ((j & 127) << 1) + (j >> 7))
    error_rows = ones_where(j == ((i & 31) << 3) + (i >> 5))
    copies[0].wait()
    for p in range(2):
        plane = vol_ref[p].reshape(256, 256)
        plane = mm(row_first, plane).astype(BF16)
        plane = mm(plane, even_odd).astype(BF16)
        for y in range(8):
            for b in range(3):
                row = 2 * y - 1 + b
                if row < 0:
                    piece = jnp.zeros((16, 256), BF16)
                else:
                    piece = plane[row * 16 : row * 16 + 16]
                send_ref[y, p * 3 + b] = piece
    copies[1].wait()
    error = mm(error_rows, err_ref[0].reshape(256, 128)).astype(BF16)
    for y in range(8):
        for u in range(2):
            start = y * 32 + u * 16
            send_ref[y, 6, :, u * 128 : u * 128 + 128] = error[start : start + 16]


def turn_body(w_ref, even_ref, odd_ref):
    i, j = iotas(256, 256)
    same = ones_where(i == j)
    for ab in range(9):
        cols = slice(ab * 128, ab * 128 + 128)
        even_ref[:, cols] = mm_nt(same, w_ref[ab, 1]).astype(BF16)
        odd_ref[:256, cols] = mm_nt(same, w_ref[ab, 2]).astype(BF16)
        odd_ref[256:, cols] = mm_nt(same, w_ref[ab, 0]).astype(BF16)


def core_rows(core):
    i, j = iotas(128, 256)
    return ones_where(j == (((i >> 1) & 7) << 5) + ((i >> 4) << 2) + (i & 1) + core * 2)


def taps_of(order, both, ze, zo):
    now = mm(order, both[:, :128]).astype(BF16)
    after = mm(order, both[:, 128:]).astype(BF16)
    return mm_nt(after, zo[...]), mm_nt(now, ze[...]), mm_nt(now, zo[...])


def conv_body(core_ref, rec_ref, rim_ref, even_ref, odd_ref, grad_ref, both_ref, ze, zo, part_ref):
    for a in range(3):
        for b in range(3):
            rows = slice((a * 3 + b) * 128, (a * 3 + b) * 128 + 128)
            tile = rim_ref[:, b] if a == 0 else rec_ref[:, (a - 1) * 3 + b]
            tile = tile.reshape(128, 256)
            ze[rows] = tile[:, :128]
            zo[rows] = tile[:, 128:]
    center = mm(even_ref[...], ze[...])
    sides = mm(odd_ref[...], zo[...])
    errors = []
    for y in range(8):
        errors += [rec_ref[y, 6][:, :128], rec_ref[y, 6][:, 128:]]
    error = jnp.concatenate(errors, 0).astype(F32)
    lane = lax.broadcasted_iota(jnp.int32, (256, 128), 1)
    before = jnp.where(lane == 0, 0.0, pltpu.roll(sides[256:], 1, 1))
    preact = center + sides[:256] + before
    sigma = jax.nn.sigmoid(preact)
    grad = (error * (sigma * (1.0 + preact * (1.0 - sigma)))).astype(BF16)
    grad_ref[...] = grad
    after = jnp.where(lane == 127, 0.0, pltpu.roll(grad.astype(F32), 127, 1)).astype(BF16)
    both = jnp.concatenate([grad, after], 1)
    both_ref[...] = both
    parts = taps_of(core_rows(1 - core_ref[0]), both, ze, zo)
    for c in range(3):
        part_ref[:, c * 1152 : c * 1152 + 1152] = parts[c].astype(BF16)


def keep_body(core_ref, both_ref, ze, zo, other_ref, part_ref):
    parts = taps_of(core_rows(core_ref[0]), both_ref[...], ze, zo)
    for c in range(3):
        cols = slice(c * 1152, c * 1152 + 1152)
        part_ref[:, cols] = (parts[c] + other_ref[:, cols].astype(F32)).astype(BF16)


def sum_body(in_ref, out_ref):
    total = in_ref[0].astype(F32)
    for n in range(1, in_ref.shape[0]):
        total = total + in_ref[n].astype(F32)
    for n in range(out_ref.shape[0]):
        rows = total if total.shape[0] == 2 else total[2 * n : 2 * n + 2]
        out_ref[n] = rows.astype(BF16)


def last_body(in_ref, out_ref):
    for m in range(16):
        rows = in_ref[m].astype(F32) * (1.0 / 256.0)
        for c in range(3):
            for ab in range(9):
                start = (c * 9 + ab) * 128
                out_ref[ab * 3 + c, 2 * m : 2 * m + 2] = rows[:, start : start + 128]


def input_body(own_ref, up_ref, w_ref, out_ref):
    lane = lax.broadcasted_iota(jnp.int32, (128, 128), 1)
    i, j = iotas(256, 256)
    weave = ones_where(j == ((i & 127) << 1) + (i >> 7))
    taps = ((( 1, 0),), ((2, 0), (0, 1)))
    for ed in range(2):
        for er in range(2):
            sums = []
            for c in range(3):
                total = None
                for a, od in taps[ed]:
                    for b, pd in taps[er]:
                        grad = (up_ref if od else own_ref)[pd]
                        term = mm(w_ref[a * 3 + b, c], grad)
                        total = term if total is None else total + term
                sums.append(total)
            nxt = jnp.where(lane == 127, 0.0, pltpu.roll(sums[0], 127, 1))
            both = jnp.concatenate([sums[1].astype(BF16), (sums[2] + nxt).astype(BF16)], 1)
            out_ref[ed, er] = mm(both, weave).astype(BF16)


def shifted_2(value, axis, steps):
    count = lax.axis_size(axis)
    first, last = (max(0, -steps), min(count, count - steps))
    return lax.ppermute(value, axis, [(source, source + steps) for source in range(first, last)])


def exchange(value, axis, groups=None):
    return lax.all_to_all(
        value, axis, split_axis=0, concat_axis=0, axis_index_groups=groups, tiled=True
    )


def add_up(value, count):
    size = value.size * 2
    out_shape = jax.ShapeDtypeStruct((count, 2, 3456), BF16)
    return call(sum_body, out_shape, [VMEM], (size, size))(value)


def on_device(volume, weights, out_error):
    core = (lax.axis_index("slab") & 1).astype(jnp.int32).reshape(1)
    taps = weights.reshape(9, 3, 128, 256)
    shape = jax.ShapeDtypeStruct
    mb = 1 << 20

    send = call(
        pack_body,
        shape((8, 7, 16, 256), BF16),
        [ANY] * 2,
        (2 * mb, mb),
        [
            pltpu.VMEM(volume.shape, BF16),
            pltpu.VMEM(out_error.shape, BF16),
            pltpu.SemaphoreType.DMA((2,)),
        ],
        62500000,
    )(volume, out_error)
    received = exchange(send, "filt")
    even, odd = call(
        turn_body, (shape((256, 1152), BF16), shape((512, 1152), BF16)), [VMEM], (452 * mb, 4 * mb)
    )(taps)
    rim = shifted_2(received[:, 3:6], "slab", 1)
    stack = shape((1152, 128), BF16)
    grad, both, ze, zo, part = call(
        conv_body,
        (shape((256, 128), BF16), shape((256, 256), BF16), stack, stack, shape((128, 3456), BF16)),
        [SMEM, VMEM, VMEM, VMEM, VMEM],
        (453 * mb, 4 * mb),
    )(core, received, rim, even, odd)

    other = lax.ppermute(part, "slab", CORE_PAIRS)
    right = shifted_2(grad, "filt", -1)
    part = call(
        keep_body, shape((128, 3456), BF16), [SMEM, VMEM, VMEM, VMEM, VMEM], (113 * mb, 3 * mb)
    )(core, both, ze, zo, other)
    own = jnp.stack([grad, right])
    upper = shifted_2(own, "slab", -1)
    tiles = exchange(part.reshape(8, 16, 3456), "slab", WIDE)
    tiles, upper = lax.optimization_barrier((tiles, upper))
    tiles = add_up(tiles, 8)
    tiles = add_up(exchange(tiles, "filt"), 4)
    tiles = add_up(exchange(tiles, "slab", FAR), 16)
    in_grad = call(
        input_body, shape((2, 2, 128, 256), BF16), [VMEM] * 3, (226 * mb, 3 * mb)
    )(own, upper, taps)
    in_grad = in_grad.transpose(0, 2, 1, 3)

    tiles = exchange(tiles, "slab", NEAR)
    out = call(last_body, shape((27, 32, 128), F32), [VMEM], (mb, mb))(tiles)
    weight_grad = out.reshape(3, 3, 3, 32, 128).transpose(0, 1, 2, 4, 3)
    return (in_grad, weight_grad)


def solution(mesh):
    in_specs = (P("slab", "filt", None, None), P(), P("slab", "filt", None, None))
    out_specs = (P("slab", None, "filt", None), P(None, None, None, None, "filt"))
    return jax.shard_map(
        on_device, mesh=mesh, in_specs=in_specs, out_specs=out_specs, check_vma=False
    )
```

```python
import jax
import jax.numpy as jnp
from jax import lax
from jax.experimental import pallas as pl
from jax.experimental.pallas import tpu as pltpu
from jax.sharding import PartitionSpec as P

F32 = jnp.float32
BF16 = jnp.bfloat16
VMEM = pl.BlockSpec(memory_space=pltpu.VMEM)
ANY = pl.BlockSpec(memory_space=pl.ANY)
SMEM = pl.BlockSpec(memory_space=pltpu.SMEM)
LIMIT = 48 * 1024 * 1024

def slab_of(x, z, core):
    return (x * 8 + z) * 2 + core


X4, Z4, B2 = range(4), range(4), range(2)
WIDE = [[slab_of(x, 2 * zh + zl, c) for x in X4 for zl in B2] for zh in Z4 for c in B2]
FAR = [[slab_of(x, 2 * zh + zl, c) for zh in Z4] for x in X4 for zl in B2 for c in B2]
NEAR = [[slab_of(x, 2 * zh + zl, c) for x in X4 for zl in B2 for c in B2] for zh in Z4]
CORE_PAIRS = [(s, s ^ 1) for s in range(64)]


def call(body, out_shape, in_specs, cost, scratch=(), limit=LIMIT, out_spec=VMEM):
    many = isinstance(out_shape, (tuple, list))
    return pl.pallas_call(
        body,
        out_shape=out_shape,
        in_specs=in_specs,
        out_specs=[out_spec] * len(out_shape) if many else out_spec,
        scratch_shapes=list(scratch),
        compiler_params=pltpu.CompilerParams(vmem_limit_bytes=limit),
        cost_estimate=pl.CostEstimate(flops=cost[0], bytes_accessed=cost[1], transcendentals=0),
    )


def mm(left, right):
    return jnp.dot(left, right, preferred_element_type=F32)


def mm_nt(left, right):
    return lax.dot_general(left, right, (((1,), (1,)), ((), ())), preferred_element_type=F32)


def ones_where(cond):
    return jnp.where(cond, 1.0, 0.0).astype(BF16)


def iotas(rows, cols):
    return (
        lax.broadcasted_iota(jnp.int32, (rows, cols), 0),
        lax.broadcasted_iota(jnp.int32, (rows, cols), 1),
    )


def pack_body(vol_hbm, err_hbm, send_hbm, vol_ref, err_ref, send_ref, sems, out_sems):
    copies = [
        pltpu.make_async_copy(vol_hbm.at[0], vol_ref.at[0], sems.at[0]),
        pltpu.make_async_copy(vol_hbm.at[1], vol_ref.at[1], sems.at[1]),
        pltpu.make_async_copy(err_hbm, err_ref, sems.at[2]),
    ]
    for copy in copies:
        copy.start()
    outs = [
        pltpu.make_async_copy(send_ref.at[:, 0:3], send_hbm.at[:, 0:3], out_sems.at[0]),
        pltpu.make_async_copy(send_ref.at[:, 3:6], send_hbm.at[:, 3:6], out_sems.at[1]),
        pltpu.make_async_copy(send_ref.at[:, 6:7], send_hbm.at[:, 6:7], out_sems.at[2]),
    ]
    i, j = iotas(256, 256)
    row_first = ones_where(j == ((i & 15) << 4) + (i >> 4))
    even_odd = ones_where(i == ((j & 127) << 1) + (j >> 7))
    error_rows = ones_where(j == ((i & 31) << 3) + (i >> 5))
    for p in range(2):
        copies[p].wait()
        plane = vol_ref[p].reshape(256, 256)
        plane = mm(row_first, plane).astype(BF16)
        plane = mm(plane, even_odd).astype(BF16)
        for y in range(8):
            for b in range(3):
                row = 2 * y - 1 + b
                if row < 0:
                    piece = jnp.zeros((16, 256), BF16)
                else:
                    piece = plane[row * 16 : row * 16 + 16]
                send_ref[y, p * 3 + b] = piece
        outs[p].start()
    copies[2].wait()
    error = mm(error_rows, err_ref[0].reshape(256, 128)).astype(BF16)
    for y in range(8):
        for u in range(2):
            start = y * 32 + u * 16
            send_ref[y, 6, :, u * 128 : u * 128 + 128] = error[start : start + 16]
    outs[2].start()
    for out in outs:
        out.wait()


def turn_body(w_ref, even_ref, odd_ref):
    i, j = iotas(256, 256)
    same = ones_where(i == j)
    for ab in range(9):
        cols = slice(ab * 128, ab * 128 + 128)
        even_ref[:, cols] = mm_nt(same, w_ref[ab, 1]).astype(BF16)
        odd_ref[:256, cols] = mm_nt(same, w_ref[ab, 2]).astype(BF16)
        odd_ref[256:, cols] = mm_nt(same, w_ref[ab, 0]).astype(BF16)


def core_rows(core):
    i, j = iotas(128, 256)
    return ones_where(j == (((i >> 1) & 7) << 5) + ((i >> 4) << 2) + (i & 1) + core * 2)


def taps_of(order, both, ze, zo):
    now = mm(order, both[:, :128]).astype(BF16)
    after = mm(order, both[:, 128:]).astype(BF16)
    return mm_nt(after, zo[...]), mm_nt(now, ze[...]), mm_nt(now, zo[...])


def conv_body(core_ref, rec_ref, rim_ref, even_ref, odd_ref, grad_ref, both_ref, ze, zo, part_ref):
    for a in range(3):
        for b in range(3):
            rows = slice((a * 3 + b) * 128, (a * 3 + b) * 128 + 128)
            tile = rim_ref[:, b] if a == 0 else rec_ref[:, (a - 1) * 3 + b]
            tile = tile.reshape(128, 256)
            ze[rows] = tile[:, :128]
            zo[rows] = tile[:, 128:]
    center = mm(even_ref[...], ze[...])
    sides = mm(odd_ref[...], zo[...])
    errors = []
    for y in range(8):
        errors += [rec_ref[y, 6][:, :128], rec_ref[y, 6][:, 128:]]
    error = jnp.concatenate(errors, 0).astype(F32)
    lane = lax.broadcasted_iota(jnp.int32, (256, 128), 1)
    before = jnp.where(lane == 0, 0.0, pltpu.roll(sides[256:], 1, 1))
    preact = center + sides[:256] + before
    sigma = jax.nn.sigmoid(preact)
    grad = (error * (sigma * (1.0 + preact * (1.0 - sigma)))).astype(BF16)
    grad_ref[...] = grad
    after = jnp.where(lane == 127, 0.0, pltpu.roll(grad.astype(F32), 127, 1)).astype(BF16)
    both = jnp.concatenate([grad, after], 1)
    both_ref[...] = both
    parts = taps_of(core_rows(1 - core_ref[0]), both, ze, zo)
    for c in range(3):
        part_ref[:, c * 1152 : c * 1152 + 1152] = parts[c].astype(BF16)


def keep_body(core_ref, both_ref, ze, zo, other_ref, part_hbm, part_ref, sems):
    order = core_rows(core_ref[0])
    both = both_ref[...]
    now = mm(order, both[:, :128]).astype(BF16)
    after = mm(order, both[:, 128:]).astype(BF16)
    copies = []
    for c, (grad, stack) in enumerate(((after, zo), (now, ze), (now, zo))):
        cols = pl.ds(c * 1152, 1152)
        total = mm_nt(grad, stack[...]) + other_ref[:, cols].astype(F32)
        part_ref[:, cols] = total.astype(BF16)
        copies.append(pltpu.make_async_copy(part_ref.at[:, cols], part_hbm.at[:, cols], sems.at[c]))
        copies[-1].start()
    for copy in copies:
        copy.wait()


def sum_body(in_ref, out_ref):
    total = in_ref[0].astype(F32)
    for n in range(1, in_ref.shape[0]):
        total = total + in_ref[n].astype(F32)
    for n in range(out_ref.shape[0]):
        rows = total if total.shape[0] == 2 else total[2 * n : 2 * n + 2]
        out_ref[n] = rows.astype(BF16)


def last_body(in_ref, out_ref):
    for m in range(16):
        rows = in_ref[m].astype(F32) * (1.0 / 256.0)
        for c in range(3):
            for ab in range(9):
                start = (c * 9 + ab) * 128
                out_ref[ab * 3 + c, 2 * m : 2 * m + 2] = rows[:, start : start + 128]


def input_body(own_ref, up_ref, w_ref, out_ref):
    lane = lax.broadcasted_iota(jnp.int32, (128, 128), 1)
    i, j = iotas(256, 256)
    weave = ones_where(j == ((i & 127) << 1) + (i >> 7))
    taps = ((( 1, 0),), ((2, 0), (0, 1)))
    for ed in range(2):
        for er in range(2):
            sums = []
            for c in range(3):
                total = None
                for a, od in taps[ed]:
                    for b, pd in taps[er]:
                        grad = (up_ref if od else own_ref)[pd]
                        term = mm(w_ref[a * 3 + b, c], grad)
                        total = term if total is None else total + term
                sums.append(total)
            nxt = jnp.where(lane == 127, 0.0, pltpu.roll(sums[0], 127, 1))
            both = jnp.concatenate([sums[1].astype(BF16), (sums[2] + nxt).astype(BF16)], 1)
            out_ref[ed, er] = mm(both, weave).astype(BF16)


def shifted_2(value, axis, steps):
    count = lax.axis_size(axis)
    first, last = (max(0, -steps), min(count, count - steps))
    return lax.ppermute(value, axis, [(source, source + steps) for source in range(first, last)])


def exchange(value, axis, groups=None):
    return lax.all_to_all(
        value, axis, split_axis=0, concat_axis=0, axis_index_groups=groups, tiled=True
    )


def add_up(value, count):
    size = value.size * 2
    out_shape = jax.ShapeDtypeStruct((count, 2, 3456), BF16)
    return call(sum_body, out_shape, [VMEM], (size, size))(value)


def on_device(volume, weights, out_error):
    core = (lax.axis_index("slab") & 1).astype(jnp.int32).reshape(1)
    taps = weights.reshape(9, 3, 128, 256)
    shape = jax.ShapeDtypeStruct
    mb = 1 << 20

    send = call(
        pack_body,
        shape((8, 7, 16, 256), BF16),
        [ANY] * 2,
        (2 * mb, mb),
        [
            pltpu.VMEM(volume.shape, BF16),
            pltpu.VMEM(out_error.shape, BF16),
            pltpu.VMEM((8, 7, 16, 256), BF16),
            pltpu.SemaphoreType.DMA((3,)),
            pltpu.SemaphoreType.DMA((3,)),
        ],
        62500000,
        ANY,
    )(volume, out_error)
    received = exchange(send, "filt")
    even, odd = call(
        turn_body, (shape((256, 1152), BF16), shape((512, 1152), BF16)), [VMEM], (452 * mb, 4 * mb)
    )(taps)
    rim = shifted_2(received[:, 3:6], "slab", 1)
    stack = shape((1152, 128), BF16)
    grad, both, ze, zo, part = call(
        conv_body,
        (shape((256, 128), BF16), shape((256, 256), BF16), stack, stack, shape((128, 3456), BF16)),
        [SMEM, VMEM, VMEM, VMEM, VMEM],
        (453 * mb, 4 * mb),
    )(core, received, rim, even, odd)

    other = lax.ppermute(part, "slab", CORE_PAIRS)
    right = shifted_2(grad, "filt", -1)
    part = call(
        keep_body,
        shape((128, 3456), BF16),
        [SMEM, VMEM, VMEM, VMEM, VMEM],
        (113 * mb, 3 * mb),
        [pltpu.VMEM((128, 3456), BF16), pltpu.SemaphoreType.DMA((3,))],
        LIMIT,
        ANY,
    )(core, both, ze, zo, other)
    own = jnp.stack([grad, right])
    upper = shifted_2(own, "slab", -1)
    tiles = exchange(part.reshape(8, 16, 3456), "slab", WIDE)
    tiles, upper = lax.optimization_barrier((tiles, upper))
    tiles = add_up(tiles, 8)
    tiles = add_up(exchange(tiles, "filt"), 4)
    tiles = add_up(exchange(tiles, "slab", FAR), 16)
    in_grad = call(
        input_body, shape((2, 2, 128, 256), BF16), [VMEM] * 3, (226 * mb, 3 * mb)
    )(own, upper, taps)
    in_grad = in_grad.transpose(0, 2, 1, 3)

    tiles = exchange(tiles, "slab", NEAR)
    out = call(last_body, shape((27, 32, 128), F32), [VMEM], (mb, mb))(tiles)
    weight_grad = out.reshape(3, 3, 3, 32, 128).transpose(0, 1, 2, 4, 3)
    return (in_grad, weight_grad)


def solution(mesh):
    in_specs = (P("slab", "filt", None, None), P(), P("slab", "filt", None, None))
    out_specs = (P("slab", None, "filt", None), P(None, None, None, None, "filt"))
    return jax.shard_map(
        on_device, mesh=mesh, in_specs=in_specs, out_specs=out_specs, check_vma=False
    )
```

```python
import jax
import jax.numpy as jnp
from jax import lax
from jax.experimental import pallas as pl
from jax.experimental.pallas import tpu as pltpu
from jax.sharding import PartitionSpec as P

F32 = jnp.float32
BF16 = jnp.bfloat16
VMEM = pl.BlockSpec(memory_space=pltpu.VMEM)
ANY = pl.BlockSpec(memory_space=pl.ANY)
SMEM = pl.BlockSpec(memory_space=pltpu.SMEM)
LIMIT = 48 * 1024 * 1024

def slab_of(x, z, core):
    return (x * 8 + z) * 2 + core


X4, Z4, B2 = range(4), range(4), range(2)
WIDE = [
    [slab_of(x, 2 * zh + zl, c) * 8 + y for x in X4 for zl in B2 for y in range(8)]
    for zh in Z4
    for c in B2
]
FAR = [[slab_of(x, 2 * zh + zl, c) for zh in Z4] for x in X4 for zl in B2 for c in B2]
NEAR = [[slab_of(x, 2 * zh + zl, c) for x in X4 for zl in B2 for c in B2] for zh in Z4]
CORE_PAIRS = [(s, s ^ 1) for s in range(64)]


def call(body, out_shape, in_specs, cost, scratch=(), limit=LIMIT, out_spec=VMEM):
    many = isinstance(out_shape, (tuple, list))
    return pl.pallas_call(
        body,
        out_shape=out_shape,
        in_specs=in_specs,
        out_specs=[out_spec] * len(out_shape) if many else out_spec,
        scratch_shapes=list(scratch),
        compiler_params=pltpu.CompilerParams(vmem_limit_bytes=limit),
        cost_estimate=pl.CostEstimate(flops=cost[0], bytes_accessed=cost[1], transcendentals=0),
    )


def mm(left, right):
    return jnp.dot(left, right, preferred_element_type=F32)


def mm_nt(left, right):
    return lax.dot_general(left, right, (((1,), (1,)), ((), ())), preferred_element_type=F32)


def ones_where(cond):
    return jnp.where(cond, 1.0, 0.0).astype(BF16)


def iotas(rows, cols):
    return (
        lax.broadcasted_iota(jnp.int32, (rows, cols), 0),
        lax.broadcasted_iota(jnp.int32, (rows, cols), 1),
    )


def pack_body(vol_hbm, err_hbm, send_hbm, vol_ref, err_ref, send_ref, sems, out_sems):
    copies = [
        pltpu.make_async_copy(vol_hbm.at[0], vol_ref.at[0], sems.at[0]),
        pltpu.make_async_copy(vol_hbm.at[1], vol_ref.at[1], sems.at[1]),
        pltpu.make_async_copy(err_hbm, err_ref, sems.at[2]),
    ]
    for copy in copies:
        copy.start()
    outs = [
        pltpu.make_async_copy(send_ref.at[:, 0:3], send_hbm.at[:, 0:3], out_sems.at[0]),
        pltpu.make_async_copy(send_ref.at[:, 3:6], send_hbm.at[:, 3:6], out_sems.at[1]),
        pltpu.make_async_copy(send_ref.at[:, 6:7], send_hbm.at[:, 6:7], out_sems.at[2]),
    ]
    i, j = iotas(256, 256)
    row_first = ones_where(j == ((i & 15) << 4) + (i >> 4))
    even_odd = ones_where(i == ((j & 127) << 1) + (j >> 7))
    error_rows = ones_where(j == ((i & 31) << 3) + (i >> 5))
    for p in range(2):
        copies[p].wait()
        plane = vol_ref[p].reshape(256, 256)
        plane = mm(row_first, plane).astype(BF16)
        plane = mm(plane, even_odd).astype(BF16)
        for y in range(8):
            for b in range(3):
                row = 2 * y - 1 + b
                if row < 0:
                    piece = jnp.zeros((16, 256), BF16)
                else:
                    piece = plane[row * 16 : row * 16 + 16]
                send_ref[y, p * 3 + b] = piece
        outs[p].start()
    copies[2].wait()
    error = mm(error_rows, err_ref[0].reshape(256, 128)).astype(BF16)
    for y in range(8):
        for u in range(2):
            start = y * 32 + u * 16
            send_ref[y, 6, :, u * 128 : u * 128 + 128] = error[start : start + 16]
    outs[2].start()
    for out in outs:
        out.wait()


def turn_body(w_ref, even_ref, odd_ref):
    i, j = iotas(256, 256)
    same = ones_where(i == j)
    for ab in range(9):
        cols = slice(ab * 128, ab * 128 + 128)
        even_ref[:, cols] = mm_nt(same, w_ref[ab, 1]).astype(BF16)
        odd_ref[:256, cols] = mm_nt(same, w_ref[ab, 2]).astype(BF16)
        odd_ref[256:, cols] = mm_nt(same, w_ref[ab, 0]).astype(BF16)


def core_rows(core):
    i, j = iotas(128, 256)
    return ones_where(j == (((i >> 1) & 7) << 5) + ((i >> 4) << 2) + (i & 1) + core * 2)


def taps_of(order, both, ze, zo):
    now = mm(order, both[:, :128]).astype(BF16)
    after = mm(order, both[:, 128:]).astype(BF16)
    return mm_nt(after, zo[...]), mm_nt(now, ze[...]), mm_nt(now, zo[...])


def conv_body(core_ref, rec_ref, rim_ref, even_ref, odd_ref, grad_ref, both_ref, ze, zo, part_ref):
    for a in range(3):
        for b in range(3):
            rows = slice((a * 3 + b) * 128, (a * 3 + b) * 128 + 128)
            tile = rim_ref[:, b] if a == 0 else rec_ref[:, (a - 1) * 3 + b]
            tile = tile.reshape(128, 256)
            ze[rows] = tile[:, :128]
            zo[rows] = tile[:, 128:]
    center = mm(even_ref[...], ze[...])
    sides = mm(odd_ref[...], zo[...])
    errors = []
    for y in range(8):
        errors += [rec_ref[y, 6][:, :128], rec_ref[y, 6][:, 128:]]
    error = jnp.concatenate(errors, 0).astype(F32)
    lane = lax.broadcasted_iota(jnp.int32, (256, 128), 1)
    before = jnp.where(lane == 0, 0.0, pltpu.roll(sides[256:], 1, 1))
    preact = center + sides[:256] + before
    sigma = jax.nn.sigmoid(preact)
    grad = (error * (sigma * (1.0 + preact * (1.0 - sigma)))).astype(BF16)
    grad_ref[...] = grad
    after = jnp.where(lane == 127, 0.0, pltpu.roll(grad.astype(F32), 127, 1)).astype(BF16)
    both = jnp.concatenate([grad, after], 1)
    both_ref[...] = both
    parts = taps_of(core_rows(1 - core_ref[0]), both, ze, zo)
    for c in range(3):
        part_ref[:, c * 1152 : c * 1152 + 1152] = parts[c].astype(BF16)


def keep_body(core_ref, both_ref, ze, zo, other_ref, part_hbm, part_ref, sems):
    order = core_rows(core_ref[0])
    both = both_ref[...]
    now = mm(order, both[:, :128]).astype(BF16)
    after = mm(order, both[:, 128:]).astype(BF16)
    copies = []
    for c, (grad, stack) in enumerate(((after, zo), (now, ze), (now, zo))):
        cols = pl.ds(c * 1152, 1152)
        total = mm_nt(grad, stack[...]) + other_ref[:, cols].astype(F32)
        part_ref[:, cols] = total.astype(BF16)
        copies.append(pltpu.make_async_copy(part_ref.at[:, cols], part_hbm.at[:, cols], sems.at[c]))
        copies[-1].start()
    for copy in copies:
        copy.wait()


def sum_body(in_ref, out_ref):
    total = in_ref[0].astype(F32)
    for n in range(1, in_ref.shape[0]):
        total = total + in_ref[n].astype(F32)
    for n in range(out_ref.shape[0]):
        rows = total if total.shape[0] == 2 else total[2 * n : 2 * n + 2]
        out_ref[n] = rows.astype(BF16)


def last_body(in_ref, out_ref):
    for m in range(16):
        rows = in_ref[m].astype(F32) * (1.0 / 256.0)
        for c in range(3):
            for ab in range(9):
                start = (c * 9 + ab) * 128
                out_ref[ab * 3 + c, 2 * m : 2 * m + 2] = rows[:, start : start + 128]


def input_body(own_ref, up_ref, w_ref, out_ref):
    lane = lax.broadcasted_iota(jnp.int32, (128, 128), 1)
    i, j = iotas(256, 256)
    weave = ones_where(j == ((i & 127) << 1) + (i >> 7))
    taps = ((( 1, 0),), ((2, 0), (0, 1)))
    for ed in range(2):
        for er in range(2):
            sums = []
            for c in range(3):
                total = None
                for a, od in taps[ed]:
                    for b, pd in taps[er]:
                        grad = (up_ref if od else own_ref)[pd]
                        term = mm(w_ref[a * 3 + b, c], grad)
                        total = term if total is None else total + term
                sums.append(total)
            nxt = jnp.where(lane == 127, 0.0, pltpu.roll(sums[0], 127, 1))
            both = jnp.concatenate([sums[1].astype(BF16), (sums[2] + nxt).astype(BF16)], 1)
            out_ref[ed, er] = mm(both, weave).astype(BF16)


def shifted_2(value, axis, steps):
    count = lax.axis_size(axis)
    first, last = (max(0, -steps), min(count, count - steps))
    return lax.ppermute(value, axis, [(source, source + steps) for source in range(first, last)])


def exchange(value, axis, groups=None):
    return lax.all_to_all(
        value, axis, split_axis=0, concat_axis=0, axis_index_groups=groups, tiled=True
    )


def add_up(value, count):
    size = value.size * 2
    out_shape = jax.ShapeDtypeStruct((count, 2, 3456), BF16)
    return call(sum_body, out_shape, [VMEM], (size, size))(value)


def on_device(volume, weights, out_error):
    core = (lax.axis_index("slab") & 1).astype(jnp.int32).reshape(1)
    taps = weights.reshape(9, 3, 128, 256)
    shape = jax.ShapeDtypeStruct
    mb = 1 << 20

    send = call(
        pack_body,
        shape((8, 7, 16, 256), BF16),
        [ANY] * 2,
        (2 * mb, mb),
        [
            pltpu.VMEM(volume.shape, BF16),
            pltpu.VMEM(out_error.shape, BF16),
            pltpu.VMEM((8, 7, 16, 256), BF16),
            pltpu.SemaphoreType.DMA((3,)),
            pltpu.SemaphoreType.DMA((3,)),
        ],
        62500000,
        ANY,
    )(volume, out_error)
    received = exchange(send, "filt")
    even, odd = call(
        turn_body, (shape((256, 1152), BF16), shape((512, 1152), BF16)), [VMEM], (452 * mb, 4 * mb)
    )(taps)
    rim = shifted_2(received[:, 3:6], "slab", 1)
    stack = shape((1152, 128), BF16)
    grad, both, ze, zo, part = call(
        conv_body,
        (shape((256, 128), BF16), shape((256, 256), BF16), stack, stack, shape((128, 3456), BF16)),
        [SMEM, VMEM, VMEM, VMEM, VMEM],
        (453 * mb, 4 * mb),
    )(core, received, rim, even, odd)

    other = lax.ppermute(part, "slab", CORE_PAIRS)
    right = shifted_2(grad, "filt", -1)
    part = call(
        keep_body,
        shape((128, 3456), BF16),
        [SMEM, VMEM, VMEM, VMEM, VMEM],
        (113 * mb, 3 * mb),
        [pltpu.VMEM((128, 3456), BF16), pltpu.SemaphoreType.DMA((3,))],
        LIMIT,
        ANY,
    )(core, both, ze, zo, other)
    own = jnp.stack([grad, right])
    upper = shifted_2(own, "slab", -1)
    tiles = exchange(part.reshape(64, 2, 3456), ("slab", "filt"), WIDE)
    tiles, upper = lax.optimization_barrier((tiles, upper))
    tiles = add_up(tiles, 4)
    tiles = add_up(exchange(tiles, "slab", FAR), 16)
    in_grad = call(
        input_body, shape((2, 2, 128, 256), BF16), [VMEM] * 3, (226 * mb, 3 * mb)
    )(own, upper, taps)
    in_grad = in_grad.transpose(0, 2, 1, 3)

    tiles = exchange(tiles, "slab", NEAR)
    out = call(last_body, shape((27, 32, 128), F32), [VMEM], (mb, mb))(tiles)
    weight_grad = out.reshape(3, 3, 3, 32, 128).transpose(0, 1, 2, 4, 3)
    return (in_grad, weight_grad)


def solution(mesh):
    in_specs = (P("slab", "filt", None, None), P(), P("slab", "filt", None, None))
    out_specs = (P("slab", None, "filt", None), P(None, None, None, None, "filt"))
    return jax.shard_map(
        on_device, mesh=mesh, in_specs=in_specs, out_specs=out_specs, check_vma=False
    )
```

```python
import jax
import jax.numpy as jnp
from jax import lax
from jax.experimental import pallas as pl
from jax.experimental.pallas import tpu as pltpu
from jax.sharding import PartitionSpec as P

F32 = jnp.float32
BF16 = jnp.bfloat16
VMEM = pl.BlockSpec(memory_space=pltpu.VMEM)
ANY = pl.BlockSpec(memory_space=pl.ANY)
SMEM = pl.BlockSpec(memory_space=pltpu.SMEM)
LIMIT = 48 * 1024 * 1024

def slab_of(x, z, core):
    return (x * 8 + z) * 2 + core


X4, Z4, B2 = range(4), range(4), range(2)
WIDE = [[slab_of(x, 2 * zh + zl, c) for x in X4 for zl in B2] for zh in Z4 for c in B2]
FAR = [[slab_of(x, 2 * zh + zl, c) for zh in Z4] for x in X4 for zl in B2 for c in B2]
NEAR = [[slab_of(x, 2 * zh + zl, c) for x in X4 for zl in B2 for c in B2] for zh in Z4]
CORE_PAIRS = [(s, s ^ 1) for s in range(64)]


def call(body, out_shape, in_specs, cost, scratch=(), limit=LIMIT, out_spec=VMEM):
    many = isinstance(out_shape, (tuple, list))
    return pl.pallas_call(
        body,
        out_shape=out_shape,
        in_specs=in_specs,
        out_specs=[out_spec] * len(out_shape) if many else out_spec,
        scratch_shapes=list(scratch),
        compiler_params=pltpu.CompilerParams(vmem_limit_bytes=limit),
        cost_estimate=pl.CostEstimate(flops=cost[0], bytes_accessed=cost[1], transcendentals=0),
    )


def mm(left, right):
    return jnp.dot(left, right, preferred_element_type=F32)


def mm_nt(left, right):
    return lax.dot_general(left, right, (((1,), (1,)), ((), ())), preferred_element_type=F32)


def ones_where(cond):
    return jnp.where(cond, 1.0, 0.0).astype(BF16)


def iotas(rows, cols):
    return (
        lax.broadcasted_iota(jnp.int32, (rows, cols), 0),
        lax.broadcasted_iota(jnp.int32, (rows, cols), 1),
    )


def pack_body(vol_hbm, err_hbm, send_ref, vol_ref, err_ref, sems):
    copies = [
        pltpu.make_async_copy(vol_hbm, vol_ref, sems.at[0]),
        pltpu.make_async_copy(err_hbm, err_ref, sems.at[1]),
    ]
    for copy in copies:
        copy.start()
    i, j = iotas(256, 256)
    row_first = ones_where(j == ((i & 15) << 4) + (i >> 4))
    even_odd = ones_where(i == ((j & 127) << 1) + (j >> 7))
    error_rows = ones_where(j == ((i & 31) << 3) + (i >> 5))
    copies[0].wait()
    for p in range(2):
        plane = vol_ref[p].reshape(256, 256)
        plane = mm(row_first, plane).astype(BF16)
        plane = mm(plane, even_odd).astype(BF16)
        for y in range(8):
            for b in range(3):
                row = 2 * y - 1 + b
                if row < 0:
                    piece = jnp.zeros((16, 256), BF16)
                else:
                    piece = plane[row * 16 : row * 16 + 16]
                send_ref[y, p * 3 + b] = piece
    copies[1].wait()
    error = mm(error_rows, err_ref[0].reshape(256, 128)).astype(BF16)
    for y in range(8):
        for u in range(2):
            start = y * 32 + u * 16
            send_ref[y, 6, :, u * 128 : u * 128 + 128] = error[start : start + 16]


def turn_body(w_ref, even_ref, odd_ref):
    i, j = iotas(256, 256)
    same = ones_where(i == j)
    for ab in range(9):
        cols = slice(ab * 128, ab * 128 + 128)
        even_ref[:, cols] = mm_nt(same, w_ref[ab, 1]).astype(BF16)
        odd_ref[:256, cols] = mm_nt(same, w_ref[ab, 2]).astype(BF16)
        odd_ref[256:, cols] = mm_nt(same, w_ref[ab, 0]).astype(BF16)


def core_rows(core):
    i, j = iotas(128, 256)
    return ones_where(j == (((i >> 1) & 7) << 5) + ((i >> 4) << 2) + (i & 1) + core * 2)


def taps_of(order, both, ze, zo):
    now = mm(order, both[:, :128]).astype(BF16)
    after = mm(order, both[:, 128:]).astype(BF16)
    return mm_nt(after, zo[...]), mm_nt(now, ze[...]), mm_nt(now, zo[...])


def conv_body(core_ref, rec_ref, rim_ref, even_ref, odd_ref, grad_ref, both_ref, ze, zo, part_ref):
    for a in range(3):
        for b in range(3):
            rows = slice((a * 3 + b) * 128, (a * 3 + b) * 128 + 128)
            tile = rim_ref[:, b] if a == 0 else rec_ref[:, (a - 1) * 3 + b]
            tile = tile.reshape(128, 256)
            ze[rows] = tile[:, :128]
            zo[rows] = tile[:, 128:]
    center = mm(even_ref[...], ze[...])
    sides = mm(odd_ref[...], zo[...])
    errors = []
    for y in range(8):
        errors += [rec_ref[y, 6][:, :128], rec_ref[y, 6][:, 128:]]
    error = jnp.concatenate(errors, 0).astype(F32)
    lane = lax.broadcasted_iota(jnp.int32, (256, 128), 1)
    before = jnp.where(lane == 0, 0.0, pltpu.roll(sides[256:], 1, 1))
    preact = center + sides[:256] + before
    sigma = jax.nn.sigmoid(preact)
    grad = (error * (sigma * (1.0 + preact * (1.0 - sigma)))).astype(BF16)
    grad_ref[...] = grad
    after = jnp.where(lane == 127, 0.0, pltpu.roll(grad.astype(F32), 127, 1)).astype(BF16)
    both = jnp.concatenate([grad, after], 1)
    both_ref[...] = both
    parts = taps_of(core_rows(1 - core_ref[0]), both, ze, zo)
    for c in range(3):
        part_ref[:, c * 1152 : c * 1152 + 1152] = parts[c].astype(BF16)


def keep_body(core_ref, both_ref, ze, zo, other_ref, part_hbm, part_ref, sems):
    order = core_rows(core_ref[0])
    both = both_ref[...]
    now = mm(order, both[:, :128]).astype(BF16)
    after = mm(order, both[:, 128:]).astype(BF16)
    copies = []
    for c, (grad, stack) in enumerate(((after, zo), (now, ze), (now, zo))):
        cols = pl.ds(c * 1152, 1152)
        total = mm_nt(grad, stack[...]) + other_ref[:, cols].astype(F32)
        part_ref[:, cols] = total.astype(BF16)
        copies.append(pltpu.make_async_copy(part_ref.at[:, cols], part_hbm.at[:, cols], sems.at[c]))
        copies[-1].start()
    for copy in copies:
        copy.wait()


def sum_body(in_ref, out_ref):
    total = in_ref[0].astype(F32)
    for n in range(1, in_ref.shape[0]):
        total = total + in_ref[n].astype(F32)
    for n in range(out_ref.shape[0]):
        rows = total if total.shape[0] == 2 else total[2 * n : 2 * n + 2]
        out_ref[n] = rows.astype(BF16)


def last_body(in_ref, out_ref):
    for m in range(16):
        rows = in_ref[m].astype(F32) * (1.0 / 256.0)
        for c in range(3):
            for ab in range(9):
                start = (c * 9 + ab) * 128
                out_ref[ab * 3 + c, 2 * m : 2 * m + 2] = rows[:, start : start + 128]


def input_body(own_ref, right_ref, up_ref, diag_ref, w_ref, out_ref):
    lane = lax.broadcasted_iota(jnp.int32, (128, 128), 1)
    i, j = iotas(256, 256)
    weave = ones_where(j == ((i & 127) << 1) + (i >> 7))
    taps = (((1, 0),), ((2, 0), (0, 1)))
    grads = ((own_ref[...], right_ref[...]), (up_ref[...], diag_ref[...]))
    for ed in range(2):
        for er in range(2):
            sums = []
            for c in range(3):
                total = None
                for a, od in taps[ed]:
                    for b, pd in taps[er]:
                        term = mm(w_ref[a * 3 + b, c], grads[od][pd])
                        total = term if total is None else total + term
                sums.append(total)
            nxt = jnp.where(lane == 127, 0.0, pltpu.roll(sums[0], 127, 1))
            both = jnp.concatenate([sums[1].astype(BF16), (sums[2] + nxt).astype(BF16)], 1)
            out_ref[ed, er] = mm(both, weave).astype(BF16)


def shifted_2(value, axis, steps):
    count = lax.axis_size(axis)
    first, last = (max(0, -steps), min(count, count - steps))
    return lax.ppermute(value, axis, [(source, source + steps) for source in range(first, last)])


def exchange(value, axis, groups=None):
    return lax.all_to_all(
        value, axis, split_axis=0, concat_axis=0, axis_index_groups=groups, tiled=True
    )


def add_up(value, count):
    size = value.size * 2
    out_shape = jax.ShapeDtypeStruct((count, 2, 3456), BF16)
    return call(sum_body, out_shape, [VMEM], (size, size))(value)


def on_device(volume, weights, out_error):
    core = (lax.axis_index("slab") & 1).astype(jnp.int32).reshape(1)
    taps = weights.reshape(9, 3, 128, 256)
    shape = jax.ShapeDtypeStruct
    mb = 1 << 20

    send = call(
        pack_body,
        shape((8, 7, 16, 256), BF16),
        [ANY] * 2,
        (2 * mb, mb),
        [
            pltpu.VMEM(volume.shape, BF16),
            pltpu.VMEM(out_error.shape, BF16),
            pltpu.SemaphoreType.DMA((2,)),
        ],
        62500000,
    )(volume, out_error)
    received = exchange(send, "filt")
    even, odd = call(
        turn_body, (shape((256, 1152), BF16), shape((512, 1152), BF16)), [VMEM], (452 * mb, 4 * mb)
    )(taps)
    rim = shifted_2(received[:, 3:6], "slab", 1)
    stack = shape((1152, 128), BF16)
    grad, both, ze, zo, part = call(
        conv_body,
        (shape((256, 128), BF16), shape((256, 256), BF16), stack, stack, shape((128, 3456), BF16)),
        [SMEM, VMEM, VMEM, VMEM, VMEM],
        (453 * mb, 4 * mb),
    )(core, received, rim, even, odd)

    other = lax.ppermute(part, "slab", CORE_PAIRS)
    right = shifted_2(grad, "filt", -1)
    part = call(
        keep_body,
        shape((128, 3456), BF16),
        [SMEM, VMEM, VMEM, VMEM, VMEM],
        (113 * mb, 3 * mb),
        [pltpu.VMEM((128, 3456), BF16), pltpu.SemaphoreType.DMA((3,))],
        LIMIT,
        ANY,
    )(core, both, ze, zo, other)
    upper = shifted_2(grad, "slab", -1)
    diagonal = lax.ppermute(
        grad,
        ("slab", "filt"),
        [(8 * s + y, 8 * s + y - 9) for s in range(1, 64) for y in range(1, 8)],
    )
    tiles = exchange(part.reshape(8, 16, 3456), "slab", WIDE)
    tiles, right, upper, diagonal = lax.optimization_barrier((tiles, right, upper, diagonal))
    tiles = add_up(tiles, 8)
    tiles = add_up(exchange(tiles, "filt"), 4)
    tiles = add_up(exchange(tiles, "slab", FAR), 16)
    in_grad = call(
        input_body, shape((2, 2, 128, 256), BF16), [VMEM] * 5, (226 * mb, 3 * mb)
    )(grad, right, upper, diagonal, taps)
    in_grad = in_grad.transpose(0, 2, 1, 3)

    tiles = exchange(tiles, "slab", NEAR)
    out = call(last_body, shape((27, 32, 128), F32), [VMEM], (mb, mb))(tiles)
    weight_grad = out.reshape(3, 3, 3, 32, 128).transpose(0, 1, 2, 4, 3)
    return (in_grad, weight_grad)


def solution(mesh):
    in_specs = (P("slab", "filt", None, None), P(), P("slab", "filt", None, None))
    out_specs = (P("slab", None, "filt", None), P(None, None, None, None, "filt"))
    return jax.shard_map(
        on_device, mesh=mesh, in_specs=in_specs, out_specs=out_specs, check_vma=False
    )
```

```python
import jax
import jax.numpy as jnp
from jax import lax
from jax.experimental import pallas as pl
from jax.experimental.pallas import tpu as pltpu
from jax.sharding import PartitionSpec as P

F32 = jnp.float32
BF16 = jnp.bfloat16
VMEM = pl.BlockSpec(memory_space=pltpu.VMEM)
ANY = pl.BlockSpec(memory_space=pl.ANY)
SMEM = pl.BlockSpec(memory_space=pltpu.SMEM)
LIMIT = 48 * 1024 * 1024

def slab_of(x, z, core):
    return (x * 8 + z) * 2 + core


X4, Z4, B2 = range(4), range(4), range(2)
WIDE = [[slab_of(x, 2 * zh + zl, c) for x in X4 for zl in B2] for zh in Z4 for c in B2]
FAR = [
    [slab_of(x, 2 * zh + zl, c) * 8 + y for zh in Z4 for y in range(8)]
    for x in X4
    for zl in B2
    for c in B2
]
NEAR = [[slab_of(x, 2 * zh + zl, c) for x in X4 for zl in B2 for c in B2] for zh in Z4]
CORE_PAIRS = [(s, s ^ 1) for s in range(64)]


def call(body, out_shape, in_specs, cost, scratch=(), limit=LIMIT, out_spec=VMEM):
    many = isinstance(out_shape, (tuple, list))
    return pl.pallas_call(
        body,
        out_shape=out_shape,
        in_specs=in_specs,
        out_specs=[out_spec] * len(out_shape) if many else out_spec,
        scratch_shapes=list(scratch),
        compiler_params=pltpu.CompilerParams(vmem_limit_bytes=limit),
        cost_estimate=pl.CostEstimate(flops=cost[0], bytes_accessed=cost[1], transcendentals=0),
    )


def mm(left, right):
    return jnp.dot(left, right, preferred_element_type=F32)


def mm_nt(left, right):
    return lax.dot_general(left, right, (((1,), (1,)), ((), ())), preferred_element_type=F32)


def ones_where(cond):
    return jnp.where(cond, 1.0, 0.0).astype(BF16)


def iotas(rows, cols):
    return (
        lax.broadcasted_iota(jnp.int32, (rows, cols), 0),
        lax.broadcasted_iota(jnp.int32, (rows, cols), 1),
    )


def pack_body(vol_hbm, err_hbm, send_ref, vol_ref, err_ref, sems):
    copies = [
        pltpu.make_async_copy(vol_hbm, vol_ref, sems.at[0]),
        pltpu.make_async_copy(err_hbm, err_ref, sems.at[1]),
    ]
    for copy in copies:
        copy.start()
    i, j = iotas(256, 256)
    row_first = ones_where(j == ((i & 15) << 4) + (i >> 4))
    even_odd = ones_where(i == ((j & 127) << 1) + (j >> 7))
    error_rows = ones_where(j == ((i & 31) << 3) + (i >> 5))
    copies[0].wait()
    for p in range(2):
        plane = vol_ref[p].reshape(256, 256)
        plane = mm(row_first, plane).astype(BF16)
        plane = mm(plane, even_odd).astype(BF16)
        for y in range(8):
            for b in range(3):
                row = 2 * y - 1 + b
                if row < 0:
                    piece = jnp.zeros((16, 256), BF16)
                else:
                    piece = plane[row * 16 : row * 16 + 16]
                send_ref[y, p * 3 + b] = piece
    copies[1].wait()
    error = mm(error_rows, err_ref[0].reshape(256, 128)).astype(BF16)
    for y in range(8):
        for u in range(2):
            start = y * 32 + u * 16
            send_ref[y, 6, :, u * 128 : u * 128 + 128] = error[start : start + 16]


def turn_body(w_ref, even_ref, odd_ref):
    i, j = iotas(256, 256)
    same = ones_where(i == j)
    for ab in range(9):
        cols = slice(ab * 128, ab * 128 + 128)
        even_ref[:, cols] = mm_nt(same, w_ref[ab, 1]).astype(BF16)
        odd_ref[:256, cols] = mm_nt(same, w_ref[ab, 2]).astype(BF16)
        odd_ref[256:, cols] = mm_nt(same, w_ref[ab, 0]).astype(BF16)


def core_rows(core):
    i, j = iotas(128, 256)
    return ones_where(j == (((i >> 1) & 7) << 5) + ((i >> 4) << 2) + (i & 1) + core * 2)


def taps_of(order, both, ze, zo):
    now = mm(order, both[:, :128]).astype(BF16)
    after = mm(order, both[:, 128:]).astype(BF16)
    return mm_nt(after, zo[...]), mm_nt(now, ze[...]), mm_nt(now, zo[...])


def conv_body(core_ref, rec_ref, rim_ref, even_ref, odd_ref, grad_ref, both_ref, ze, zo, part_ref):
    for a in range(3):
        for b in range(3):
            rows = slice((a * 3 + b) * 128, (a * 3 + b) * 128 + 128)
            tile = rim_ref[:, b] if a == 0 else rec_ref[:, (a - 1) * 3 + b]
            tile = tile.reshape(128, 256)
            ze[rows] = tile[:, :128]
            zo[rows] = tile[:, 128:]
    center = mm(even_ref[...], ze[...])
    sides = mm(odd_ref[...], zo[...])
    errors = []
    for y in range(8):
        errors += [rec_ref[y, 6][:, :128], rec_ref[y, 6][:, 128:]]
    error = jnp.concatenate(errors, 0).astype(F32)
    lane = lax.broadcasted_iota(jnp.int32, (256, 128), 1)
    before = jnp.where(lane == 0, 0.0, pltpu.roll(sides[256:], 1, 1))
    preact = center + sides[:256] + before
    sigma = jax.nn.sigmoid(preact)
    grad = (error * (sigma * (1.0 + preact * (1.0 - sigma)))).astype(BF16)
    grad_ref[...] = grad
    after = jnp.where(lane == 127, 0.0, pltpu.roll(grad.astype(F32), 127, 1)).astype(BF16)
    both = jnp.concatenate([grad, after], 1)
    both_ref[...] = both
    parts = taps_of(core_rows(1 - core_ref[0]), both, ze, zo)
    for c in range(3):
        part_ref[:, c * 1152 : c * 1152 + 1152] = parts[c].astype(BF16)


def keep_body(core_ref, both_ref, ze, zo, other_ref, part_hbm, part_ref, sems):
    order = core_rows(core_ref[0])
    both = both_ref[...]
    now = mm(order, both[:, :128]).astype(BF16)
    after = mm(order, both[:, 128:]).astype(BF16)
    copies = []
    for c, (grad, stack) in enumerate(((after, zo), (now, ze), (now, zo))):
        cols = pl.ds(c * 1152, 1152)
        total = mm_nt(grad, stack[...]) + other_ref[:, cols].astype(F32)
        part_ref[:, cols] = total.astype(BF16)
        copies.append(pltpu.make_async_copy(part_ref.at[:, cols], part_hbm.at[:, cols], sems.at[c]))
        copies[-1].start()
    for copy in copies:
        copy.wait()


def sum_body(in_ref, out_ref):
    total = in_ref[0].astype(F32)
    for n in range(1, in_ref.shape[0]):
        total = total + in_ref[n].astype(F32)
    for n in range(out_ref.shape[0]):
        start = 2 * n % total.shape[0]
        out_ref[n] = total[start : start + 2].astype(BF16)


def last_body(in_ref, out_ref):
    for m in range(16):
        rows = in_ref[m].astype(F32) * (1.0 / 256.0)
        for c in range(3):
            for ab in range(9):
                start = (c * 9 + ab) * 128
                out_ref[ab * 3 + c, 2 * m : 2 * m + 2] = rows[:, start : start + 128]


def input_body(own_ref, right_ref, up_ref, diag_ref, w_ref, out_ref):
    lane = lax.broadcasted_iota(jnp.int32, (128, 128), 1)
    i, j = iotas(256, 256)
    weave = ones_where(j == ((i & 127) << 1) + (i >> 7))
    taps = (((1, 0),), ((2, 0), (0, 1)))
    grads = ((own_ref[...], right_ref[...]), (up_ref[...], diag_ref[...]))
    for ed in range(2):
        for er in range(2):
            sums = []
            for c in range(3):
                total = None
                for a, od in taps[ed]:
                    for b, pd in taps[er]:
                        term = mm(w_ref[a * 3 + b, c], grads[od][pd])
                        total = term if total is None else total + term
                sums.append(total)
            nxt = jnp.where(lane == 127, 0.0, pltpu.roll(sums[0], 127, 1))
            both = jnp.concatenate([sums[1].astype(BF16), (sums[2] + nxt).astype(BF16)], 1)
            out_ref[ed, er] = mm(both, weave).astype(BF16)


def shifted_2(value, axis, steps):
    count = lax.axis_size(axis)
    first, last = (max(0, -steps), min(count, count - steps))
    return lax.ppermute(value, axis, [(source, source + steps) for source in range(first, last)])


def exchange(value, axis, groups=None):
    return lax.all_to_all(
        value, axis, split_axis=0, concat_axis=0, axis_index_groups=groups, tiled=True
    )


def add_up(value, count):
    size = value.size * 2
    out_shape = jax.ShapeDtypeStruct((count, 2, 3456), BF16)
    return call(sum_body, out_shape, [VMEM], (size, size))(value)


def on_device(volume, weights, out_error):
    core = (lax.axis_index("slab") & 1).astype(jnp.int32).reshape(1)
    taps = weights.reshape(9, 3, 128, 256)
    shape = jax.ShapeDtypeStruct
    mb = 1 << 20

    send = call(
        pack_body,
        shape((8, 7, 16, 256), BF16),
        [ANY] * 2,
        (2 * mb, mb),
        [
            pltpu.VMEM(volume.shape, BF16),
            pltpu.VMEM(out_error.shape, BF16),
            pltpu.SemaphoreType.DMA((2,)),
        ],
        62500000,
    )(volume, out_error)
    received = exchange(send, "filt")
    even, odd = call(
        turn_body, (shape((256, 1152), BF16), shape((512, 1152), BF16)), [VMEM], (452 * mb, 4 * mb)
    )(taps)
    rim = shifted_2(received[:, 3:6], "slab", 1)
    stack = shape((1152, 128), BF16)
    grad, both, ze, zo, part = call(
        conv_body,
        (shape((256, 128), BF16), shape((256, 256), BF16), stack, stack, shape((128, 3456), BF16)),
        [SMEM, VMEM, VMEM, VMEM, VMEM],
        (453 * mb, 4 * mb),
    )(core, received, rim, even, odd)

    other = lax.ppermute(part, "slab", CORE_PAIRS)
    right = shifted_2(grad, "filt", -1)
    part = call(
        keep_body,
        shape((128, 3456), BF16),
        [SMEM, VMEM, VMEM, VMEM, VMEM],
        (113 * mb, 3 * mb),
        [pltpu.VMEM((128, 3456), BF16), pltpu.SemaphoreType.DMA((3,))],
        LIMIT,
        ANY,
    )(core, both, ze, zo, other)
    upper = shifted_2(grad, "slab", -1)
    diagonal = lax.ppermute(
        grad,
        ("slab", "filt"),
        [(8 * s + y, 8 * s + y - 9) for s in range(1, 64) for y in range(1, 8)],
    )
    tiles = exchange(part.reshape(8, 16, 3456), "slab", WIDE)
    tiles, right, upper, diagonal = lax.optimization_barrier((tiles, right, upper, diagonal))
    tiles = add_up(tiles, 32)
    tiles = add_up(exchange(tiles, ("slab", "filt"), FAR), 16)
    in_grad = call(
        input_body, shape((2, 2, 128, 256), BF16), [VMEM] * 5, (226 * mb, 3 * mb)
    )(grad, right, upper, diagonal, taps)
    in_grad = in_grad.transpose(0, 2, 1, 3)

    tiles = exchange(tiles, "slab", NEAR)
    out = call(last_body, shape((27, 32, 128), F32), [VMEM], (mb, mb))(tiles)
    weight_grad = out.reshape(3, 3, 3, 32, 128).transpose(0, 1, 2, 4, 3)
    return (in_grad, weight_grad)


def solution(mesh):
    in_specs = (P("slab", "filt", None, None), P(), P("slab", "filt", None, None))
    out_specs = (P("slab", None, "filt", None), P(None, None, None, None, "filt"))
    return jax.shard_map(
        on_device, mesh=mesh, in_specs=in_specs, out_specs=out_specs, check_vma=False
    )
```

```python
import jax
import jax.numpy as jnp
from jax import lax
from jax.experimental import pallas as pl
from jax.experimental.pallas import tpu as pltpu
from jax.sharding import PartitionSpec as P

F32 = jnp.float32
BF16 = jnp.bfloat16
VMEM = pl.BlockSpec(memory_space=pltpu.VMEM)
ANY = pl.BlockSpec(memory_space=pl.ANY)
SMEM = pl.BlockSpec(memory_space=pltpu.SMEM)
LIMIT = 48 * 1024 * 1024

def slab_of(x, z, core):
    return (x * 8 + z) * 2 + core


X4, Q4, B2 = range(4), range(4), range(2)


def member_of(x, zh, zl, c, yh, yl):
    return slab_of(x, 2 * zh + zl, c) * 8 + 2 * yh + yl


WIDE = [
    [member_of(x, zh, zl, c, yh, yl) for x in X4 for zl in B2 for yl in B2]
    for zh in Q4
    for c in B2
    for yh in Q4
]
FAR = [
    [member_of(x, zh, zl, c, yh, yl) for zh in Q4 for yh in Q4]
    for x in X4
    for zl in B2
    for c in B2
    for yl in B2
]
NEAR = [[slab_of(x, 2 * zh + zl, c) for x in X4 for zl in B2 for c in B2] for zh in Q4]
CORE_PAIRS = [(s, s ^ 1) for s in range(64)]


def call(body, out_shape, in_specs, cost, scratch=(), limit=LIMIT, out_spec=VMEM):
    many = isinstance(out_shape, (tuple, list))
    return pl.pallas_call(
        body,
        out_shape=out_shape,
        in_specs=in_specs,
        out_specs=[out_spec] * len(out_shape) if many else out_spec,
        scratch_shapes=list(scratch),
        compiler_params=pltpu.CompilerParams(vmem_limit_bytes=limit),
        cost_estimate=pl.CostEstimate(flops=cost[0], bytes_accessed=cost[1], transcendentals=0),
    )


def mm(left, right):
    return jnp.dot(left, right, preferred_element_type=F32)


def mm_nt(left, right):
    return lax.dot_general(left, right, (((1,), (1,)), ((), ())), preferred_element_type=F32)


def ones_where(cond):
    return jnp.where(cond, 1.0, 0.0).astype(BF16)


def iotas(rows, cols):
    return (
        lax.broadcasted_iota(jnp.int32, (rows, cols), 0),
        lax.broadcasted_iota(jnp.int32, (rows, cols), 1),
    )


def pack_body(vol_hbm, err_hbm, send_ref, vol_ref, err_ref, sems):
    copies = [
        pltpu.make_async_copy(vol_hbm, vol_ref, sems.at[0]),
        pltpu.make_async_copy(err_hbm, err_ref, sems.at[1]),
    ]
    for copy in copies:
        copy.start()
    i, j = iotas(256, 256)
    row_first = ones_where(j == ((i & 15) << 4) + (i >> 4))
    even_odd = ones_where(i == ((j & 127) << 1) + (j >> 7))
    error_rows = ones_where(j == ((i & 31) << 3) + (i >> 5))
    copies[0].wait()
    for p in range(2):
        plane = vol_ref[p].reshape(256, 256)
        plane = mm(row_first, plane).astype(BF16)
        plane = mm(plane, even_odd).astype(BF16)
        for y in range(8):
            for b in range(3):
                row = 2 * y - 1 + b
                if row < 0:
                    piece = jnp.zeros((16, 256), BF16)
                else:
                    piece = plane[row * 16 : row * 16 + 16]
                send_ref[y, p * 3 + b] = piece
    copies[1].wait()
    error = mm(error_rows, err_ref[0].reshape(256, 128)).astype(BF16)
    for y in range(8):
        for u in range(2):
            start = y * 32 + u * 16
            send_ref[y, 6, :, u * 128 : u * 128 + 128] = error[start : start + 16]


def turn_body(w_ref, even_ref, odd_ref):
    i, j = iotas(256, 256)
    same = ones_where(i == j)
    for ab in range(9):
        cols = slice(ab * 128, ab * 128 + 128)
        even_ref[:, cols] = mm_nt(same, w_ref[ab, 1]).astype(BF16)
        odd_ref[:256, cols] = mm_nt(same, w_ref[ab, 2]).astype(BF16)
        odd_ref[256:, cols] = mm_nt(same, w_ref[ab, 0]).astype(BF16)


def core_rows(core):
    i, j = iotas(128, 256)
    tile = (((i >> 1) & 3) << 6) + (((i >> 3) & 1) << 5)
    return ones_where(j == tile + ((i >> 4) << 2) + (i & 1) + core * 2)


def taps_of(order, both, ze, zo):
    now = mm(order, both[:, :128]).astype(BF16)
    after = mm(order, both[:, 128:]).astype(BF16)
    return mm_nt(after, zo[...]), mm_nt(now, ze[...]), mm_nt(now, zo[...])


def conv_body(core_ref, rec_ref, rim_ref, even_ref, odd_ref, grad_ref, both_ref, ze, zo, part_ref):
    for a in range(3):
        for b in range(3):
            rows = slice((a * 3 + b) * 128, (a * 3 + b) * 128 + 128)
            tile = rim_ref[:, b] if a == 0 else rec_ref[:, (a - 1) * 3 + b]
            tile = tile.reshape(128, 256)
            ze[rows] = tile[:, :128]
            zo[rows] = tile[:, 128:]
    center = mm(even_ref[...], ze[...])
    sides = mm(odd_ref[...], zo[...])
    errors = []
    for y in range(8):
        errors += [rec_ref[y, 6][:, :128], rec_ref[y, 6][:, 128:]]
    error = jnp.concatenate(errors, 0).astype(F32)
    lane = lax.broadcasted_iota(jnp.int32, (256, 128), 1)
    before = jnp.where(lane == 0, 0.0, pltpu.roll(sides[256:], 1, 1))
    preact = center + sides[:256] + before
    sigma = jax.nn.sigmoid(preact)
    grad = (error * (sigma * (1.0 + preact * (1.0 - sigma)))).astype(BF16)
    grad_ref[...] = grad
    after = jnp.where(lane == 127, 0.0, pltpu.roll(grad.astype(F32), 127, 1)).astype(BF16)
    both = jnp.concatenate([grad, after], 1)
    both_ref[...] = both
    parts = taps_of(core_rows(1 - core_ref[0]), both, ze, zo)
    for c in range(3):
        part_ref[:, c * 1152 : c * 1152 + 1152] = parts[c].astype(BF16)


def keep_body(core_ref, both_ref, ze, zo, other_ref, part_hbm, part_ref, sems):
    order = core_rows(core_ref[0])
    both = both_ref[...]
    now = mm(order, both[:, :128]).astype(BF16)
    after = mm(order, both[:, 128:]).astype(BF16)
    copies = []
    for c, (grad, stack) in enumerate(((after, zo), (now, ze), (now, zo))):
        cols = pl.ds(c * 1152, 1152)
        total = mm_nt(grad, stack[...]) + other_ref[:, cols].astype(F32)
        part_ref[:, cols] = total.astype(BF16)
        copies.append(pltpu.make_async_copy(part_ref.at[:, cols], part_hbm.at[:, cols], sems.at[c]))
        copies[-1].start()
    for copy in copies:
        copy.wait()


def sum_body(in_ref, out_ref):
    total = in_ref[0].astype(F32)
    for n in range(1, in_ref.shape[0]):
        total = total + in_ref[n].astype(F32)
    for n in range(out_ref.shape[0]):
        start = 2 * n % total.shape[0]
        out_ref[n] = total[start : start + 2].astype(BF16)


def last_body(in_ref, out_ref):
    for m in range(16):
        rows = in_ref[m].astype(F32) * (1.0 / 256.0)
        for c in range(3):
            for ab in range(9):
                start = (c * 9 + ab) * 128
                out_ref[ab * 3 + c, 2 * m : 2 * m + 2] = rows[:, start : start + 128]


def input_body(own_ref, right_ref, up_ref, diag_ref, w_ref, out_ref):
    lane = lax.broadcasted_iota(jnp.int32, (128, 128), 1)
    i, j = iotas(256, 256)
    weave = ones_where(j == ((i & 127) << 1) + (i >> 7))
    taps = (((1, 0),), ((2, 0), (0, 1)))
    grads = ((own_ref[...], right_ref[...]), (up_ref[...], diag_ref[...]))
    for ed in range(2):
        for er in range(2):
            sums = []
            for c in range(3):
                total = None
                for a, od in taps[ed]:
                    for b, pd in taps[er]:
                        term = mm(w_ref[a * 3 + b, c], grads[od][pd])
                        total = term if total is None else total + term
                sums.append(total)
            nxt = jnp.where(lane == 127, 0.0, pltpu.roll(sums[0], 127, 1))
            both = jnp.concatenate([sums[1].astype(BF16), (sums[2] + nxt).astype(BF16)], 1)
            out_ref[ed, er] = mm(both, weave).astype(BF16)


def shifted_2(value, axis, steps):
    count = lax.axis_size(axis)
    first, last = (max(0, -steps), min(count, count - steps))
    return lax.ppermute(value, axis, [(source, source + steps) for source in range(first, last)])


def exchange(value, axis, groups=None):
    return lax.all_to_all(
        value, axis, split_axis=0, concat_axis=0, axis_index_groups=groups, tiled=True
    )


def add_up(value, count):
    size = value.size * 2
    out_shape = jax.ShapeDtypeStruct((count, 2, 3456), BF16)
    return call(sum_body, out_shape, [VMEM], (size, size))(value)


def on_device(volume, weights, out_error):
    core = (lax.axis_index("slab") & 1).astype(jnp.int32).reshape(1)
    taps = weights.reshape(9, 3, 128, 256)
    shape = jax.ShapeDtypeStruct
    mb = 1 << 20

    send = call(
        pack_body,
        shape((8, 7, 16, 256), BF16),
        [ANY] * 2,
        (2 * mb, mb),
        [
            pltpu.VMEM(volume.shape, BF16),
            pltpu.VMEM(out_error.shape, BF16),
            pltpu.SemaphoreType.DMA((2,)),
        ],
        62500000,
    )(volume, out_error)
    received = exchange(send, "filt")
    even, odd = call(
        turn_body, (shape((256, 1152), BF16), shape((512, 1152), BF16)), [VMEM], (452 * mb, 4 * mb)
    )(taps)
    rim = shifted_2(received[:, 3:6], "slab", 1)
    stack = shape((1152, 128), BF16)
    grad, both, ze, zo, part = call(
        conv_body,
        (shape((256, 128), BF16), shape((256, 256), BF16), stack, stack, shape((128, 3456), BF16)),
        [SMEM, VMEM, VMEM, VMEM, VMEM],
        (453 * mb, 4 * mb),
    )(core, received, rim, even, odd)

    other = lax.ppermute(part, "slab", CORE_PAIRS)
    right = shifted_2(grad, "filt", -1)
    part = call(
        keep_body,
        shape((128, 3456), BF16),
        [SMEM, VMEM, VMEM, VMEM, VMEM],
        (113 * mb, 3 * mb),
        [pltpu.VMEM((128, 3456), BF16), pltpu.SemaphoreType.DMA((3,))],
        LIMIT,
        ANY,
    )(core, both, ze, zo, other)
    upper = shifted_2(grad, "slab", -1)
    diagonal = lax.ppermute(
        grad,
        ("slab", "filt"),
        [(8 * s + y, 8 * s + y - 9) for s in range(1, 64) for y in range(1, 8)],
    )
    tiles = exchange(part.reshape(16, 8, 3456), ("slab", "filt"), WIDE)
    tiles, right, upper, diagonal = lax.optimization_barrier((tiles, right, upper, diagonal))
    tiles = add_up(tiles, 16)
    tiles = add_up(exchange(tiles, ("slab", "filt"), FAR), 16)
    in_grad = call(
        input_body, shape((2, 2, 128, 256), BF16), [VMEM] * 5, (226 * mb, 3 * mb)
    )(grad, right, upper, diagonal, taps)
    in_grad = in_grad.transpose(0, 2, 1, 3)

    tiles = exchange(tiles, "slab", NEAR)
    out = call(last_body, shape((27, 32, 128), F32), [VMEM], (mb, mb))(tiles)
    weight_grad = out.reshape(3, 3, 3, 32, 128).transpose(0, 1, 2, 4, 3)
    return (in_grad, weight_grad)


def solution(mesh):
    in_specs = (P("slab", "filt", None, None), P(), P("slab", "filt", None, None))
    out_specs = (P("slab", None, "filt", None), P(None, None, None, None, "filt"))
    return jax.shard_map(
        on_device, mesh=mesh, in_specs=in_specs, out_specs=out_specs, check_vma=False
    )
```

```python
import jax
import jax.numpy as jnp
from jax import lax
from jax.experimental import pallas as pl
from jax.experimental.pallas import tpu as pltpu
from jax.sharding import PartitionSpec as P

F32 = jnp.float32
BF16 = jnp.bfloat16
VMEM = pl.BlockSpec(memory_space=pltpu.VMEM)
ANY = pl.BlockSpec(memory_space=pl.ANY)
SMEM = pl.BlockSpec(memory_space=pltpu.SMEM)
LIMIT = 48 * 1024 * 1024

def slab_of(x, z, core):
    return (x * 8 + z) * 2 + core


X4, Q4, B2 = range(4), range(4), range(2)


def member_of(x, zh, zl, c, yh, yl):
    return slab_of(x, 2 * zh + zl, c) * 8 + 2 * yh + yl


WIDE = [
    [member_of(x, zh, zl, c, yh, yl) for x in X4 for zl in B2 for yl in B2]
    for zh in Q4
    for c in B2
    for yh in Q4
]
FAR = [
    [member_of(x, zh, zl, c, yh, yl) for zh in Q4 for yh in Q4]
    for x in X4
    for zl in B2
    for c in B2
    for yl in B2
]
NEAR = [[slab_of(x, 2 * zh + zl, c) for x in X4 for zl in B2 for c in B2] for zh in Q4]
CORE_PAIRS = [(s, s ^ 1) for s in range(64)]


def call(body, out_shape, in_specs, cost, scratch=(), limit=LIMIT, out_spec=VMEM):
    many = isinstance(out_shape, (tuple, list))
    return pl.pallas_call(
        body,
        out_shape=out_shape,
        in_specs=in_specs,
        out_specs=[out_spec] * len(out_shape) if many else out_spec,
        scratch_shapes=list(scratch),
        compiler_params=pltpu.CompilerParams(vmem_limit_bytes=limit),
        cost_estimate=pl.CostEstimate(flops=cost[0], bytes_accessed=cost[1], transcendentals=0),
    )


def mm(left, right):
    return jnp.dot(left, right, preferred_element_type=F32)


def mm_nt(left, right):
    return lax.dot_general(left, right, (((1,), (1,)), ((), ())), preferred_element_type=F32)


def ones_where(cond):
    return jnp.where(cond, 1.0, 0.0).astype(BF16)


def iotas(rows, cols):
    return (
        lax.broadcasted_iota(jnp.int32, (rows, cols), 0),
        lax.broadcasted_iota(jnp.int32, (rows, cols), 1),
    )


def pack_body(vol_hbm, err_hbm, send_ref, vol_ref, err_ref, sems):
    copies = [
        pltpu.make_async_copy(vol_hbm, vol_ref, sems.at[0]),
        pltpu.make_async_copy(err_hbm, err_ref, sems.at[1]),
    ]
    for copy in copies:
        copy.start()
    i, j = iotas(256, 256)
    row_first = ones_where(j == ((i & 15) << 4) + (i >> 4))
    even_odd = ones_where(i == ((j & 127) << 1) + (j >> 7))
    error_rows = ones_where(j == ((i & 31) << 3) + (i >> 5))
    copies[0].wait()
    for p in range(2):
        plane = vol_ref[p].reshape(256, 256)
        plane = mm(row_first, plane).astype(BF16)
        plane = mm(plane, even_odd).astype(BF16)
        for y in range(8):
            for b in range(3):
                row = 2 * y - 1 + b
                if row < 0:
                    piece = jnp.zeros((16, 256), BF16)
                else:
                    piece = plane[row * 16 : row * 16 + 16]
                send_ref[y, p * 3 + b] = piece
    copies[1].wait()
    error = mm(error_rows, err_ref[0].reshape(256, 128)).astype(BF16)
    for y in range(8):
        for u in range(2):
            start = y * 32 + u * 16
            send_ref[y, 6, :, u * 128 : u * 128 + 128] = error[start : start + 16]


def turn_body(w_ref, even_ref, odd_ref):
    i, j = iotas(256, 256)
    same = ones_where(i == j)
    for ab in range(9):
        cols = slice(ab * 128, ab * 128 + 128)
        even_ref[:, cols] = mm_nt(same, w_ref[ab, 1]).astype(BF16)
        odd_ref[:256, cols] = mm_nt(same, w_ref[ab, 2]).astype(BF16)
        odd_ref[256:, cols] = mm_nt(same, w_ref[ab, 0]).astype(BF16)


def core_rows(core):
    i, j = iotas(128, 256)
    tile = (((i >> 1) & 3) << 6) + (((i >> 3) & 1) << 5)
    return ones_where(j == tile + ((i >> 4) << 2) + (i & 1) + core * 2)


def taps_of(order, both, ze, zo):
    now = mm(order, both[:, :128]).astype(BF16)
    after = mm(order, both[:, 128:]).astype(BF16)
    return mm_nt(after, zo[...]), mm_nt(now, ze[...]), mm_nt(now, zo[...])


def conv_body(core_ref, rec_ref, rim_ref, even_ref, odd_ref, grad_ref, both_ref, ze, zo, part_ref):
    for a in range(3):
        for b in range(3):
            rows = slice((a * 3 + b) * 128, (a * 3 + b) * 128 + 128)
            tile = rim_ref[:, b] if a == 0 else rec_ref[:, (a - 1) * 3 + b]
            tile = tile.reshape(128, 256)
            ze[rows] = tile[:, :128]
            zo[rows] = tile[:, 128:]
    center = mm(even_ref[...], ze[...])
    sides = mm(odd_ref[...], zo[...])
    errors = []
    for y in range(8):
        errors += [rec_ref[y, 6][:, :128], rec_ref[y, 6][:, 128:]]
    error = jnp.concatenate(errors, 0).astype(F32)
    lane = lax.broadcasted_iota(jnp.int32, (256, 128), 1)
    before = jnp.where(lane == 0, 0.0, pltpu.roll(sides[256:], 1, 1))
    preact = center + sides[:256] + before
    sigma = jax.nn.sigmoid(preact)
    grad = (error * (sigma * (1.0 + preact * (1.0 - sigma)))).astype(BF16)
    grad_ref[...] = grad
    after = jnp.where(lane == 127, 0.0, pltpu.roll(grad.astype(F32), 127, 1)).astype(BF16)
    both = jnp.concatenate([grad, after], 1)
    both_ref[...] = both
    parts = taps_of(core_rows(1 - core_ref[0]), both, ze, zo)
    for c in range(3):
        part_ref[:, c * 1152 : c * 1152 + 1152] = parts[c].astype(BF16)


def keep_body(core_ref, both_ref, ze, zo, other_ref, part_hbm, part_ref, sems):
    order = core_rows(core_ref[0])
    both = both_ref[...]
    now = mm(order, both[:, :128]).astype(BF16)
    after = mm(order, both[:, 128:]).astype(BF16)
    copies = []
    for c, (grad, stack) in enumerate(((after, zo), (now, ze), (now, zo))):
        cols = pl.ds(c * 1152, 1152)
        total = mm_nt(grad, stack[...]) + other_ref[:, cols].astype(F32)
        part_ref[:, cols] = total.astype(BF16)
        copies.append(pltpu.make_async_copy(part_ref.at[:, cols], part_hbm.at[:, cols], sems.at[c]))
        copies[-1].start()
    for copy in copies:
        copy.wait()


def sum_body(in_ref, out_ref):
    total = in_ref[0].astype(F32)
    for n in range(1, in_ref.shape[0]):
        total = total + in_ref[n].astype(F32)
    for n in range(out_ref.shape[0]):
        start = 2 * n % total.shape[0]
        out_ref[n] = total[start : start + 2].astype(BF16)


def last_body(in_ref, out_ref):
    for m in range(16):
        rows = in_ref[m].astype(F32) * (1.0 / 256.0)
        for c in range(3):
            for ab in range(9):
                start = (c * 9 + ab) * 128
                out_ref[ab * 3 + c, 2 * m : 2 * m + 2] = rows[:, start : start + 128]


def input_body(own_ref, right_ref, up_ref, diag_ref, w_ref, out_ref):
    lane = lax.broadcasted_iota(jnp.int32, (128, 128), 1)
    i, j = iotas(256, 256)
    weave = ones_where(j == ((i & 127) << 1) + (i >> 7))
    taps = (((1, 0),), ((2, 0), (0, 1)))
    grads = ((own_ref[...], right_ref[...]), (up_ref[...], diag_ref[...]))
    for ed in range(2):
        for er in range(2):
            sums = []
            for c in range(3):
                total = None
                for a, od in taps[ed]:
                    for b, pd in taps[er]:
                        term = mm(w_ref[a * 3 + b, c], grads[od][pd])
                        total = term if total is None else total + term
                sums.append(total)
            nxt = jnp.where(lane == 127, 0.0, pltpu.roll(sums[0], 127, 1))
            both = jnp.concatenate([sums[1].astype(BF16), (sums[2] + nxt).astype(BF16)], 1)
            out_ref[ed, er] = mm(both, weave).astype(BF16)


def shifted_2(value, axis, steps):
    count = lax.axis_size(axis)
    first, last = (max(0, -steps), min(count, count - steps))
    return lax.ppermute(value, axis, [(source, source + steps) for source in range(first, last)])


def exchange(value, axis, groups=None):
    return lax.all_to_all(
        value, axis, split_axis=0, concat_axis=0, axis_index_groups=groups, tiled=True
    )


def add_up(value, count):
    size = value.size * 2
    out_shape = jax.ShapeDtypeStruct((count, 2, 3456), BF16)
    return call(sum_body, out_shape, [VMEM], (size, size))(value)


def on_device(volume, weights, out_error):
    core = (lax.axis_index("slab") & 1).astype(jnp.int32).reshape(1)
    taps = weights.reshape(9, 3, 128, 256)
    shape = jax.ShapeDtypeStruct
    mb = 1 << 20

    send = call(
        pack_body,
        shape((8, 7, 16, 256), BF16),
        [ANY] * 2,
        (2 * mb, mb),
        [
            pltpu.VMEM(volume.shape, BF16),
            pltpu.VMEM(out_error.shape, BF16),
            pltpu.SemaphoreType.DMA((2,)),
        ],
        62500000,
    )(volume, out_error)
    received = exchange(send, "filt")
    even, odd = call(
        turn_body, (shape((256, 1152), BF16), shape((512, 1152), BF16)), [VMEM], (452 * mb, 4 * mb)
    )(taps)
    rim = shifted_2(received[:, 3:6], "slab", 1)
    stack = shape((1152, 128), BF16)
    grad, both, ze, zo, part = call(
        conv_body,
        (shape((256, 128), BF16), shape((256, 256), BF16), stack, stack, shape((128, 3456), BF16)),
        [SMEM, VMEM, VMEM, VMEM, VMEM],
        (453 * mb, 4 * mb),
    )(core, received, rim, even, odd)

    other = lax.ppermute(part, "slab", CORE_PAIRS)
    part = call(
        keep_body,
        shape((128, 3456), BF16),
        [SMEM, VMEM, VMEM, VMEM, VMEM],
        (113 * mb, 3 * mb),
        [pltpu.VMEM((128, 3456), BF16), pltpu.SemaphoreType.DMA((3,))],
        LIMIT,
        ANY,
    )(core, both, ze, zo, other)
    tiles = exchange(part.reshape(16, 8, 3456), ("slab", "filt"), WIDE)
    tiles, late = lax.optimization_barrier((tiles, grad))
    right = shifted_2(late, "filt", -1)
    upper = shifted_2(late, "slab", -1)
    diagonal = lax.ppermute(
        late,
        ("slab", "filt"),
        [(8 * s + y, 8 * s + y - 9) for s in range(1, 64) for y in range(1, 8)],
    )
    tiles = exchange(add_up(tiles, 16), ("slab", "filt"), FAR)
    tiles, right, upper, diagonal = lax.optimization_barrier((tiles, right, upper, diagonal))
    tiles = add_up(tiles, 16)

    in_grad = call(
        input_body, shape((2, 2, 128, 256), BF16), [VMEM] * 5, (226 * mb, 3 * mb)
    )(grad, right, upper, diagonal, taps)
    in_grad = in_grad.transpose(0, 2, 1, 3)

    tiles = exchange(tiles, "slab", NEAR)
    out = call(last_body, shape((27, 32, 128), F32), [VMEM], (mb, mb))(tiles)
    weight_grad = out.reshape(3, 3, 3, 32, 128).transpose(0, 1, 2, 4, 3)
    return (in_grad, weight_grad)


def solution(mesh):
    in_specs = (P("slab", "filt", None, None), P(), P("slab", "filt", None, None))
    out_specs = (P("slab", None, "filt", None), P(None, None, None, None, "filt"))
    return jax.shard_map(
        on_device, mesh=mesh, in_specs=in_specs, out_specs=out_specs, check_vma=False
    )
```

```python
import jax
import jax.numpy as jnp
from jax import lax
from jax.experimental import pallas as pl
from jax.experimental.pallas import tpu as pltpu
from jax.sharding import PartitionSpec as P

F32 = jnp.float32
BF16 = jnp.bfloat16
VMEM = pl.BlockSpec(memory_space=pltpu.VMEM)
ANY = pl.BlockSpec(memory_space=pl.ANY)
SMEM = pl.BlockSpec(memory_space=pltpu.SMEM)
LIMIT = 48 * 1024 * 1024

def slab_of(x, z, core):
    return (x * 8 + z) * 2 + core


X4, Q4, B2 = range(4), range(4), range(2)


def member_of(x, zh, zl, c, yh, yl):
    return slab_of(x, 2 * zh + zl, c) * 8 + 2 * yh + yl


WIDE = [
    [member_of(x, zh, zl, c, yh, yl) for x in X4 for zl in B2 for yl in B2]
    for zh in Q4
    for c in B2
    for yh in Q4
]
FAR = [
    [member_of(x, zh, zl, c, yh, yl) for zh in Q4 for yh in Q4]
    for x in X4
    for zl in B2
    for c in B2
    for yl in B2
]
NEAR = [[slab_of(x, 2 * zh + zl, c) for x in X4 for zl in B2 for c in B2] for zh in Q4]
CORE_PAIRS = [(s, s ^ 1) for s in range(64)]


def call(body, out_shape, in_specs, cost, scratch=(), limit=LIMIT, out_spec=VMEM):
    many = isinstance(out_shape, (tuple, list))
    return pl.pallas_call(
        body,
        out_shape=out_shape,
        in_specs=in_specs,
        out_specs=[out_spec] * len(out_shape) if many else out_spec,
        scratch_shapes=list(scratch),
        compiler_params=pltpu.CompilerParams(vmem_limit_bytes=limit),
        cost_estimate=pl.CostEstimate(flops=cost[0], bytes_accessed=cost[1], transcendentals=0),
    )


def mm(left, right):
    return jnp.dot(left, right, preferred_element_type=F32)


def mm_nt(left, right):
    return lax.dot_general(left, right, (((1,), (1,)), ((), ())), preferred_element_type=F32)


def ones_where(cond):
    return jnp.where(cond, 1.0, 0.0).astype(BF16)


def iotas(rows, cols):
    return (
        lax.broadcasted_iota(jnp.int32, (rows, cols), 0),
        lax.broadcasted_iota(jnp.int32, (rows, cols), 1),
    )


def pack_body(vol_hbm, err_hbm, send_ref, vol_ref, err_ref, sems):
    copies = [
        pltpu.make_async_copy(vol_hbm, vol_ref, sems.at[0]),
        pltpu.make_async_copy(err_hbm, err_ref, sems.at[1]),
    ]
    for copy in copies:
        copy.start()
    i, j = iotas(256, 256)
    row_first = ones_where(j == ((i & 15) << 4) + (i >> 4))
    even_odd = ones_where(i == ((j & 127) << 1) + (j >> 7))
    error_rows = ones_where(j == ((i & 31) << 3) + (i >> 5))
    copies[0].wait()
    for p in range(2):
        plane = vol_ref[p].reshape(256, 256)
        plane = mm(row_first, plane).astype(BF16)
        plane = mm(plane, even_odd).astype(BF16)
        for y in range(8):
            for b in range(3):
                row = 2 * y - 1 + b
                if row < 0:
                    piece = jnp.zeros((16, 256), BF16)
                else:
                    piece = plane[row * 16 : row * 16 + 16]
                send_ref[y, p * 3 + b] = piece
    copies[1].wait()
    error = mm(error_rows, err_ref[0].reshape(256, 128)).astype(BF16)
    for y in range(8):
        for u in range(2):
            start = y * 32 + u * 16
            send_ref[y, 6, :, u * 128 : u * 128 + 128] = error[start : start + 16]


def turn_body(w_ref, even_ref, odd_ref):
    i, j = iotas(256, 256)
    same = ones_where(i == j)
    for ab in range(9):
        cols = slice(ab * 128, ab * 128 + 128)
        even_ref[:, cols] = mm_nt(same, w_ref[ab, 1]).astype(BF16)
        odd_ref[:256, cols] = mm_nt(same, w_ref[ab, 2]).astype(BF16)
        odd_ref[256:, cols] = mm_nt(same, w_ref[ab, 0]).astype(BF16)


def core_rows(core):
    i, j = iotas(128, 256)
    tile = (((i >> 1) & 3) << 6) + (((i >> 3) & 1) << 5)
    return ones_where(j == tile + ((i >> 4) << 2) + (i & 1) + core * 2)


def taps_of(order, both, ze, zo):
    now = mm(order, both[:, :128]).astype(BF16)
    after = mm(order, both[:, 128:]).astype(BF16)
    return mm_nt(after, zo[...]), mm_nt(now, ze[...]), mm_nt(now, zo[...])


def conv_body(core_ref, rec_ref, rim_ref, even_ref, odd_ref, grad_ref, both_ref, ze, zo, part_ref):
    for a in range(3):
        for b in range(3):
            rows = slice((a * 3 + b) * 128, (a * 3 + b) * 128 + 128)
            tile = rim_ref[:, b] if a == 0 else rec_ref[:, (a - 1) * 3 + b]
            tile = tile.reshape(128, 256)
            ze[rows] = tile[:, :128]
            zo[rows] = tile[:, 128:]
    center = mm(even_ref[...], ze[...])
    sides = mm(odd_ref[...], zo[...])
    errors = []
    for y in range(8):
        errors += [rec_ref[y, 6][:, :128], rec_ref[y, 6][:, 128:]]
    error = jnp.concatenate(errors, 0).astype(F32)
    lane = lax.broadcasted_iota(jnp.int32, (256, 128), 1)
    before = jnp.where(lane == 0, 0.0, pltpu.roll(sides[256:], 1, 1))
    preact = center + sides[:256] + before
    sigma = jax.nn.sigmoid(preact)
    grad = (error * (sigma * (1.0 + preact * (1.0 - sigma)))).astype(BF16)
    grad_ref[...] = grad
    after = jnp.where(lane == 127, 0.0, pltpu.roll(grad.astype(F32), 127, 1)).astype(BF16)
    both = jnp.concatenate([grad, after], 1)
    both_ref[...] = both
    parts = taps_of(core_rows(1 - core_ref[0]), both, ze, zo)
    for c in range(3):
        part_ref[:, c * 1152 : c * 1152 + 1152] = parts[c].astype(BF16)


def keep_body(core_ref, both_ref, ze, zo, other_ref, part_hbm, part_ref, sems):
    order = core_rows(core_ref[0])
    both = both_ref[...]
    now = mm(order, both[:, :128]).astype(BF16)
    after = mm(order, both[:, 128:]).astype(BF16)
    copies = []
    for c, (grad, stack) in enumerate(((after, zo), (now, ze), (now, zo))):
        cols = pl.ds(c * 1152, 1152)
        total = mm_nt(grad, stack[...]) + other_ref[:, cols].astype(F32)
        part_ref[:, cols] = total.astype(BF16)
        copies.append(pltpu.make_async_copy(part_ref.at[:, cols], part_hbm.at[:, cols], sems.at[c]))
        copies[-1].start()
    for copy in copies:
        copy.wait()


def sum_body(in_ref, out_ref):
    total = in_ref[0].astype(F32)
    for n in range(1, in_ref.shape[0]):
        total = total + in_ref[n].astype(F32)
    for n in range(out_ref.shape[0]):
        start = 2 * n % total.shape[0]
        out_ref[n] = total[start : start + 2].astype(BF16)


def last_body(in_ref, out_ref):
    for m in range(16):
        rows = in_ref[m].astype(F32) * (1.0 / 256.0)
        for c in range(3):
            for ab in range(9):
                start = (c * 9 + ab) * 128
                out_ref[ab * 3 + c, 2 * m : 2 * m + 2] = rows[:, start : start + 128]


def input_body(own_ref, up_ref, w_ref, out_ref):
    lane = lax.broadcasted_iota(jnp.int32, (128, 128), 1)
    i, j = iotas(256, 256)
    weave = ones_where(j == ((i & 127) << 1) + (i >> 7))
    taps = (((1, 0),), ((2, 0), (0, 1)))
    grads = ((own_ref[0], own_ref[1]), (up_ref[0], up_ref[1]))
    for ed in range(2):
        for er in range(2):
            sums = []
            for c in range(3):
                total = None
                for a, od in taps[ed]:
                    for b, pd in taps[er]:
                        term = mm(w_ref[a * 3 + b, c], grads[od][pd])
                        total = term if total is None else total + term
                sums.append(total)
            nxt = jnp.where(lane == 127, 0.0, pltpu.roll(sums[0], 127, 1))
            both = jnp.concatenate([sums[1].astype(BF16), (sums[2] + nxt).astype(BF16)], 1)
            out_ref[ed, er] = mm(both, weave).astype(BF16)


def shifted_2(value, axis, steps):
    count = lax.axis_size(axis)
    first, last = (max(0, -steps), min(count, count - steps))
    return lax.ppermute(value, axis, [(source, source + steps) for source in range(first, last)])


def exchange(value, axis, groups=None):
    return lax.all_to_all(
        value, axis, split_axis=0, concat_axis=0, axis_index_groups=groups, tiled=True
    )


def add_up(value, count):
    size = value.size * 2
    out_shape = jax.ShapeDtypeStruct((count, 2, 3456), BF16)
    return call(sum_body, out_shape, [VMEM], (size, size))(value)


def on_device(volume, weights, out_error):
    core = (lax.axis_index("slab") & 1).astype(jnp.int32).reshape(1)
    taps = weights.reshape(9, 3, 128, 256)
    shape = jax.ShapeDtypeStruct
    mb = 1 << 20

    send = call(
        pack_body,
        shape((8, 7, 16, 256), BF16),
        [ANY] * 2,
        (2 * mb, mb),
        [
            pltpu.VMEM(volume.shape, BF16),
            pltpu.VMEM(out_error.shape, BF16),
            pltpu.SemaphoreType.DMA((2,)),
        ],
        62500000,
    )(volume, out_error)
    received = exchange(send, "filt")
    even, odd = call(
        turn_body, (shape((256, 1152), BF16), shape((512, 1152), BF16)), [VMEM], (452 * mb, 4 * mb)
    )(taps)
    rim = shifted_2(received[:, 3:6], "slab", 1)
    stack = shape((1152, 128), BF16)
    grad, both, ze, zo, part = call(
        conv_body,
        (shape((256, 128), BF16), shape((256, 256), BF16), stack, stack, shape((128, 3456), BF16)),
        [SMEM, VMEM, VMEM, VMEM, VMEM],
        (453 * mb, 4 * mb),
    )(core, received, rim, even, odd)

    other = lax.ppermute(part, "slab", CORE_PAIRS)
    right = shifted_2(grad, "filt", -1)
    part = call(
        keep_body,
        shape((128, 3456), BF16),
        [SMEM, VMEM, VMEM, VMEM, VMEM],
        (113 * mb, 3 * mb),
        [pltpu.VMEM((128, 3456), BF16), pltpu.SemaphoreType.DMA((3,))],
        LIMIT,
        ANY,
    )(core, both, ze, zo, other)
    tiles = exchange(part.reshape(16, 8, 3456), ("slab", "filt"), WIDE)
    tiles, right = lax.optimization_barrier((tiles, right))
    own = jnp.stack([grad, right])
    upper = shifted_2(own, "slab", -1)
    tiles = exchange(add_up(tiles, 16), ("slab", "filt"), FAR)
    tiles, upper = lax.optimization_barrier((tiles, upper))
    tiles = add_up(tiles, 16)

    in_grad = call(
        input_body, shape((2, 2, 128, 256), BF16), [VMEM] * 3, (226 * mb, 3 * mb)
    )(own, upper, taps)
    in_grad = in_grad.transpose(0, 2, 1, 3)

    tiles = exchange(tiles, "slab", NEAR)
    out = call(last_body, shape((27, 32, 128), F32), [VMEM], (mb, mb))(tiles)
    weight_grad = out.reshape(3, 3, 3, 32, 128).transpose(0, 1, 2, 4, 3)
    return (in_grad, weight_grad)


def solution(mesh):
    in_specs = (P("slab", "filt", None, None), P(), P("slab", "filt", None, None))
    out_specs = (P("slab", None, "filt", None), P(None, None, None, None, "filt"))
    return jax.shard_map(
        on_device, mesh=mesh, in_specs=in_specs, out_specs=out_specs, check_vma=False
    )
```

```python
import jax
import jax.numpy as jnp
from jax import lax
from jax.experimental import pallas as pl
from jax.experimental.pallas import tpu as pltpu
from jax.sharding import PartitionSpec as P

F32 = jnp.float32
BF16 = jnp.bfloat16
VMEM = pl.BlockSpec(memory_space=pltpu.VMEM)
ANY = pl.BlockSpec(memory_space=pl.ANY)
SMEM = pl.BlockSpec(memory_space=pltpu.SMEM)
LIMIT = 48 * 1024 * 1024

def slab_of(x, z, core):
    return (x * 8 + z) * 2 + core


X4, Q4, B2 = range(4), range(4), range(2)


def member_of(x, zh, zl, c, yh, yl):
    return slab_of(x, 2 * zh + zl, c) * 8 + 2 * yh + yl


WIDE = [
    [member_of(x, zh, zl, c, yh, yl) for x in X4 for zl in B2 for yl in B2]
    for zh in Q4
    for c in B2
    for yh in Q4
]
FAR = [
    [member_of(x, zh, zl, c, yh, yl) for zh in Q4 for yh in Q4]
    for x in X4
    for zl in B2
    for c in B2
    for yl in B2
]
NEAR = [[slab_of(x, 2 * zh + zl, c) for x in X4 for zl in B2 for c in B2] for zh in Q4]
CORE_PAIRS = [(s, s ^ 1) for s in range(64)]


def call(body, out_shape, in_specs, cost, scratch=(), limit=LIMIT):
    many = isinstance(out_shape, (tuple, list))
    return pl.pallas_call(
        body,
        out_shape=out_shape,
        in_specs=in_specs,
        out_specs=[VMEM] * len(out_shape) if many else VMEM,
        scratch_shapes=list(scratch),
        compiler_params=pltpu.CompilerParams(vmem_limit_bytes=limit),
        cost_estimate=pl.CostEstimate(flops=cost[0], bytes_accessed=cost[1], transcendentals=0),
    )


def mm(left, right):
    return jnp.dot(left, right, preferred_element_type=F32)


def mm_nt(left, right):
    return lax.dot_general(left, right, (((1,), (1,)), ((), ())), preferred_element_type=F32)


def ones_where(cond):
    return jnp.where(cond, 1.0, 0.0).astype(BF16)


def iotas(rows, cols):
    return (
        lax.broadcasted_iota(jnp.int32, (rows, cols), 0),
        lax.broadcasted_iota(jnp.int32, (rows, cols), 1),
    )


def pack_body(vol_hbm, err_hbm, send_ref, vol_ref, err_ref, sems):
    copies = [
        pltpu.make_async_copy(vol_hbm, vol_ref, sems.at[0]),
        pltpu.make_async_copy(err_hbm, err_ref, sems.at[1]),
    ]
    for copy in copies:
        copy.start()
    i, j = iotas(256, 256)
    row_first = ones_where(j == ((i & 15) << 4) + (i >> 4))
    even_odd = ones_where(i == ((j & 127) << 1) + (j >> 7))
    error_rows = ones_where(j == ((i & 31) << 3) + (i >> 5))
    copies[0].wait()
    for p in range(2):
        plane = vol_ref[p].reshape(256, 256)
        plane = mm(row_first, plane).astype(BF16)
        plane = mm(plane, even_odd).astype(BF16)
        for y in range(8):
            for b in range(3):
                row = 2 * y - 1 + b
                if row < 0:
                    piece = jnp.zeros((16, 256), BF16)
                else:
                    piece = plane[row * 16 : row * 16 + 16]
                send_ref[y, p * 3 + b] = piece
    copies[1].wait()
    error = mm(error_rows, err_ref[0].reshape(256, 128)).astype(BF16)
    for y in range(8):
        for u in range(2):
            start = y * 32 + u * 16
            send_ref[y, 6, :, u * 128 : u * 128 + 128] = error[start : start + 16]


def turn_body(w_ref, even_ref, odd_ref):
    i, j = iotas(256, 256)
    same = ones_where(i == j)
    for ab in range(9):
        cols = slice(ab * 128, ab * 128 + 128)
        even_ref[:, cols] = mm_nt(same, w_ref[ab, 1]).astype(BF16)
        odd_ref[:256, cols] = mm_nt(same, w_ref[ab, 2]).astype(BF16)
        odd_ref[256:, cols] = mm_nt(same, w_ref[ab, 0]).astype(BF16)


def core_rows(core):
    i, j = iotas(128, 256)
    tile = (((i >> 1) & 3) << 6) + (((i >> 3) & 1) << 5)
    return ones_where(j == tile + ((i >> 4) << 2) + (i & 1) + core * 2)


def taps_of(order, both, ze, zo):
    now = mm(order, both[:, :128]).astype(BF16)
    after = mm(order, both[:, 128:]).astype(BF16)
    return mm_nt(after, zo[...]), mm_nt(now, ze[...]), mm_nt(now, zo[...])


def conv_body(core_ref, rec_ref, rim_ref, even_ref, odd_ref, grad_ref, both_ref, ze, zo, part_ref):
    for a in range(3):
        for b in range(3):
            rows = slice((a * 3 + b) * 128, (a * 3 + b) * 128 + 128)
            tile = rim_ref[:, b] if a == 0 else rec_ref[:, (a - 1) * 3 + b]
            tile = tile.reshape(128, 256)
            ze[rows] = tile[:, :128]
            zo[rows] = tile[:, 128:]
    center = mm(even_ref[...], ze[...])
    sides = mm(odd_ref[...], zo[...])
    errors = []
    for y in range(8):
        errors += [rec_ref[y, 6][:, :128], rec_ref[y, 6][:, 128:]]
    error = jnp.concatenate(errors, 0).astype(F32)
    lane = lax.broadcasted_iota(jnp.int32, (256, 128), 1)
    before = jnp.where(lane == 0, 0.0, pltpu.roll(sides[256:], 1, 1))
    preact = center + sides[:256] + before
    sigma = jax.nn.sigmoid(preact)
    grad = (error * (sigma * (1.0 + preact * (1.0 - sigma)))).astype(BF16)
    grad_ref[...] = grad
    after = jnp.where(lane == 127, 0.0, pltpu.roll(grad.astype(F32), 127, 1)).astype(BF16)
    both = jnp.concatenate([grad, after], 1)
    both_ref[...] = both
    parts = taps_of(core_rows(1 - core_ref[0]), both, ze, zo)
    for c in range(3):
        part_ref[:, c * 1152 : c * 1152 + 1152] = parts[c].astype(BF16)


def keep_body(core_ref, both_ref, ze, zo, other_ref, part_ref):
    parts = taps_of(core_rows(core_ref[0]), both_ref[...], ze, zo)
    for c in range(3):
        cols = slice(c * 1152, c * 1152 + 1152)
        part_ref[:, cols] = (parts[c] + other_ref[:, cols].astype(F32)).astype(BF16)


def sum_body(in_ref, out_ref):
    total = in_ref[0].astype(F32)
    for n in range(1, in_ref.shape[0]):
        total = total + in_ref[n].astype(F32)
    for n in range(out_ref.shape[0]):
        start = 2 * n % total.shape[0]
        out_ref[n] = total[start : start + 2].astype(BF16)


def last_body(in_ref, out_ref):
    for m in range(16):
        rows = in_ref[m].astype(F32) * (1.0 / 256.0)
        for c in range(3):
            for ab in range(9):
                start = (c * 9 + ab) * 128
                out_ref[ab * 3 + c, 2 * m : 2 * m + 2] = rows[:, start : start + 128]


def input_body(own_ref, right_ref, up_ref, diag_ref, w_ref, out_ref):
    lane = lax.broadcasted_iota(jnp.int32, (128, 128), 1)
    i, j = iotas(256, 256)
    weave = ones_where(j == ((i & 127) << 1) + (i >> 7))
    taps = (((1, 0),), ((2, 0), (0, 1)))
    grads = ((own_ref[...], right_ref[...]), (up_ref[...], diag_ref[...]))
    for ed in range(2):
        for er in range(2):
            sums = []
            for c in range(3):
                total = None
                for a, od in taps[ed]:
                    for b, pd in taps[er]:
                        term = mm(w_ref[a * 3 + b, c], grads[od][pd])
                        total = term if total is None else total + term
                sums.append(total)
            nxt = jnp.where(lane == 127, 0.0, pltpu.roll(sums[0], 127, 1))
            both = jnp.concatenate([sums[1].astype(BF16), (sums[2] + nxt).astype(BF16)], 1)
            out_ref[ed, er] = mm(both, weave).astype(BF16)


def shifted_2(value, axis, steps):
    count = lax.axis_size(axis)
    first, last = (max(0, -steps), min(count, count - steps))
    return lax.ppermute(value, axis, [(source, source + steps) for source in range(first, last)])


def exchange(value, axis, groups=None):
    return lax.all_to_all(
        value, axis, split_axis=0, concat_axis=0, axis_index_groups=groups, tiled=True
    )


def add_up(value, count):
    size = value.size * 2
    out_shape = jax.ShapeDtypeStruct((count, 2, 3456), BF16)
    return call(sum_body, out_shape, [VMEM], (size, size))(value)


def on_device(volume, weights, out_error):
    core = (lax.axis_index("slab") & 1).astype(jnp.int32).reshape(1)
    taps = weights.reshape(9, 3, 128, 256)
    shape = jax.ShapeDtypeStruct
    mb = 1 << 20

    send = call(
        pack_body,
        shape((8, 7, 16, 256), BF16),
        [ANY] * 2,
        (2 * mb, mb),
        [
            pltpu.VMEM(volume.shape, BF16),
            pltpu.VMEM(out_error.shape, BF16),
            pltpu.SemaphoreType.DMA((2,)),
        ],
        62500000,
    )(volume, out_error)
    received = exchange(send, "filt")
    even, odd = call(
        turn_body, (shape((256, 1152), BF16), shape((512, 1152), BF16)), [VMEM], (452 * mb, 4 * mb)
    )(taps)
    rim = shifted_2(received[:, 3:6], "slab", 1)
    stack = shape((1152, 128), BF16)
    grad, both, ze, zo, part = call(
        conv_body,
        (shape((256, 128), BF16), shape((256, 256), BF16), stack, stack, shape((128, 3456), BF16)),
        [SMEM, VMEM, VMEM, VMEM, VMEM],
        (453 * mb, 4 * mb),
    )(core, received, rim, even, odd)

    other = lax.ppermute(part, "slab", CORE_PAIRS)
    part = call(
        keep_body, shape((128, 3456), BF16), [SMEM, VMEM, VMEM, VMEM, VMEM], (113 * mb, 3 * mb)
    )(core, both, ze, zo, other)
    tiles = exchange(part.reshape(16, 8, 3456), ("slab", "filt"), WIDE)
    tiles, late = lax.optimization_barrier((tiles, grad))
    right = shifted_2(late, "filt", -1)
    upper = shifted_2(late, "slab", -1)
    diagonal = lax.ppermute(
        late,
        ("slab", "filt"),
        [(8 * s + y, 8 * s + y - 9) for s in range(1, 64) for y in range(1, 8)],
    )
    tiles = exchange(add_up(tiles, 16), ("slab", "filt"), FAR)
    tiles, right, upper, diagonal = lax.optimization_barrier((tiles, right, upper, diagonal))
    tiles = add_up(tiles, 16)

    in_grad = call(
        input_body, shape((2, 2, 128, 256), BF16), [VMEM] * 5, (226 * mb, 3 * mb)
    )(grad, right, upper, diagonal, taps)
    in_grad = in_grad.transpose(0, 2, 1, 3)

    tiles = exchange(tiles, "slab", NEAR)
    out = call(last_body, shape((27, 32, 128), F32), [VMEM], (mb, mb))(tiles)
    weight_grad = out.reshape(3, 3, 3, 32, 128).transpose(0, 1, 2, 4, 3)
    return (in_grad, weight_grad)


def solution(mesh):
    in_specs = (P("slab", "filt", None, None), P(), P("slab", "filt", None, None))
    out_specs = (P("slab", None, "filt", None), P(None, None, None, None, "filt"))
    return jax.shard_map(
        on_device, mesh=mesh, in_specs=in_specs, out_specs=out_specs, check_vma=False
    )
```

```python
import jax
import jax.numpy as jnp
from jax import lax
from jax.experimental import pallas as pl
from jax.experimental.pallas import tpu as pltpu
from jax.sharding import PartitionSpec as P

F32 = jnp.float32
BF16 = jnp.bfloat16
VMEM = pl.BlockSpec(memory_space=pltpu.VMEM)
ANY = pl.BlockSpec(memory_space=pl.ANY)
SMEM = pl.BlockSpec(memory_space=pltpu.SMEM)
LIMIT = 48 * 1024 * 1024

def slab_of(x, z, core):
    return (x * 8 + z) * 2 + core


X4, Q4, B2 = range(4), range(4), range(2)


def member_of(x, zh, zl, c, yh, yl):
    return slab_of(x, 2 * zh + zl, c) * 8 + 2 * yh + yl


WIDE = [
    [member_of(x, zh, zl, c, yh, yl) for x in X4 for zl in B2 for yl in B2]
    for zh in Q4
    for c in B2
    for yh in Q4
]
FAR = [
    [member_of(x, zh, zl, c, yh, yl) for zh in Q4 for yh in Q4]
    for x in X4
    for zl in B2
    for c in B2
    for yl in B2
]
NEAR = [[slab_of(x, 2 * zh + zl, c) for x in X4 for zl in B2 for c in B2] for zh in Q4]
CORE_PAIRS = [(s, s ^ 1) for s in range(64)]


def call(body, out_shape, in_specs, cost, scratch=(), limit=LIMIT):
    many = isinstance(out_shape, (tuple, list))
    return pl.pallas_call(
        body,
        out_shape=out_shape,
        in_specs=in_specs,
        out_specs=[VMEM] * len(out_shape) if many else VMEM,
        scratch_shapes=list(scratch),
        compiler_params=pltpu.CompilerParams(vmem_limit_bytes=limit),
        cost_estimate=pl.CostEstimate(flops=cost[0], bytes_accessed=cost[1], transcendentals=0),
    )


def mm(left, right):
    return jnp.dot(left, right, preferred_element_type=F32)


def mm_nt(left, right):
    return lax.dot_general(left, right, (((1,), (1,)), ((), ())), preferred_element_type=F32)


def ones_where(cond):
    return jnp.where(cond, 1.0, 0.0).astype(BF16)


def iotas(rows, cols):
    return (
        lax.broadcasted_iota(jnp.int32, (rows, cols), 0),
        lax.broadcasted_iota(jnp.int32, (rows, cols), 1),
    )


def pack_body(vol_hbm, err_hbm, send_ref, vol_ref, err_ref, sems):
    copies = [
        pltpu.make_async_copy(vol_hbm, vol_ref, sems.at[0]),
        pltpu.make_async_copy(err_hbm, err_ref, sems.at[1]),
    ]
    for copy in copies:
        copy.start()
    i, j = iotas(256, 256)
    row_first = ones_where(j == ((i & 15) << 4) + (i >> 4))
    even_odd = ones_where(i == ((j & 127) << 1) + (j >> 7))
    error_rows = ones_where(j == ((i & 31) << 3) + (i >> 5))
    copies[0].wait()
    for p in range(2):
        plane = vol_ref[p].reshape(256, 256)
        plane = mm(row_first, plane).astype(BF16)
        plane = mm(plane, even_odd).astype(BF16)
        for y in range(8):
            for b in range(3):
                row = 2 * y - 1 + b
                if row < 0:
                    piece = jnp.zeros((16, 256), BF16)
                else:
                    piece = plane[row * 16 : row * 16 + 16]
                send_ref[y, p * 3 + b] = piece
    copies[1].wait()
    error = mm(error_rows, err_ref[0].reshape(256, 128)).astype(BF16)
    for y in range(8):
        for u in range(2):
            start = y * 32 + u * 16
            send_ref[y, 6, :, u * 128 : u * 128 + 128] = error[start : start + 16]


def turn_body(w_ref, even_ref, odd_ref):
    i, j = iotas(256, 256)
    same = ones_where(i == j)
    for ab in range(9):
        cols = slice(ab * 128, ab * 128 + 128)
        even_ref[:, cols] = mm_nt(same, w_ref[ab, 1]).astype(BF16)
        odd_ref[:256, cols] = mm_nt(same, w_ref[ab, 2]).astype(BF16)
        odd_ref[256:, cols] = mm_nt(same, w_ref[ab, 0]).astype(BF16)


def core_rows(core):
    i, j = iotas(128, 256)
    tile = (((i >> 1) & 3) << 6) + (((i >> 3) & 1) << 5)
    return ones_where(j == tile + ((i >> 4) << 2) + (i & 1) + core * 2)


def taps_of(order, both, ze, zo):
    now = mm(order, both[:, :128]).astype(BF16)
    after = mm(order, both[:, 128:]).astype(BF16)
    return mm_nt(after, zo[...]), mm_nt(now, ze[...]), mm_nt(now, zo[...])


def conv_body(core_ref, rec_ref, rim_ref, even_ref, odd_ref, grad_ref, both_ref, ze, zo, part_ref):
    for a in range(3):
        for b in range(3):
            rows = slice((a * 3 + b) * 128, (a * 3 + b) * 128 + 128)
            tile = rim_ref[:, b] if a == 0 else rec_ref[:, (a - 1) * 3 + b]
            tile = tile.reshape(128, 256)
            ze[rows] = tile[:, :128]
            zo[rows] = tile[:, 128:]
    center = mm(even_ref[...], ze[...])
    sides = mm(odd_ref[...], zo[...])
    errors = []
    for y in range(8):
        errors += [rec_ref[y, 6][:, :128], rec_ref[y, 6][:, 128:]]
    error = jnp.concatenate(errors, 0).astype(F32)
    lane = lax.broadcasted_iota(jnp.int32, (256, 128), 1)
    before = jnp.where(lane == 0, 0.0, pltpu.roll(sides[256:], 1, 1))
    preact = center + sides[:256] + before
    sigma = jax.nn.sigmoid(preact)
    grad = (error * (sigma * (1.0 + preact * (1.0 - sigma)))).astype(BF16)
    grad_ref[...] = grad
    after = jnp.where(lane == 127, 0.0, pltpu.roll(grad.astype(F32), 127, 1)).astype(BF16)
    both = jnp.concatenate([grad, after], 1)
    both_ref[...] = both
    parts = taps_of(core_rows(1 - core_ref[0]), both, ze, zo)
    for c in range(3):
        part_ref[:, c * 1152 : c * 1152 + 1152] = parts[c].astype(BF16)


def keep_body(core_ref, both_ref, ze, zo, other_ref, part_ref):
    parts = taps_of(core_rows(core_ref[0]), both_ref[...], ze, zo)
    for c in range(3):
        cols = slice(c * 1152, c * 1152 + 1152)
        part_ref[:, cols] = (parts[c] + other_ref[:, cols].astype(F32)).astype(BF16)


def sum_body(in_ref, out_ref):
    total = in_ref[0].astype(F32)
    for n in range(1, in_ref.shape[0]):
        total = total + in_ref[n].astype(F32)
    for n in range(out_ref.shape[0]):
        start = 2 * n % total.shape[0]
        out_ref[n] = total[start : start + 2].astype(BF16)


def last_body(in_ref, out_ref):
    for m in range(16):
        rows = in_ref[m].astype(F32) * (1.0 / 256.0)
        for c in range(3):
            for ab in range(9):
                start = (c * 9 + ab) * 128
                out_ref[ab * 3 + c, 2 * m : 2 * m + 2] = rows[:, start : start + 128]


def input_body(own_ref, right_ref, up_ref, diag_ref, w_ref, out_ref):
    lane = lax.broadcasted_iota(jnp.int32, (128, 128), 1)
    i, j = iotas(256, 256)
    weave = ones_where(j == ((i & 127) << 1) + (i >> 7))
    taps = (((1, 0),), ((2, 0), (0, 1)))
    grads = ((own_ref[...], right_ref[...]), (up_ref[...], diag_ref[...]))
    for ed in range(2):
        for er in range(2):
            sums = []
            for c in range(3):
                total = None
                for a, od in taps[ed]:
                    for b, pd in taps[er]:
                        term = mm(w_ref[a * 3 + b, c], grads[od][pd])
                        total = term if total is None else total + term
                sums.append(total)
            nxt = jnp.where(lane == 127, 0.0, pltpu.roll(sums[0], 127, 1))
            both = jnp.concatenate([sums[1].astype(BF16), (sums[2] + nxt).astype(BF16)], 1)
            out_ref[ed, er] = mm(both, weave).astype(BF16)


def shifted_2(value, axis, steps):
    count = lax.axis_size(axis)
    first, last = (max(0, -steps), min(count, count - steps))
    return lax.ppermute(value, axis, [(source, source + steps) for source in range(first, last)])


def exchange(value, axis, groups=None):
    return lax.all_to_all(
        value, axis, split_axis=0, concat_axis=0, axis_index_groups=groups, tiled=True
    )


def add_up(value, count):
    size = value.size * 2
    out_shape = jax.ShapeDtypeStruct((count, 2, 3456), BF16)
    return call(sum_body, out_shape, [VMEM], (size, size))(value)


def on_device(volume, weights, out_error):
    core = (lax.axis_index("slab") & 1).astype(jnp.int32).reshape(1)
    taps = weights.reshape(9, 3, 128, 256)
    shape = jax.ShapeDtypeStruct
    mb = 1 << 20

    send = call(
        pack_body,
        shape((8, 7, 16, 256), BF16),
        [ANY] * 2,
        (2 * mb, mb),
        [
            pltpu.VMEM(volume.shape, BF16),
            pltpu.VMEM(out_error.shape, BF16),
            pltpu.SemaphoreType.DMA((2,)),
        ],
        62500000,
    )(volume, out_error)
    received = exchange(send, "filt")
    even, odd = call(
        turn_body, (shape((256, 1152), BF16), shape((512, 1152), BF16)), [VMEM], (452 * mb, 4 * mb)
    )(taps)
    rim = shifted_2(received[:, 3:6], "slab", 1)
    stack = shape((1152, 128), BF16)
    grad, both, ze, zo, part = call(
        conv_body,
        (shape((256, 128), BF16), shape((256, 256), BF16), stack, stack, shape((128, 3456), BF16)),
        [SMEM, VMEM, VMEM, VMEM, VMEM],
        (453 * mb, 4 * mb),
    )(core, received, rim, even, odd)

    other = lax.ppermute(part, "slab", CORE_PAIRS)
    part = call(
        keep_body, shape((128, 3456), BF16), [SMEM, VMEM, VMEM, VMEM, VMEM], (113 * mb, 3 * mb)
    )(core, both, ze, zo, other)
    tiles = exchange(part.reshape(16, 8, 3456), ("slab", "filt"), WIDE)
    tiles, late = lax.optimization_barrier((tiles, grad))
    right = shifted_2(late, "filt", -1)
    upper = shifted_2(late, "slab", -1)
    diagonal = lax.ppermute(
        late,
        ("slab", "filt"),
        [(8 * s + y, 8 * s + y - 9) for s in range(1, 64) for y in range(1, 8)],
    )
    tiles = exchange(add_up(tiles, 16), ("slab", "filt"), FAR)
    tiles, upper, diagonal = lax.optimization_barrier((tiles, upper, diagonal))
    tiles = add_up(tiles, 16)

    in_grad = call(
        input_body, shape((2, 2, 128, 256), BF16), [VMEM] * 5, (226 * mb, 3 * mb)
    )(grad, right, upper, diagonal, taps)
    in_grad = in_grad.transpose(0, 2, 1, 3)

    tiles = exchange(tiles, "slab", NEAR)
    out = call(last_body, shape((27, 32, 128), F32), [VMEM], (mb, mb))(tiles)
    weight_grad = out.reshape(3, 3, 3, 32, 128).transpose(0, 1, 2, 4, 3)
    return (in_grad, weight_grad)


def solution(mesh):
    in_specs = (P("slab", "filt", None, None), P(), P("slab", "filt", None, None))
    out_specs = (P("slab", None, "filt", None), P(None, None, None, None, "filt"))
    return jax.shard_map(
        on_device, mesh=mesh, in_specs=in_specs, out_specs=out_specs, check_vma=False
    )
```

```python
import jax
import jax.numpy as jnp
from jax import lax
from jax.experimental import pallas as pl
from jax.experimental.pallas import tpu as pltpu
from jax.sharding import PartitionSpec as P

F32 = jnp.float32
BF16 = jnp.bfloat16
VMEM = pl.BlockSpec(memory_space=pltpu.VMEM)
ANY = pl.BlockSpec(memory_space=pl.ANY)
SMEM = pl.BlockSpec(memory_space=pltpu.SMEM)
LIMIT = 48 * 1024 * 1024

def slab_of(x, z, core):
    return (x * 8 + z) * 2 + core


X4, Q4, B2 = range(4), range(4), range(2)


def member_of(x, zh, zl, c, yh, yl):
    return slab_of(x, 2 * zh + zl, c) * 8 + 2 * yh + yl


WIDE = [
    [member_of(x, zh, zl, c, yh, yl) for x in X4 for zl in B2 for yl in B2]
    for zh in Q4
    for c in B2
    for yh in Q4
]
FAR = [
    [member_of(x, zh, zl, c, yh, yl) for zh in Q4 for yh in Q4]
    for x in X4
    for zl in B2
    for c in B2
    for yl in B2
]
NEAR = [[slab_of(x, 2 * zh + zl, c) for x in X4 for zl in B2 for c in B2] for zh in Q4]
CORE_PAIRS = [(s, s ^ 1) for s in range(64)]


def call(body, out_shape, in_specs, cost, scratch=(), limit=LIMIT):
    many = isinstance(out_shape, (tuple, list))
    return pl.pallas_call(
        body,
        out_shape=out_shape,
        in_specs=in_specs,
        out_specs=[VMEM] * len(out_shape) if many else VMEM,
        scratch_shapes=list(scratch),
        compiler_params=pltpu.CompilerParams(vmem_limit_bytes=limit),
        cost_estimate=pl.CostEstimate(flops=cost[0], bytes_accessed=cost[1], transcendentals=0),
    )


def mm(left, right):
    return jnp.dot(left, right, preferred_element_type=F32)


def mm_nt(left, right):
    return lax.dot_general(left, right, (((1,), (1,)), ((), ())), preferred_element_type=F32)


def ones_where(cond):
    return jnp.where(cond, 1.0, 0.0).astype(BF16)


def iotas(rows, cols):
    return (
        lax.broadcasted_iota(jnp.int32, (rows, cols), 0),
        lax.broadcasted_iota(jnp.int32, (rows, cols), 1),
    )


def pack_body(vol_hbm, err_hbm, send_ref, vol_ref, err_ref, sems):
    copies = [
        pltpu.make_async_copy(vol_hbm, vol_ref, sems.at[0]),
        pltpu.make_async_copy(err_hbm, err_ref, sems.at[1]),
    ]
    for copy in copies:
        copy.start()
    i, j = iotas(256, 256)
    row_first = ones_where(j == ((i & 15) << 4) + (i >> 4))
    even_odd = ones_where(i == ((j & 127) << 1) + (j >> 7))
    error_rows = ones_where(j == ((i & 31) << 3) + (i >> 5))
    copies[0].wait()
    for p in range(2):
        plane = vol_ref[p].reshape(256, 256)
        plane = mm(row_first, plane).astype(BF16)
        plane = mm(plane, even_odd).astype(BF16)
        for y in range(8):
            for b in range(3):
                row = 2 * y - 1 + b
                if row < 0:
                    piece = jnp.zeros((16, 256), BF16)
                else:
                    piece = plane[row * 16 : row * 16 + 16]
                send_ref[y, p * 3 + b] = piece
    copies[1].wait()
    error = mm(error_rows, err_ref[0].reshape(256, 128)).astype(BF16)
    for y in range(8):
        for u in range(2):
            start = y * 32 + u * 16
            send_ref[y, 6, :, u * 128 : u * 128 + 128] = error[start : start + 16]


def turn_body(w_ref, even_ref, odd_ref):
    i, j = iotas(256, 256)
    same = ones_where(i == j)
    for ab in range(9):
        cols = slice(ab * 128, ab * 128 + 128)
        even_ref[:, cols] = mm_nt(same, w_ref[ab, 1]).astype(BF16)
        odd_ref[:256, cols] = mm_nt(same, w_ref[ab, 2]).astype(BF16)
        odd_ref[256:, cols] = mm_nt(same, w_ref[ab, 0]).astype(BF16)


def core_rows(core):
    i, j = iotas(128, 256)
    tile = (((i >> 1) & 3) << 6) + (((i >> 3) & 1) << 5)
    return ones_where(j == tile + ((i >> 4) << 2) + (i & 1) + core * 2)


def taps_of(order, both, ze, zo):
    now = mm(order, both[:, :128]).astype(BF16)
    after = mm(order, both[:, 128:]).astype(BF16)
    return mm_nt(after, zo[...]), mm_nt(now, ze[...]), mm_nt(now, zo[...])


def conv_body(core_ref, rec_ref, rim_ref, even_ref, odd_ref, grad_ref, both_ref, ze, zo, part_ref):
    for a in range(3):
        for b in range(3):
            rows = slice((a * 3 + b) * 128, (a * 3 + b) * 128 + 128)
            tile = rim_ref[:, b] if a == 0 else rec_ref[:, (a - 1) * 3 + b]
            tile = tile.reshape(128, 256)
            ze[rows] = tile[:, :128]
            zo[rows] = tile[:, 128:]
    center = mm(even_ref[...], ze[...])
    sides = mm(odd_ref[...], zo[...])
    errors = []
    for y in range(8):
        errors += [rec_ref[y, 6][:, :128], rec_ref[y, 6][:, 128:]]
    error = jnp.concatenate(errors, 0).astype(F32)
    lane = lax.broadcasted_iota(jnp.int32, (256, 128), 1)
    before = jnp.where(lane == 0, 0.0, pltpu.roll(sides[256:], 1, 1))
    preact = center + sides[:256] + before
    sigma = jax.nn.sigmoid(preact)
    grad = (error * (sigma * (1.0 + preact * (1.0 - sigma)))).astype(BF16)
    grad_ref[...] = grad
    after = jnp.where(lane == 127, 0.0, pltpu.roll(grad.astype(F32), 127, 1)).astype(BF16)
    both = jnp.concatenate([grad, after], 1)
    both_ref[...] = both
    parts = taps_of(core_rows(1 - core_ref[0]), both, ze, zo)
    for c in range(3):
        part_ref[:, c * 1152 : c * 1152 + 1152] = parts[c].astype(BF16)


def keep_body(core_ref, both_ref, ze, zo, other_ref, part_ref):
    parts = taps_of(core_rows(core_ref[0]), both_ref[...], ze, zo)
    for c in range(3):
        cols = slice(c * 1152, c * 1152 + 1152)
        part_ref[:, cols] = (parts[c] + other_ref[:, cols].astype(F32)).astype(BF16)


def sum_body(in_ref, out_ref):
    total = in_ref[0].astype(F32)
    for n in range(1, in_ref.shape[0]):
        total = total + in_ref[n].astype(F32)
    for n in range(out_ref.shape[0]):
        start = 2 * n % total.shape[0]
        out_ref[n] = total[start : start + 2].astype(BF16)


def last_body(in_ref, out_ref):
    for m in range(16):
        rows = in_ref[m].astype(F32) * (1.0 / 256.0)
        for c in range(3):
            for ab in range(9):
                start = (c * 9 + ab) * 128
                out_ref[ab * 3 + c, 2 * m : 2 * m + 2] = rows[:, start : start + 128]


def input_body(own_ref, right_ref, up_ref, diag_ref, w_ref, out_ref):
    lane = lax.broadcasted_iota(jnp.int32, (128, 128), 1)
    i, j = iotas(256, 256)
    weave = ones_where(j == ((i & 127) << 1) + (i >> 7))
    taps = (((1, 0),), ((2, 0), (0, 1)))
    grads = ((own_ref[...], right_ref[...]), (up_ref[...], diag_ref[...]))
    for ed in range(2):
        rows = []
        for er in range(2):
            sums = []
            for c in range(3):
                total = None
                for a, od in taps[ed]:
                    for b, pd in taps[er]:
                        term = mm(w_ref[a * 3 + b, c], grads[od][pd])
                        total = term if total is None else total + term
                sums.append(total)
            nxt = jnp.where(lane == 127, 0.0, pltpu.roll(sums[0], 127, 1))
            both = jnp.concatenate([sums[1].astype(BF16), (sums[2] + nxt).astype(BF16)], 1)
            rows.append(mm(both, weave))
        out_ref[ed] = jnp.stack(rows, 1).astype(BF16)


def shifted_2(value, axis, steps):
    count = lax.axis_size(axis)
    first, last = (max(0, -steps), min(count, count - steps))
    return lax.ppermute(value, axis, [(source, source + steps) for source in range(first, last)])


def exchange(value, axis, groups=None):
    return lax.all_to_all(
        value, axis, split_axis=0, concat_axis=0, axis_index_groups=groups, tiled=True
    )


def add_up(value, count):
    size = value.size * 2
    out_shape = jax.ShapeDtypeStruct((count, 2, 3456), BF16)
    return call(sum_body, out_shape, [VMEM], (size, size))(value)


def on_device(volume, weights, out_error):
    core = (lax.axis_index("slab") & 1).astype(jnp.int32).reshape(1)
    taps = weights.reshape(9, 3, 128, 256)
    shape = jax.ShapeDtypeStruct
    mb = 1 << 20

    send = call(
        pack_body,
        shape((8, 7, 16, 256), BF16),
        [ANY] * 2,
        (2 * mb, mb),
        [
            pltpu.VMEM(volume.shape, BF16),
            pltpu.VMEM(out_error.shape, BF16),
            pltpu.SemaphoreType.DMA((2,)),
        ],
        62500000,
    )(volume, out_error)
    received = exchange(send, "filt")
    even, odd = call(
        turn_body, (shape((256, 1152), BF16), shape((512, 1152), BF16)), [VMEM], (452 * mb, 4 * mb)
    )(taps)
    rim = shifted_2(received[:, 3:6], "slab", 1)
    stack = shape((1152, 128), BF16)
    grad, both, ze, zo, part = call(
        conv_body,
        (shape((256, 128), BF16), shape((256, 256), BF16), stack, stack, shape((128, 3456), BF16)),
        [SMEM, VMEM, VMEM, VMEM, VMEM],
        (453 * mb, 4 * mb),
    )(core, received, rim, even, odd)

    other = lax.ppermute(part, "slab", CORE_PAIRS)
    part = call(
        keep_body, shape((128, 3456), BF16), [SMEM, VMEM, VMEM, VMEM, VMEM], (113 * mb, 3 * mb)
    )(core, both, ze, zo, other)
    tiles = exchange(part.reshape(16, 8, 3456), ("slab", "filt"), WIDE)
    tiles, late = lax.optimization_barrier((tiles, grad))
    right = shifted_2(late, "filt", -1)
    upper = shifted_2(late, "slab", -1)
    diagonal = lax.ppermute(
        late,
        ("slab", "filt"),
        [(8 * s + y, 8 * s + y - 9) for s in range(1, 64) for y in range(1, 8)],
    )
    tiles = exchange(add_up(tiles, 16), ("slab", "filt"), FAR)
    tiles, upper, diagonal = lax.optimization_barrier((tiles, upper, diagonal))
    tiles = add_up(tiles, 16)

    in_grad = call(
        input_body, shape((2, 128, 2, 256), BF16), [VMEM] * 5, (226 * mb, 3 * mb)
    )(grad, right, upper, diagonal, taps)

    tiles = exchange(tiles, "slab", NEAR)
    out = call(last_body, shape((27, 32, 128), F32), [VMEM], (mb, mb))(tiles)
    weight_grad = out.reshape(3, 3, 3, 32, 128).transpose(0, 1, 2, 4, 3)
    return (in_grad, weight_grad)


def solution(mesh):
    in_specs = (P("slab", "filt", None, None), P(), P("slab", "filt", None, None))
    out_specs = (P("slab", None, "filt", None), P(None, None, None, None, "filt"))
    return jax.shard_map(
        on_device, mesh=mesh, in_specs=in_specs, out_specs=out_specs, check_vma=False
    )
```
